32 devices in a mesh: section: 2 (over x), dp: 16 (over z, y, core).
Axes of the slice: x: 2, y: 2, z: 4, core: 2. Of those that a mesh axis runs over, the one named last changes fastest.
Arguments:
- tokens: bfloat16 [2, 16, 1024, 512], P(None, 'dp'), may hold values from -6 to 6
- cotangent: bfloat16 [2, 2, 16, 1024, 512], P('section', None, 'dp'), may hold values from -6 to 6
- w_qkv: float32 [2, 512, 1536], P('section', 'dp'), may hold values from -0.25 to 0.25
- w_out: float32 [2, 512, 512], P('section', 'dp'), may hold values from -1 to 1
- w_gates: float32 [2, 2, 512, 512], P('section', None, 'dp'), may hold values from -0.25 to 0.25
- w_up: float32 [2, 512, 2048], P('section', 'dp'), may hold values from -0.25 to 0.25
- w_down: float32 [2, 2048, 512], P('section', 'dp'), may hold values from -0.125 to 0.125
- norm_gains: float32 [2, 2, 512], P('section', None, 'dp'), may hold values from 0.5 to 1.5
- gate_biases: float32 [2, 2, 512], P('section', None, 'dp'), may hold values from -4 to 4
Outputs:
- block_outputs: bfloat16 [2, 2, 16, 1024, 512], P('section', None, 'dp')
- input_grads: float32 [2, 2, 16, 1024, 512], P('section', None, 'dp')
- grad_qkv: float32 [2, 512, 1536], P('section', 'dp')
- grad_out: float32 [2, 512, 512], P('section', 'dp')
- grad_gates: float32 [2, 2, 512, 512], P('section', None, 'dp')
- grad_up: float32 [2, 512, 2048], P('section', 'dp')
- grad_down: float32 [2, 2048, 512], P('section', 'dp')
- grad_gains: float32 [2, 2, 512], P('section', None, 'dp')
- grad_biases: float32 [2, 2, 512], P('section', None, 'dp')
The draws below stay inside these ranges and needn't reach their ends.
All inputs are finite; a program needn't handle non-finite values.
Results may differ from the reference program's by a relative error of at most 0.015.
Values may be sent and summed in bfloat16 or wider, within the bound.
No kernel may reach another device: no remote copies, remote signals or barrier semaphores. Data moves between devices by JAX's collectives and lax.ppermute only.
A program may use at most 576 MiB of HBM per device.

```python
import jax
import jax.numpy as jnp
from jax import lax

H = 8
HD = 64
D = 512
FF = 2048
LEN = 1024
MB = 2
SEQS = 16


def level_of(key, extent, split, low, top_value):
    level, own = 1.0, jax.random.fold_in(key, 6)
    for axis_at, shards_of in split:
        draws = jnp.exp(jax.random.uniform(jax.random.fold_in(own, axis_at), (shards_of,), jnp.float32, low / len(split), top_value / len(split)))
        level = level * jnp.repeat(draws, extent[axis_at] // shards_of).reshape([-1 if axis == axis_at else 1 for axis in range(len(extent))])
    return level


def gaussian(own_key, extent, scale, most, cuts=(), dtype=jnp.bfloat16):
    factor_of = level_of(own_key, extent, cuts, -0.22, 0.18) if cuts else 1.0
    array = jax.random.normal(own_key, extent, jnp.float32) * scale * factor_of
    return jnp.minimum(jnp.maximum(array, -most), most).astype(dtype)


def setup_inputs(seed: int = 0) -> dict:
    splits = jax.random.split(jax.random.key(seed), 10)
    return {
        "tokens": gaussian(splits[0], (MB, SEQS, LEN, D), 1.0, 6.0, ((1, 16),)),
        "cotangent": gaussian(splits[1], (2, MB, SEQS, LEN, D), 1.0, 6.0, ((0, 2), (2, 16))),
        "w_qkv": gaussian(splits[2], (2, D, 3 * D), D ** -0.5, 0.25, ((0, 2), (1, 16)), jnp.float32),
        "w_out": gaussian(splits[3], (2, D, D), (D // 16) ** -0.5, 1.0, ((0, 2), (1, 16)), jnp.float32),
        "w_gates": gaussian(splits[4], (2, 2, D, D), D ** -0.5, 0.25, ((0, 2), (2, 16)), jnp.float32),
        "w_up": gaussian(splits[5], (2, D, FF), D ** -0.5, 0.25, ((0, 2), (1, 16)), jnp.float32),
        "w_down": gaussian(splits[6], (2, FF, D), FF ** -0.5, 0.125, ((0, 2), (1, 16)), jnp.float32),
        "norm_gains": jnp.clip(1.0 + 0.1 * jax.random.normal(splits[7], (2, 2, D), jnp.float32), 0.5, 1.5),
        "gate_biases": gaussian(splits[8], (2, 2, D), 1.0, 4.0, ((0, 2), (2, 16)), jnp.float32),
    }


precise = lax.Precision.HIGHEST
root_term = 0.7978845608
cube_term = 0.044715

@jax.custom_vjp
def low(v):
    return lax.optimization_barrier(v.astype(jnp.bfloat16)).astype(jnp.float32)

@jax.custom_vjp
def low_back(v):
    return v

def low_keep(v):
    return (low(v), None)

def low_pass(kept, grad):
    return (grad,)

def back_keep(v):
    return (v, None)

def back_low(kept, grad):
    return (low(grad),)
low.defvjp(low_keep, low_pass)
low_back.defvjp(back_keep, back_low)

def layer_norm(values, gain):
    average = lax.optimization_barrier(jnp.mean(values, axis=-1, keepdims=True))
    centred = values - average
    spread = lax.optimization_barrier(jnp.mean(centred * centred, axis=-1, keepdims=True))
    return centred * lax.rsqrt(spread + 1e-05) * gain

def smooth(hidden):
    return 0.5 * hidden * (1.0 + jnp.tanh(root_term * (hidden + cube_term * hidden * hidden * hidden)))

def attend(query, keyed, valued):
    raw = jnp.einsum('qhd,khd->hqk', query, keyed, precision=precise)
    scores = low_back(raw) * 0.125
    length = query.shape[0]
    causal = jnp.arange(length)[:, None] >= jnp.arange(length)[None, :]
    scores = jnp.where(causal[None], scores, -1e+30)
    highest = lax.optimization_barrier(jnp.max(scores, axis=-1, keepdims=True))
    weights = jnp.exp(scores - highest)
    probs = weights / lax.optimization_barrier(jnp.sum(weights, axis=-1, keepdims=True))
    return jnp.einsum('hqk,khd->qhd', low(probs), valued, precision=precise)
attend_saved = jax.checkpoint(attend)

def project(values, matrix):
    return jnp.einsum('gld,de->gle', values, matrix, precision=precise)

def layer(inputs, params, level):
    w_qkv, w_out, w_gates, w_up, w_down, gains, biases = params
    groups, length, width = inputs.shape
    normed = low(layer_norm(inputs, gains[level, 0]))
    mixed = low_back(low(project(normed, w_qkv[level])))
    mixed = mixed.reshape(groups, length, 3, H, HD)
    attended = lax.map(lambda triple: attend_saved(triple[0], triple[1], triple[2]), (mixed[:, :, 0], mixed[:, :, 1], mixed[:, :, 2]))
    attended = low_back(low(attended.reshape(groups, length, width)))
    branch = low_back(project(attended, w_out[level]))
    opening = jax.nn.sigmoid(low_back(project(normed, w_gates[level, 0]) + biases[level, 0]))
    middle = inputs + opening * branch
    second = low(layer_norm(middle, gains[level, 1]))
    hidden = low_back(project(second, w_up[level]))
    active = low(smooth(hidden))
    feed = low_back(project(active, w_down[level]))
    closing = jax.nn.sigmoid(low_back(project(second, w_gates[level, 1]) + biases[level, 1]))
    return middle + closing * feed

def reference(tokens, cotangent, w_qkv, w_out, w_gates, w_up, w_down, norm_gains, gate_biases):
    masters = (w_qkv, w_out, w_gates, w_up, w_down, norm_gains, gate_biases)
    number = MB * SEQS
    inputs = tokens.astype(jnp.float32).reshape(number // 4, 4, LEN, D)
    seeds = cotangent.astype(jnp.float32).reshape(2, number // 4, 4, LEN, D)

    def forward(start, offset, *weights):
        params = tuple((low(w) for w in weights))
        first = low(layer(start, params, 0))
        second = layer(low_back(first) + offset, params, 1)
        return (first, second)

    def group(totals, pieces):
        start, seed_first, seed_second = pieces
        offset = jnp.zeros_like(start)
        outputs, pullback = jax.vjp(forward, start, offset, *masters)
        grads = pullback((seed_first, seed_second))
        totals = tuple((total + grad for total, grad in zip(totals, grads[2:])))
        return (totals, (outputs[0], outputs[1], grads[0], grads[1]))
    initial = tuple((jnp.zeros_like(master) for master in masters))
    totals, results = lax.scan(group, initial, (inputs, seeds[0], seeds[1]))
    first_out, second_out, start_grad, offset_grad = results
    block = jnp.stack([first_out, second_out]).reshape(2, MB, SEQS, LEN, D).astype(jnp.bfloat16)
    in_grads = jnp.stack([start_grad, offset_grad]).reshape(2, MB, SEQS, LEN, D)
    return (block, in_grads, totals[0], totals[1], totals[2], totals[3], totals[4], totals[5], totals[6])
```

```python
import functools

import jax
import jax.numpy as jnp
from jax import lax
from jax.experimental import pallas as pl
from jax.experimental.pallas import tpu as pltpu
from jax.sharding import PartitionSpec as P

HD = 64
ROWS = 256
bf16 = jnp.bfloat16
f32 = jnp.float32
root_term = 0.7978845608
cube_term = 0.044715
VMEM = 56 * 1024 * 1024
PARTS = 16
UNIT = 32
FIRST = 3 * UNIT + 16
REST = 11 * UNIT


def dense(left, right):
    return jnp.dot(left, right, preferred_element_type=f32)


def cross(left, right):
    return lax.dot_general(left, right, (((0,), (0,)), ((), ())), preferred_element_type=f32)


def against(left, right):
    return lax.dot_general(left, right, (((1,), (1,)), ((), ())), preferred_element_type=f32)


def normalise(values):
    centred = values - jnp.mean(values, axis=-1, keepdims=True)
    spread = jnp.mean(centred * centred, axis=-1, keepdims=True)
    scale = lax.rsqrt(spread + 1e-05)
    return centred * scale, scale


def norm_back(grad, hat, scale, gain):
    spread = grad * gain
    first = jnp.mean(spread, axis=-1, keepdims=True)
    second = jnp.mean(spread * hat, axis=-1, keepdims=True)
    return scale * (spread - first - hat * second)


def struct(shape, dtype):
    return jax.ShapeDtypeStruct(shape, dtype)


def rows_of(width):
    return pl.BlockSpec((ROWS, width), lambda i, place: (i, 0))


def whole(*shape):
    return pl.BlockSpec(shape, lambda i, place: (0,) * len(shape))


def call(kernel, grid, in_specs, out_specs, out_shape, scratch=(), flops=0, moved=0):
    return pl.pallas_call(
        kernel,
        grid_spec=pltpu.PrefetchScalarGridSpec(
            num_scalar_prefetch=1, grid=grid, in_specs=in_specs, out_specs=out_specs, scratch_shapes=list(scratch)
        ),
        out_shape=out_shape,
        compiler_params=pltpu.CompilerParams(dimension_semantics=("arbitrary",), vmem_limit_bytes=VMEM),
        cost_estimate=pl.CostEstimate(flops=flops, bytes_accessed=moved, transcendentals=0),
    )


def fetches(place, sources, target, sems, cuts):
    copies = []
    for number, (start, stop) in enumerate(cuts):
        group = []
        for index, source in enumerate(sources):
            for slot in range(4):
                part = ((place[0] - slot) & 3) * 4 + (place[1] ^ (index & 1)) * 2 + (place[2] ^ (index >> 1))
                group.append(
                    pltpu.make_async_copy(
                        source.at[slot, pl.ds(start, stop - start)],
                        target.at[part, pl.ds(start, stop - start)],
                        sems.at[number],
                    )
                )
        copies.append(group)
    return copies


def unit(ref, at):
    return ref[:, at * UNIT : (at + 1) * UNIT, :].reshape(PARTS * UNIT, ref.shape[2])


def down_part(ref, at):
    return ref[at * 4 : at * 4 + 4, 7 * UNIT : 11 * UNIT, :].reshape(16 * UNIT, ref.shape[2])


ANY4 = [pl.BlockSpec(memory_space=pl.ANY)] * 4
REST_CUTS = ((0, 3 * UNIT), (3 * UNIT, 7 * UNIT), (7 * UNIT, 11 * UNIT))


def qkv_kernel(place, x_ref, w0, w1, w2, w3, n_ref, q_ref, k_ref, v_ref, vec_ref, buf, sems):
    copies = fetches(place, (w0, w1, w2, w3), buf, sems, ((0, FIRST),))[0]

    @pl.when(pl.program_id(0) == 0)
    def _():
        for copy in copies:
            copy.start()
        for copy in copies:
            copy.wait()
        vec_ref[...] = jnp.sum(buf[:, 3 * UNIT : 3 * UNIT + 16, :].astype(f32), axis=0)

    hat, _ = normalise(x_ref[...].astype(f32))
    n1 = (hat * vec_ref[0:1, :]).astype(bf16)
    n_ref[...] = n1
    q_ref[...] = (dense(n1, unit(buf, 0)).astype(bf16) * 0.125).astype(bf16)
    k_ref[...] = dense(n1, unit(buf, 1)).astype(bf16)
    v_ref[...] = dense(n1, unit(buf, 2)).astype(bf16)


def qkv_forward(place, x, weights):
    length, width = x.shape
    row = rows_of(width)
    return call(
        qkv_kernel,
        (length // ROWS,),
        [row] + ANY4,
        [row] * 4 + [whole(16, width)],
        [struct((length, width), bf16)] * 4 + [struct((16, width), f32)],
        [pltpu.VMEM((PARTS, FIRST, width), bf16), pltpu.SemaphoreType.DMA((1,))],
        flops=2 * length * width * 3 * width,
        moved=8_000_000,
    )(place, x, *weights)


def attend_kernel(block, place, q_ref, k_ref, v_ref, o_ref, s_ref):
    length = q_ref.shape[0]
    lane = lax.broadcasted_iota(jnp.int32, (block, 128), 1)
    row = lax.broadcasted_iota(jnp.int32, (block, block), 0)
    col = lax.broadcasted_iota(jnp.int32, (block, block), 1)
    for index in range(length // block):
        start, stop = index * block, (index + 1) * block
        q = q_ref[start:stop, :]
        outs, logs = [], []
        for head in range(2):
            mine = (lane >= head * HD) & (lane < (head + 1) * HD)
            own = jnp.where(mine, q, jnp.zeros_like(q))
            scores = against(own, k_ref[:stop, :])
            last = jnp.where(row >= col, scores[:, start:], -1e30)
            scores = jnp.concatenate([scores[:, :start], last], axis=1) if start else last
            highest = jnp.max(scores, axis=1, keepdims=True)
            weights = jnp.exp(scores - highest)
            total = jnp.sum(weights, axis=1, keepdims=True)
            outs.append(dense(weights.astype(bf16), v_ref[:stop, :]) * (1.0 / total))
            logs.append(highest + jnp.log(total))
        o_ref[start:stop, :] = jnp.where(lane < HD, outs[0], outs[1]).astype(bf16)
        s_ref[start:stop, :] = jnp.where(lane < HD, logs[0], logs[1])


def attend_forward(place, q, k, v, block=256):
    length, width = q.shape
    pair = pl.BlockSpec((length, 128), lambda i, place: (0, i))
    return call(
        functools.partial(attend_kernel, block),
        (width // 128,),
        [pair] * 3,
        [pair, pair],
        [struct((length, width), bf16), struct((length, width), f32)],
        flops=12_000_000_000,
        moved=6_000_000,
    )(place, q, k, v)


def feed_kernel(place, x_ref, n1_ref, o_ref, vec_ref, w0, w1, w2, w3,
                y_ref, n2_ref, scale_ref, ga_ref, ta_ref, h_ref, slope_ref, gf_ref, tf_ref, buf, sems):
    copies = fetches(place, (w0, w1, w2, w3), buf, sems, REST_CUTS)
    at_first = pl.program_id(0) == 0

    @pl.when(at_first)
    def _():
        for group in copies:
            for copy in group:
                copy.start()
        for group in copies:
            for copy in group:
                copy.wait()

    branch = dense(o_ref[...], unit(buf, 0))
    opening = jax.nn.sigmoid(dense(n1_ref[...], unit(buf, 1)) + vec_ref[2:3, :])
    gated = opening * branch
    middle = x_ref[...].astype(f32) + gated
    ga_ref[...] = opening.astype(bf16)
    ta_ref[...] = (gated * (1.0 - opening)).astype(bf16)
    hat, scale = normalise(middle)
    n2 = (hat * vec_ref[1:2, :]).astype(bf16)
    n2_ref[...] = n2
    scale_ref[...] = scale
    feed = None
    for at in range(4):
        cut = slice(at * 512, at * 512 + 512)
        u = dense(n2, unit(buf, 3 + at))
        square = u * u
        inner = jnp.tanh(u * (root_term + (root_term * cube_term) * square))
        half = 0.5 + 0.5 * inner
        active = (u * half).astype(bf16)
        h_ref[:, cut] = active
        slope = half + u * (0.5 - 0.5 * inner * inner) * (root_term + (3.0 * root_term * cube_term) * square)
        slope_ref[:, cut] = slope.astype(bf16)
        part = dense(active, down_part(buf, at))
        feed = part if feed is None else feed + part
    closing = jax.nn.sigmoid(dense(n2, unit(buf, 2)) + vec_ref[3:4, :])
    gated = closing * feed
    gf_ref[...] = closing.astype(bf16)
    tf_ref[...] = (gated * (1.0 - closing)).astype(bf16)
    y_ref[...] = (middle + gated).astype(bf16)


def feed_forward(place, x, n1, o, vec, weights):
    length, width = x.shape
    wide = 4 * width
    row, half = rows_of(width), struct((length, width), bf16)
    big, bigs = rows_of(wide), struct((length, wide), bf16)
    return call(
        feed_kernel,
        (length // ROWS,),
        [row, row, row, whole(16, width)] + ANY4,
        [row, row, rows_of(1), row, row, big, big, row, row],
        [half, half, struct((length, 1), f32), half, half, bigs, bigs, half, half],
        [pltpu.VMEM((PARTS, REST, width), bf16), pltpu.SemaphoreType.DMA((3,))],
        flops=2 * length * width * (3 * width + 2 * wide),
        moved=24_000_000,
    )(place, x, n1, o, vec, *weights)


def feed_back_kernel(extra, place, *refs):
    at = 1 + extra
    e_refs = refs[:at]
    n2_ref, scale_ref, ga_ref, ta_ref, slope_ref, gf_ref, tf_ref, vec_ref, w0, w1, w2, w3 = refs[at : at + 12]
    dm_ref, df_ref, dzf_ref, du_ref, da_ref, dza_ref, do_ref, small_ref, buf, sems = refs[at + 12 :]
    copies = fetches(place, (w0, w1, w2, w3), buf, sems, REST_CUTS)
    at_first = pl.program_id(0) == 0

    @pl.when(at_first)
    def _():
        for group in copies:
            for copy in group:
                copy.start()
        for group in copies:
            for copy in group:
                copy.wait()

    e = e_refs[0][...].astype(f32)
    for ref in e_refs[1:]:
        e = e + ref[...].astype(f32)
    df = (e * gf_ref[...].astype(f32)).astype(bf16)
    dzf = (e * tf_ref[...].astype(f32)).astype(bf16)
    df_ref[...] = df
    dzf_ref[...] = dzf
    dn2 = against(dzf, unit(buf, 2))
    for at in range(4):
        cut = slice(at * 512, at * 512 + 512)
        dh = against(df, down_part(buf, at))
        du = (dh * slope_ref[:, cut].astype(f32)).astype(bf16)
        du_ref[:, cut] = du
        dn2 = dn2 + against(du, unit(buf, 3 + at))
    gain = vec_ref[1:2, :]
    hat = n2_ref[...].astype(f32) * (1.0 / gain)
    dm = e + norm_back(dn2, hat, scale_ref[...], gain)
    dm_ref[...] = dm
    da = (dm * ga_ref[...].astype(f32)).astype(bf16)
    dza = (dm * ta_ref[...].astype(f32)).astype(bf16)
    da_ref[...] = da
    dza_ref[...] = dza
    do_ref[...] = against(da, unit(buf, 0)).astype(bf16)
    sums = jnp.concatenate(
        [jnp.sum(part, axis=0, keepdims=True) for part in (dn2 * hat, dza.astype(f32), dzf.astype(f32))]
        + [jnp.zeros((5, e.shape[1]), f32)],
        axis=0,
    )

    @pl.when(at_first)
    def _():
        small_ref[...] = sums

    @pl.when(pl.program_id(0) > 0)
    def _():
        small_ref[...] += sums


def feed_back(place, es, n2, scale, ga, ta, slope, gf, tf, vec, weights):
    length, width = n2.shape
    wide = 4 * width
    row, half = rows_of(width), struct((length, width), bf16)
    big, bigs = rows_of(wide), struct((length, wide), bf16)
    return call(
        functools.partial(feed_back_kernel, len(es) - 1),
        (length // ROWS,),
        [row] * len(es) + [row, rows_of(1), row, row, big, row, row, whole(16, width)] + ANY4,
        [row, row, row, big, row, row, row, whole(8, width)],
        [struct((length, width), f32), half, half, bigs, half, half, half, struct((8, width), f32)],
        [pltpu.VMEM((PARTS, REST, width), bf16), pltpu.SemaphoreType.DMA((3,))],
        flops=2 * length * width * (2 * width + 2 * wide),
        moved=24_000_000,
    )(place, *es, n2, scale, ga, ta, slope, gf, tf, vec, *weights)


def split3(value):
    first = value.astype(bf16)
    rest = value - first.astype(f32)
    second = rest.astype(bf16)
    third = (rest - second.astype(f32)).astype(bf16)
    return first, second, third


def attend_back_kernel(block, place, q_ref, k_ref, v_ref, o_ref, s_ref, do_ref, dq_ref, dk_ref, dv_ref,
                       q_s, k_s, v_s, do_s, acc):
    length = q_ref.shape[0]
    lane = lax.broadcasted_iota(jnp.int32, (length, 128), 1)
    row = lax.broadcasted_iota(jnp.int32, (block, block), 0)
    col = lax.broadcasted_iota(jnp.int32, (block, block), 1)
    q, k, v, do = q_ref[...], k_ref[...], v_ref[...], do_ref[...]
    zero = jnp.zeros_like(q)
    product = do.astype(f32) * o_ref[...].astype(f32)
    for head in range(2):
        low = head * HD
        other = (1 - head) * HD
        mine = (lane >= low) & (lane < low + HD)
        logs = -s_ref[:, low : low + 1]
        delta = -jnp.sum(jnp.where(mine, product, 0.0), axis=1, keepdims=True)
        one = jnp.where((lane >= other) & (lane < other + 3), jnp.ones_like(q), zero)
        q_aug, do_aug = jnp.where(mine, q, zero), jnp.where(mine, do, zero)
        for at, (part, piece) in enumerate(zip(split3(logs), split3(delta))):
            here = lane == other + at
            q_aug = jnp.where(here, part, q_aug)
            do_aug = jnp.where(here, piece, do_aug)
        q_s[head] = q_aug
        do_s[head] = do_aug
        k_s[head] = jnp.where(mine, k, one)
        v_s[head] = jnp.where(mine, v, one)
    for index in range(length // block):
        start, stop = index * block, (index + 1) * block
        kgrads, vgrads = [], []
        for head in range(2):
            kb, vb = k_s[head, start:stop, :], v_s[head, start:stop, :]
            scores = against(kb, q_s[head, start:, :])
            first = jnp.where(row <= col, scores[:, :block], -1e30)
            scores = jnp.concatenate([first, scores[:, block:]], axis=1) if stop < length else first
            probs = jnp.exp(scores)
            grads = (probs * against(vb, do_s[head, start:, :])).astype(bf16)
            vgrads.append(dense(probs.astype(bf16), do_ref[start:, :]))
            kgrads.append(dense(grads, q_ref[start:, :]))
            part = cross(grads, kb)
            if index == 0:
                acc[head] = part
            else:
                acc[head, start:, :] += part
        half = lane[:block] < HD
        dk_ref[start:stop, :] = jnp.where(half, kgrads[0], kgrads[1]).astype(bf16)
        dv_ref[start:stop, :] = jnp.where(half, vgrads[0], vgrads[1]).astype(bf16)
    dq_ref[...] = (jnp.where(lane < HD, acc[0], acc[1]) * 0.125).astype(bf16)


def attend_back(place, q, k, v, o, s, do, block=256):
    length, width = q.shape
    pair = pl.BlockSpec((length, 128), lambda i, place: (0, i))
    return call(
        functools.partial(attend_back_kernel, block),
        (width // 128,),
        [pair] * 6,
        [pair] * 3,
        [struct((length, width), bf16)] * 3,
        [pltpu.VMEM((2, length, 128), bf16)] * 4 + [pltpu.VMEM((2, length, 128), f32)],
        flops=20_000_000_000,
        moved=10_000_000,
    )(place, q, k, v, o, s, do)


def qkv_back_kernel(place, x_ref, dm_ref, dq_ref, dk_ref, dv_ref, dza_ref, vec_ref, w0, w1, w2, w3, r0, r1, r2, r3,
                    dx_ref, low_ref, small_ref, buf, gate, sems):
    copies = fetches(place, (w0, w1, w2, w3), buf, sems, ((0, 3 * UNIT),))[0]
    for index, source in enumerate((r0, r1, r2, r3)):
        for slot in range(4):
            part = ((place[0] - slot) & 3) * 4 + (place[1] ^ (index & 1)) * 2 + (place[2] ^ (index >> 1))
            copies.append(pltpu.make_async_copy(source.at[slot, pl.ds(UNIT, UNIT)], gate.at[part], sems.at[1]))
    at_first = pl.program_id(0) == 0

    @pl.when(at_first)
    def _():
        for copy in copies:
            copy.start()
        for copy in copies:
            copy.wait()

    dn = against(dza_ref[...], gate[...].reshape(PARTS * UNIT, gate.shape[2]))
    for at, ref in enumerate((dq_ref, dk_ref, dv_ref)):
        dn = dn + against(ref[...], unit(buf, at))
    hat, scale = normalise(x_ref[...].astype(f32))
    dx = dm_ref[...] + norm_back(dn, hat, scale, vec_ref[0:1, :])
    dx_ref[...] = dx
    low_ref[...] = dx.astype(bf16)
    sums = jnp.concatenate([jnp.sum(dn * hat, axis=0, keepdims=True), jnp.zeros((7, dx.shape[1]), f32)], axis=0)

    @pl.when(at_first)
    def _():
        small_ref[...] = sums

    @pl.when(pl.program_id(0) > 0)
    def _():
        small_ref[...] += sums


def qkv_back(place, x, dm, dq, dk, dv, dza, vec, weights, rest):
    length, width = x.shape
    row = rows_of(width)
    return call(
        qkv_back_kernel,
        (length // ROWS,),
        [row] * 6 + [whole(16, width)] + ANY4 + ANY4,
        [row, row, whole(8, width)],
        [struct((length, width), f32), struct((length, width), bf16), struct((8, width), f32)],
        [pltpu.VMEM((PARTS, 3 * UNIT, width), bf16), pltpu.VMEM((PARTS, UNIT, width), bf16), pltpu.SemaphoreType.DMA((2,))],
        flops=2 * length * width * 4 * width,
        moved=12_000_000,
    )(place, x, dm, dq, dk, dv, dza, vec, *weights, *rest)


def put(place, keep, send, values, rows, first):
    for y in range(2):
        low, high = (values[(y * 2 + c) * rows : (y * 2 + c + 1) * rows] for c in range(2))
        at = place[1] ^ y
        swap = place[2] == 1
        keep[at, 0, first : first + rows, :] = jnp.where(swap, high, low)
        send[at, 0, first : first + rows, :] = jnp.where(swap, low, high)


def rest_grad_kernel(place, o_ref, n1_ref, n2_ref, h_ref, da_ref, dza_ref, dzf_ref, du_ref, df_ref, keep, send):
    put(place, keep, send, cross(o_ref[...], da_ref[...]).astype(bf16), UNIT, 0)
    put(place, keep, send, cross(n1_ref[...], dza_ref[...]).astype(bf16), UNIT, UNIT)
    put(place, keep, send, cross(n2_ref[...], dzf_ref[...]).astype(bf16), UNIT, 2 * UNIT)
    up = cross(n2_ref[...], du_ref[...]).astype(bf16)
    for at in range(4):
        put(place, keep, send, up[:, at * 512 : at * 512 + 512], UNIT, (3 + at) * UNIT)
    put(place, keep, send, cross(h_ref[...], df_ref[...]).astype(bf16), 4 * UNIT, 7 * UNIT)


def rest_grad(place, o, n1, n2, h, da, dza, dzf, du, df):
    length, width = o.shape
    wide = h.shape[1]
    cols = pl.BlockSpec((length, width // 4), lambda i, place: (0, i))
    wides = pl.BlockSpec((length, wide // 4), lambda i, place: (0, i))
    out = pl.BlockSpec((2, 1, REST, width), lambda i, place: (0, (i - place[0]) & 3, 0, 0))
    return call(
        rest_grad_kernel,
        (4,),
        [cols] * 3 + [wides] + [whole(length, width)] * 3 + [whole(length, wide), whole(length, width)],
        [out, out],
        [struct((2, 4, REST, width), bf16)] * 2,
        flops=2 * length * width * (3 * width + 2 * wide),
        moved=26_000_000,
    )(place, o, n1, n2, h, da, dza, dzf, du, df)


def first_grad_kernel(place, n1_ref, dq_ref, dk_ref, dv_ref, s1_ref, s2_ref, keep, send):
    for at, ref in enumerate((dq_ref, dk_ref, dv_ref)):
        put(place, keep, send, cross(n1_ref[...], ref[...]).astype(bf16), UNIT, at * UNIT)
    small = jnp.concatenate([s1_ref[0:1, :], s2_ref[0:3, :], jnp.zeros((12, n1_ref.shape[1] * 4), f32)], axis=0).astype(bf16)
    for y in range(2):
        keep[y, 0, 3 * UNIT :, :] = small
        send[y, 0, 3 * UNIT :, :] = small


def first_grad(place, n1, dq, dk, dv, small1, small2):
    length, width = n1.shape
    cols = pl.BlockSpec((length, width // 4), lambda i, place: (0, i))
    out = pl.BlockSpec((2, 1, FIRST, width), lambda i, place: (0, (i - place[0]) & 3, 0, 0))
    return call(
        first_grad_kernel,
        (4,),
        [cols] + [whole(length, width)] * 3 + [whole(8, width)] * 2,
        [out, out],
        [struct((2, 4, FIRST, width), bf16)] * 2,
        flops=2 * length * width * 3 * width,
        moved=9_000_000,
    )(place, n1, dq, dk, dv, small1, small2)


def moved_z(value, steps):
    count = lax.axis_size("dp")
    return lax.ppermute(value, "dp", [(d, (d + 4 * steps) % count) for d in range(count)])


def swapped(value, bit):
    return lax.ppermute(value, "dp", [(d, d ^ bit) for d in range(lax.axis_size("dp"))])


def crossed(value, sources=(0, 1)):
    return lax.ppermute(value, "section", [(s, 1 - s) for s in sources])


def spread(block):
    own = jnp.stack([block] + [moved_z(block, k) for k in (1, 2, 3)])
    beside = swapped(own, 2)
    return own, beside, swapped(own, 1), swapped(beside, 1)


def spread_whole(blocks):
    blocks = blocks.reshape(4, 2, 2, *blocks.shape[1:])
    blocks = jnp.stack([blocks[0], blocks[3], blocks[2], blocks[1]])
    return tuple(blocks[:, index & 1, index >> 1] for index in range(4))


def gather_whole(values, axis):
    values = lax.all_gather(values.astype(bf16), "dp", axis=axis, tiled=True)
    return lax.all_gather(values, "section", axis=0, tiled=True)


def split_rows(matrix, cols):
    rows, width = matrix.shape[0] // PARTS, matrix.shape[1] // cols
    return matrix.reshape(PARTS, rows, cols, width).transpose(0, 2, 1, 3).reshape(PARTS, cols * rows, width)


def merge_rows(blocks, cols):
    rows, width = blocks.shape[1] // cols, blocks.shape[2]
    return blocks.reshape(PARTS, cols, rows, width).transpose(0, 2, 1, 3).reshape(PARTS * rows, cols * width)


def weights_whole(w_qkv, w_out, w_gates, w_up, w_down, gains, biases):
    w_qkv, w_out, w_up, w_down = (gather_whole(w, 1) for w in (w_qkv, w_out, w_up, w_down))
    w_gates, gains, biases = (gather_whole(w, 2) for w in (w_gates, gains, biases))
    heads, tails = [], []
    for layer in range(2):
        lines = jnp.concatenate([gains[layer], biases[layer], jnp.zeros((12, gains.shape[2]), bf16)], axis=0)
        lines = jnp.concatenate([lines[None], jnp.zeros((PARTS - 1, *lines.shape), bf16)], axis=0)
        heads.append(spread_whole(jnp.concatenate([split_rows(w_qkv[layer], 3), lines], axis=1)))
        parts = [w_out[layer], w_gates[layer, 0], w_gates[layer, 1]]
        parts = [split_rows(part, 1) for part in parts] + [split_rows(w_up[layer], 4), split_rows(w_down[layer], 1)]
        tails.append(spread_whole(jnp.concatenate(parts, axis=1)))
    return heads, tails


def collect_whole(early, rest):
    early, rest = (jnp.stack(pair).transpose(2, 1, 0, 3, 4).reshape(PARTS, *pair[0].shape[2:]) for pair in (early, rest))
    parts = [merge_rows(early[:, : 3 * UNIT], 3)]
    parts += [merge_rows(rest[:, :UNIT], 1)]
    parts += [jnp.stack([merge_rows(rest[:, at * UNIT : (at + 1) * UNIT], 1) for at in (1, 2)])]
    parts += [merge_rows(rest[:, 3 * UNIT : 7 * UNIT], 4), merge_rows(rest[:, 7 * UNIT :], 1)]
    lines = early[0, 3 * UNIT : 3 * UNIT + 4]
    parts += [lines[0:2], lines[2:4]]
    axes = (0, 0, 1, 0, 0, 1, 1)
    parts = [lax.psum_scatter(part.astype(f32), "dp", scatter_dimension=axis, tiled=True) for part, axis in zip(parts, axes)]
    return [lax.psum(part, "section")[None] for part in parts]


def collect(keep, send):
    got = swapped(send, 1)
    away = (keep[1].astype(f32) + got[1].astype(f32)).astype(bf16)
    near = keep[0].astype(f32) + got[0].astype(f32)
    got = swapped(away, 2)
    near = near + got.astype(f32)
    total = near[0]
    for k in (1, 2, 3):
        total = total + moved_z(near[k].astype(bf16), k).astype(f32)
    return total


def packed_first(w_qkv, gains, biases, index):
    rows, width = w_qkv.shape[1], 512
    qkv = [w_qkv[0][:, at * width : (at + 1) * width] for at in range(3)]
    count = width // rows
    lines = jnp.concatenate([gains[0], biases[0]], axis=0)
    lines = jnp.where(jnp.arange(width)[None, :] // rows == index, jnp.tile(lines, (1, count)), 0.0)
    return jnp.concatenate(qkv + [lines, jnp.zeros((12, width), f32)], axis=0).astype(bf16)


def packed_rest(w_out, w_gates, w_up, w_down):
    width = w_out.shape[2]
    ups = [w_up[0][:, at * width : (at + 1) * width] for at in range(4)]
    return jnp.concatenate([w_out[0], w_gates[0, 0], w_gates[0, 1]] + ups + [w_down[0]], axis=0).astype(bf16)


def per_device(tokens, cotangent, w_qkv, w_out, w_gates, w_up, w_down, norm_gains, gate_biases):
    section = lax.axis_index("section")
    index = lax.axis_index("dp")
    count = lax.axis_size("dp")
    fast = count == PARTS
    number, length, width = tokens.shape[0], tokens.shape[2], tokens.shape[3]
    first = section == 0

    def pick(own, other):
        return jnp.where(first, own, other), jnp.where(first, other, own)

    if not fast:
        place = jnp.zeros((3,), jnp.int32)
        heads, tails = weights_whole(w_qkv, w_out, w_gates, w_up, w_down, norm_gains, gate_biases)
    else:
        place = jnp.stack([index // 4, (index // 2) & 1, index & 1]).astype(jnp.int32)
        head = packed_first(w_qkv, norm_gains, gate_biases, index)
        tail = packed_rest(w_out, w_gates, w_up, w_down)
        heads = [spread(block) for block in pick(head, crossed(head))]
        tails = [spread(block) for block in pick(tail, crossed(tail))]
    x = jnp.where(first, tokens[0, 0], tokens[1, 0])
    seeds = [cotangent[0, m, 0] for m in range(2)]
    seeds = pick(jnp.where(first, seeds[0], seeds[1]), crossed(jnp.where(first, seeds[1], seeds[0])))

    kept = []
    value = x
    for layer in range(2):
        n1, q, k, v, vec = qkv_forward(place, value, heads[layer])
        o, s = attend_forward(place, q, k, v)
        y, n2, scale, ga, ta, h, slope, gf, tf = feed_forward(place, value, n1, o, vec, tails[layer])
        kept.append((value, n1, q, k, v, vec, o, s, n2, scale, ga, ta, h, slope, gf, tf))
        value = y
    y0, y1 = kept[1][0], value
    mine, theirs = pick(y0, y1)
    theirs = crossed(theirs)
    block = jnp.stack([jnp.where(first, mine, theirs), jnp.where(first, theirs, mine)])[None, :, None]

    extra = []
    results = {}
    for layer in (1, 0):
        value, n1, q, k, v, vec, o, s, n2, scale, ga, ta, h, slope, gf, tf = kept[layer]
        dm, df, dzf, du, da, dza, do, small2 = feed_back(
            place, [seeds[layer]] + extra, n2, scale, ga, ta, slope, gf, tf, vec, tails[layer]
        )
        rest = rest_grad(place, o, n1, n2, h, da, dza, dzf, du, df)
        if fast:
            rest = collect(*rest)
        dq, dk, dv = attend_back(place, q, k, v, o, s, do)
        dx, low, small1 = qkv_back(place, value, dm, dq, dk, dv, dza, vec, heads[layer], tails[layer])
        early = first_grad(place, n1, dq, dk, dv, small1, small2)
        extra = [low]
        if fast:
            early = collect(*early)
            sums = [part + crossed(part.astype(bf16), (1 - layer,)).astype(f32) for part in (early, rest)]
        else:
            sums = collect_whole(early, rest)
        results[layer] = (dx, crossed(low, (1 - layer,)), *sums)

    dx = jnp.where(first, results[0][0], results[1][0])
    other = jnp.where(first, results[0][1], results[1][1]).astype(f32)
    in_grads = jnp.stack([jnp.where(first, dx, other), jnp.where(first, other, dx)])[None, :, None]
    if not fast:
        return (block, in_grads, *(jnp.where(first, one, two) for one, two in zip(results[0][2:], results[1][2:])))
    early = jnp.where(first, results[0][2], results[1][2])
    rest = jnp.where(first, results[0][3], results[1][3])
    lines = lax.dynamic_slice(early, (3 * UNIT, index * UNIT), (4, UNIT))
    return (
        block,
        in_grads,
        jnp.concatenate([early[at * UNIT : (at + 1) * UNIT] for at in range(3)], axis=1)[None],
        rest[:UNIT][None],
        rest[UNIT : 3 * UNIT].reshape(1, 2, UNIT, width),
        jnp.concatenate([rest[(3 + at) * UNIT : (4 + at) * UNIT] for at in range(4)], axis=1)[None],
        rest[7 * UNIT :][None],
        lines[None, 0:2],
        lines[None, 2:4],
    )


def solution(mesh):
    placed = (
        P(None, "dp", None, None),
        P("section", None, "dp", None, None),
        P("section", "dp", None),
        P("section", "dp", None),
        P("section", None, "dp", None),
        P("section", "dp", None),
        P("section", "dp", None),
        P("section", None, "dp"),
        P("section", None, "dp"),
    )
    return jax.shard_map(
        per_device,
        mesh=mesh,
        in_specs=placed,
        out_specs=(P("section", None, "dp", None, None), P("section", None, "dp", None, None)) + placed[2:],
        check_vma=False,
    )
```

```python
import functools

import jax
import jax.numpy as jnp
from jax import lax
from jax.experimental import pallas as pl
from jax.experimental.pallas import tpu as pltpu
from jax.sharding import PartitionSpec as P

HD = 64
ROWS = 256
bf16 = jnp.bfloat16
f32 = jnp.float32
root_term = 0.7978845608
cube_term = 0.044715
VMEM = 56 * 1024 * 1024
PARTS = 16
UNIT = 32
FIRST = 3 * UNIT + 16
REST = 11 * UNIT


def dense(left, right):
    return jnp.dot(left, right, preferred_element_type=f32)


def cross(left, right):
    return lax.dot_general(left, right, (((0,), (0,)), ((), ())), preferred_element_type=f32)


def against(left, right):
    return lax.dot_general(left, right, (((1,), (1,)), ((), ())), preferred_element_type=f32)


def normalise(values):
    centred = values - jnp.mean(values, axis=-1, keepdims=True)
    spread = jnp.mean(centred * centred, axis=-1, keepdims=True)
    scale = lax.rsqrt(spread + 1e-05)
    return centred * scale, scale


def norm_back(grad, hat, scale, gain):
    spread = grad * gain
    first = jnp.mean(spread, axis=-1, keepdims=True)
    second = jnp.mean(spread * hat, axis=-1, keepdims=True)
    return scale * (spread - first - hat * second)


ANY = pl.BlockSpec(memory_space=pl.ANY)


def struct(shape, dtype):
    return jax.ShapeDtypeStruct(shape, dtype)


def rows_of(width):
    return pl.BlockSpec((ROWS, width), lambda i, place: (i, 0))


def whole(*shape):
    return pl.BlockSpec(shape, lambda i, place: (0,) * len(shape))


def call(kernel, grid, in_specs, out_specs, out_shape, scratch=(), flops=0, moved=0, waits=(), onto=()):
    extra = len(onto) + len(waits)
    count = len(in_specs)

    def run(*args):
        def body(*refs):
            kernel(*refs[: 1 + count], *refs[1 + count + extra :])

        return pl.pallas_call(
            body,
            grid_spec=pltpu.PrefetchScalarGridSpec(
                num_scalar_prefetch=1, grid=grid, in_specs=in_specs + [ANY] * extra, out_specs=out_specs, scratch_shapes=list(scratch)
            ),
            out_shape=out_shape,
            input_output_aliases={1 + count + at: at for at in range(len(onto))},
            compiler_params=pltpu.CompilerParams(dimension_semantics=("arbitrary",), vmem_limit_bytes=VMEM),
            cost_estimate=pl.CostEstimate(flops=flops, bytes_accessed=moved, transcendentals=0),
        )(*args, *onto, *waits)

    return run


def fetches(place, sources, target, sems, cuts, base=0):
    copies = []
    for number, (start, stop) in enumerate(cuts):
        group = []
        for index, source in enumerate(sources):
            for slot in range(4):
                part = ((place[0] - slot) & 3) * 4 + (place[1] ^ (index & 1)) * 2 + (place[2] ^ (index >> 1))
                group.append(
                    pltpu.make_async_copy(
                        source.at[slot, pl.ds(start, stop - start)],
                        target.at[part, pl.ds(start - base, stop - start)],
                        sems.at[number],
                    )
                )
        copies.append(group)
    return copies


def unit(ref, at):
    return ref[:, at * UNIT : (at + 1) * UNIT, :].reshape(PARTS * UNIT, ref.shape[2])


def down_part(ref, at, start=7):
    return ref[at * 4 : at * 4 + 4, start * UNIT : (start + 4) * UNIT, :].reshape(16 * UNIT, ref.shape[2])


def rest_copy(layer, source, target, sem, start, stop, base):
    cut, goal = pl.ds(start, stop - start), pl.ds(start - base, stop - start)
    return pltpu.make_async_copy(source.at[:, cut], target.at[:, goal], sem)


def at_start(copies):
    @pl.when(pl.program_id(0) == 0)
    def _():
        for copy in copies:
            copy.start()
        for copy in copies:
            copy.wait()


def qkv_kernel(many, place, x_ref, *refs):
    n_ref, q_ref, k_ref, v_ref, vec_ref, buf, sems = refs[many:]
    copies = fetches(place, refs[:many], buf, sems, ((0, FIRST),))[0]

    @pl.when(pl.program_id(0) == 0)
    def _():
        for copy in copies:
            copy.start()
        for copy in copies:
            copy.wait()
        vec_ref[...] = jnp.sum(buf[:, 3 * UNIT : 3 * UNIT + 16, :].astype(f32), axis=0)

    hat, _ = normalise(x_ref[...].astype(f32))
    n1 = (hat * vec_ref[0:1, :]).astype(bf16)
    n_ref[...] = n1
    q_ref[...] = (dense(n1, unit(buf, 0)).astype(bf16) * 0.125).astype(bf16)
    k_ref[...] = dense(n1, unit(buf, 1)).astype(bf16)
    v_ref[...] = dense(n1, unit(buf, 2)).astype(bf16)


def qkv_forward(place, x, weights, waits=()):
    length, width = x.shape
    row = rows_of(width)
    return call(
        functools.partial(qkv_kernel, len(weights)),
        (length // ROWS,),
        [row] + [ANY] * len(weights),
        [row] * 4 + [whole(16, width)],
        [struct((length, width), bf16)] * 4 + [struct((16, width), f32)],
        [pltpu.VMEM((PARTS, FIRST, width), bf16), pltpu.SemaphoreType.DMA((1,))],
        flops=2 * length * width * 3 * width,
        moved=8_000_000,
        waits=waits,
    )(place, x, *weights)


def attend_kernel(block, place, q_ref, k_ref, v_ref, o_ref, s_ref):
    length = q_ref.shape[0]
    lane = lax.broadcasted_iota(jnp.int32, (block, 128), 1)
    row = lax.broadcasted_iota(jnp.int32, (block, block), 0)
    col = lax.broadcasted_iota(jnp.int32, (block, block), 1)
    for index in range(length // block):
        start, stop = index * block, (index + 1) * block
        q = q_ref[start:stop, :]
        outs, logs = [], []
        for head in range(2):
            mine = (lane >= head * HD) & (lane < (head + 1) * HD)
            own = jnp.where(mine, q, jnp.zeros_like(q))
            scores = against(own, k_ref[:stop, :])
            last = jnp.where(row >= col, scores[:, start:], -1e30)
            scores = jnp.concatenate([scores[:, :start], last], axis=1) if start else last
            highest = jnp.max(scores, axis=1, keepdims=True)
            weights = jnp.exp(scores - highest)
            total = jnp.sum(weights, axis=1, keepdims=True)
            outs.append(dense(weights.astype(bf16), v_ref[:stop, :]) * (1.0 / total))
            logs.append(highest + jnp.log(total))
        o_ref[start:stop, :] = jnp.where(lane < HD, outs[0], outs[1]).astype(bf16)
        s_ref[start:stop, :] = jnp.where(lane < HD, logs[0], logs[1])


def attend_forward(place, q, k, v, start, onto=(), waits=(), block=256):
    length, width = q.shape
    pair = pl.BlockSpec((length, 128), lambda i, place: (0, i + start))
    return call(
        functools.partial(attend_kernel, block),
        (width // 256,),
        [pair] * 3,
        [pair, pair],
        [struct((length, width), bf16), struct((length, width), f32)],
        flops=6_000_000_000,
        moved=3_000_000,
        onto=onto,
        waits=waits,
    )(place, q, k, v)


def gate_kernel(layer, place, x_ref, n1_ref, o_ref, vec_ref, rest_ref,
                middle_ref, n2_ref, scale_ref, ga_ref, ta_ref, buf, sems):
    at_start([rest_copy(layer, rest_ref, buf, sems.at[0], 0, 2 * UNIT, 0)])

    branch = dense(o_ref[...], unit(buf, 0))
    opening = jax.nn.sigmoid(dense(n1_ref[...], unit(buf, 1)) + vec_ref[2:3, :])
    gated = opening * branch
    middle = x_ref[...].astype(f32) + gated
    middle_ref[...] = middle
    ga_ref[...] = opening.astype(bf16)
    ta_ref[...] = (gated * (1.0 - opening)).astype(bf16)
    hat, scale = normalise(middle)
    n2_ref[...] = (hat * vec_ref[1:2, :]).astype(bf16)
    scale_ref[...] = scale


def gate_forward(place, layer, x, n1, o, vec, rest, waits=()):
    length, width = x.shape
    row, half = rows_of(width), struct((length, width), bf16)
    return call(
        functools.partial(gate_kernel, layer),
        (length // ROWS,),
        [row, row, row, whole(16, width), ANY],
        [row, row, rows_of(1), row, row],
        [struct((length, width), f32), half, struct((length, 1), f32), half, half],
        [pltpu.VMEM((PARTS, 2 * UNIT, width), bf16), pltpu.SemaphoreType.DMA((1,))],
        flops=2 * length * width * 2 * width,
        moved=9_000_000,
        waits=waits,
    )(place, x, n1, o, vec, rest)


def feed_kernel(layer, place, middle_ref, n2_ref, vec_ref, rest_ref, y_ref, h_ref, slope_ref, gf_ref, tf_ref, buf, sems):
    at_start([rest_copy(layer, rest_ref, buf, sems.at[0], 2 * UNIT, REST, 2 * UNIT)])

    n2 = n2_ref[...]
    feed = None
    for at in range(4):
        cut = slice(at * 512, at * 512 + 512)
        u = dense(n2, unit(buf, 1 + at))
        square = u * u
        inner = jnp.tanh(u * (root_term + (root_term * cube_term) * square))
        half = 0.5 + 0.5 * inner
        active = (u * half).astype(bf16)
        h_ref[:, cut] = active
        slope = half + u * (0.5 - 0.5 * inner * inner) * (root_term + (3.0 * root_term * cube_term) * square)
        slope_ref[:, cut] = slope.astype(bf16)
        part = dense(active, down_part(buf, at, 5))
        feed = part if feed is None else feed + part
    closing = jax.nn.sigmoid(dense(n2, unit(buf, 0)) + vec_ref[3:4, :])
    gated = closing * feed
    gf_ref[...] = closing.astype(bf16)
    tf_ref[...] = (gated * (1.0 - closing)).astype(bf16)
    y_ref[...] = (middle_ref[...] + gated).astype(bf16)


def feed_forward(place, layer, middle, n2, vec, rest, waits=()):
    length, width = middle.shape
    wide = 4 * width
    row, half = rows_of(width), struct((length, width), bf16)
    big, bigs = rows_of(wide), struct((length, wide), bf16)
    return call(
        functools.partial(feed_kernel, layer),
        (length // ROWS,),
        [row, row, whole(16, width), ANY],
        [row, big, big, row, row],
        [half, bigs, bigs, half, half],
        [pltpu.VMEM((PARTS, REST - 2 * UNIT, width), bf16), pltpu.SemaphoreType.DMA((1,))],
        flops=2 * length * width * (width + 2 * wide),
        moved=20_000_000,
        waits=waits,
    )(place, middle, n2, vec, rest)


def feed_back_kernel(layer, extra, place, *refs):
    at = 1 + extra
    e_refs = refs[:at]
    n2_ref, scale_ref, ga_ref, ta_ref, slope_ref, gf_ref, tf_ref, vec_ref, rest_ref = refs[at : at + 9]
    dm_ref, df_ref, dzf_ref, du_ref, da_ref, dza_ref, do_ref, small_ref, buf, sems = refs[at + 9 :]
    at_start([rest_copy(layer, rest_ref, buf, sems.at[0], 0, REST, 0)])
    at_first = pl.program_id(0) == 0

    e = e_refs[0][...].astype(f32)
    for ref in e_refs[1:]:
        e = e + ref[...].astype(f32)
    df = (e * gf_ref[...].astype(f32)).astype(bf16)
    dzf = (e * tf_ref[...].astype(f32)).astype(bf16)
    df_ref[...] = df
    dzf_ref[...] = dzf
    dn2 = against(dzf, unit(buf, 2))
    for at in range(4):
        cut = slice(at * 512, at * 512 + 512)
        dh = against(df, down_part(buf, at))
        du = (dh * slope_ref[:, cut].astype(f32)).astype(bf16)
        du_ref[:, cut] = du
        dn2 = dn2 + against(du, unit(buf, 3 + at))
    gain = vec_ref[1:2, :]
    hat = n2_ref[...].astype(f32) * (1.0 / gain)
    dm = e + norm_back(dn2, hat, scale_ref[...], gain)
    dm_ref[...] = dm
    da = (dm * ga_ref[...].astype(f32)).astype(bf16)
    dza = (dm * ta_ref[...].astype(f32)).astype(bf16)
    da_ref[...] = da
    dza_ref[...] = dza
    do_ref[...] = against(da, unit(buf, 0)).astype(bf16)
    sums = jnp.concatenate(
        [jnp.sum(part.astype(f32), axis=0, keepdims=True) for part in (dza, dzf)] + [jnp.zeros((14, e.shape[1]), f32)],
        axis=0,
    )

    @pl.when(at_first)
    def _():
        small_ref[...] = sums

    @pl.when(pl.program_id(0) > 0)
    def _():
        small_ref[...] += sums


def feed_back(place, layer, es, n2, scale, ga, ta, slope, gf, tf, vec, rest, waits=()):
    length, width = n2.shape
    wide = 4 * width
    row, half = rows_of(width), struct((length, width), bf16)
    big, bigs = rows_of(wide), struct((length, wide), bf16)
    return call(
        functools.partial(feed_back_kernel, layer, len(es) - 1),
        (length // ROWS,),
        [row] * len(es) + [row, rows_of(1), row, row, big, row, row, whole(16, width), ANY],
        [row, row, row, big, row, row, row, whole(16, width)],
        [struct((length, width), f32), half, half, bigs, half, half, half, struct((16, width), f32)],
        [pltpu.VMEM((PARTS, REST, width), bf16), pltpu.SemaphoreType.DMA((1,))],
        flops=2 * length * width * (2 * width + 2 * wide),
        moved=24_000_000,
        waits=waits,
    )(place, *es, n2, scale, ga, ta, slope, gf, tf, vec, rest)


def split3(value):
    first = value.astype(bf16)
    rest = value - first.astype(f32)
    second = rest.astype(bf16)
    third = (rest - second.astype(f32)).astype(bf16)
    return first, second, third


def attend_back_kernel(block, place, q_ref, k_ref, v_ref, o_ref, s_ref, do_ref, dq_ref, dk_ref, dv_ref,
                       q_s, k_s, v_s, do_s, acc):
    length = q_ref.shape[0]
    lane = lax.broadcasted_iota(jnp.int32, (length, 128), 1)
    row = lax.broadcasted_iota(jnp.int32, (block, block), 0)
    col = lax.broadcasted_iota(jnp.int32, (block, block), 1)
    q, k, v, do = q_ref[...], k_ref[...], v_ref[...], do_ref[...]
    zero = jnp.zeros_like(q)
    product = do.astype(f32) * o_ref[...].astype(f32)
    for head in range(2):
        low = head * HD
        other = (1 - head) * HD
        mine = (lane >= low) & (lane < low + HD)
        logs = -s_ref[:, low : low + 1]
        delta = -jnp.sum(jnp.where(mine, product, 0.0), axis=1, keepdims=True)
        one = jnp.where((lane >= other) & (lane < other + 3), jnp.ones_like(q), zero)
        q_aug, do_aug = jnp.where(mine, q, zero), jnp.where(mine, do, zero)
        for at, (part, piece) in enumerate(zip(split3(logs), split3(delta))):
            here = lane == other + at
            q_aug = jnp.where(here, part, q_aug)
            do_aug = jnp.where(here, piece, do_aug)
        q_s[head] = q_aug
        do_s[head] = do_aug
        k_s[head] = jnp.where(mine, k, one)
        v_s[head] = jnp.where(mine, v, one)
    for index in range(length // block):
        start, stop = index * block, (index + 1) * block
        kgrads, vgrads = [], []
        for head in range(2):
            kb, vb = k_s[head, start:stop, :], v_s[head, start:stop, :]
            scores = against(kb, q_s[head, start:, :])
            first = jnp.where(row <= col, scores[:, :block], -1e30)
            scores = jnp.concatenate([first, scores[:, block:]], axis=1) if stop < length else first
            probs = jnp.exp(scores)
            grads = (probs * against(vb, do_s[head, start:, :])).astype(bf16)
            vgrads.append(dense(probs.astype(bf16), do_ref[start:, :]))
            kgrads.append(dense(grads, q_ref[start:, :]))
            part = cross(grads, kb)
            if index == 0:
                acc[head] = part
            else:
                acc[head, start:, :] += part
        half = lane[:block] < HD
        dk_ref[start:stop, :] = jnp.where(half, kgrads[0], kgrads[1]).astype(bf16)
        dv_ref[start:stop, :] = jnp.where(half, vgrads[0], vgrads[1]).astype(bf16)
    dq_ref[...] = (jnp.where(lane < HD, acc[0], acc[1]) * 0.125).astype(bf16)


def attend_back(place, q, k, v, o, s, do, start, onto=(), waits=(), block=256):
    length, width = q.shape
    pair = pl.BlockSpec((length, 128), lambda i, place: (0, i + start))
    return call(
        functools.partial(attend_back_kernel, block),
        (width // 256,),
        [pair] * 6,
        [pair] * 3,
        [struct((length, width), bf16)] * 3,
        [pltpu.VMEM((2, length, 128), bf16)] * 4 + [pltpu.VMEM((2, length, 128), f32)],
        flops=10_000_000_000,
        moved=5_000_000,
        onto=onto,
        waits=waits,
    )(place, q, k, v, o, s, do)


def qkv_back_kernel(layer, many, place, x_ref, dm_ref, dq_ref, dk_ref, dv_ref, dza_ref, vec_ref, rest_ref, *refs):
    dx_ref, low_ref, buf, gate, sems = refs[many:]
    copies = fetches(place, refs[:many], buf, sems, ((0, 3 * UNIT),))[0]
    at_start(copies + [rest_copy(layer, rest_ref, gate, sems.at[1], UNIT, 2 * UNIT, UNIT)])
    dn = against(dza_ref[...], gate[...].reshape(PARTS * UNIT, gate.shape[2]))
    for at, ref in enumerate((dq_ref, dk_ref, dv_ref)):
        dn = dn + against(ref[...], unit(buf, at))
    hat, scale = normalise(x_ref[...].astype(f32))
    dx = dm_ref[...] + norm_back(dn, hat, scale, vec_ref[0:1, :])
    dx_ref[...] = dx
    low_ref[...] = dx.astype(bf16)


def qkv_back(place, layer, x, dm, dq, dk, dv, dza, vec, weights, rest, waits=()):
    length, width = x.shape
    row = rows_of(width)
    return call(
        functools.partial(qkv_back_kernel, layer, len(weights)),
        (length // ROWS,),
        [row] * 6 + [whole(16, width), ANY] + [ANY] * len(weights),
        [row, row],
        [struct((length, width), f32), struct((length, width), bf16)],
        [pltpu.VMEM((PARTS, 3 * UNIT, width), bf16), pltpu.VMEM((PARTS, UNIT, width), bf16), pltpu.SemaphoreType.DMA((2,))],
        flops=2 * length * width * 4 * width,
        moved=12_000_000,
        waits=waits,
    )(place, x, dm, dq, dk, dv, dza, vec, rest, *weights)


def put(place, outs, values, rows, first):
    keep, send = outs
    for y in range(2):
        low, high = (values[(y * 2 + c) * rows : (y * 2 + c + 1) * rows] for c in range(2))
        at = place[1] ^ y
        swap = place[2] == 1
        keep[at, 0, first : first + rows, :] = jnp.where(swap, high, low)
        send[at, 0, first : first + rows, :] = jnp.where(swap, low, high)


def put_plain(out, values, rows, first):
    for part in range(4):
        out[part, first : first + rows, :] = values[part * rows : (part + 1) * rows]


def grad_outs(rows, width):
    out = pl.BlockSpec((2, 1, rows, width), lambda i, place: (0, (i - place[0]) & 3, 0, 0))
    return [out, out], [struct((2, 4, rows, width), bf16)] * 2


def rest_grad_kernel(place, o_ref, n1_ref, n2_ref, h_ref, da_ref, dza_ref, dzf_ref, du_ref, df_ref, small_ref, out):
    put_plain(out, cross(o_ref[...], da_ref[...]).astype(bf16), UNIT, 0)
    put_plain(out, cross(n1_ref[...], dza_ref[...]).astype(bf16), UNIT, UNIT)
    put_plain(out, cross(n2_ref[...], dzf_ref[...]).astype(bf16), UNIT, 2 * UNIT)
    up = cross(n2_ref[...], du_ref[...]).astype(bf16)
    for at in range(4):
        put_plain(out, up[:, at * 512 : at * 512 + 512], UNIT, (3 + at) * UNIT)
    put_plain(out, cross(h_ref[...], df_ref[...]).astype(bf16), 4 * UNIT, 7 * UNIT)
    for part in range(4):
        out[part, REST:, :] = small_ref[...].astype(bf16)


def rest_grad(place, o, n1, n2, h, da, dza, dzf, du, df, small, waits=()):
    length, width = o.shape
    wide = h.shape[1]
    cols = pl.BlockSpec((length, width // 4), lambda i, place: (0, i))
    wides = pl.BlockSpec((length, wide // 4), lambda i, place: (0, i))
    full = whole(length, width)
    return call(
        rest_grad_kernel,
        (4,),
        [cols] * 3 + [wides] + [full] * 3 + [whole(length, wide), full, whole(16, width)],
        pl.BlockSpec((4, REST + 16, width), lambda i, place: (i, 0, 0)),
        struct((PARTS, REST + 16, width), bf16),
        flops=2 * length * width * (3 * width + 2 * wide),
        moved=26_000_000,
        waits=waits,
    )(place, o, n1, n2, h, da, dza, dzf, du, df, small)


def first_grad_kernel(place, *refs):
    outs = refs[-2:]
    for layer in range(len(refs) // 4):
        n1_ref = refs[4 * layer]
        for at, ref in enumerate(refs[4 * layer + 1 : 4 * layer + 4]):
            put(place, outs, cross(n1_ref[...], ref[...]).astype(bf16), UNIT, (3 * layer + at) * UNIT)


def first_grad(place, *layers, waits=()):
    length, width = layers[0][0].shape
    cols = pl.BlockSpec((length, width // 4), lambda i, place: (0, i))
    specs, shapes = grad_outs(3 * UNIT * len(layers), width)
    return call(
        first_grad_kernel,
        (4,),
        ([cols] + [whole(length, width)] * 3) * len(layers),
        specs,
        shapes,
        flops=2 * length * width * 3 * width * len(layers),
        moved=9_000_000 * len(layers),
        waits=waits,
    )(place, *(value for layer in layers for value in layer))


def moved_z(value, steps):
    count = lax.axis_size("dp")
    return lax.ppermute(value, "dp", [(d, (d + 4 * steps) % count) for d in range(count)])


def swapped(value, bit):
    return lax.ppermute(value, "dp", [(d, d ^ bit) for d in range(lax.axis_size("dp"))])


def crossed(value, sources=(0, 1)):
    return lax.ppermute(value, "section", [(s, 1 - s) for s in sources])


def along_z(block):
    return [block] + [moved_z(block, k) for k in (1, 2, 3)]


def across(own):
    beside = swapped(own, 2)
    return own, beside, swapped(own, 1), swapped(beside, 1)


def spread_whole(blocks):
    blocks = blocks.reshape(4, 2, 2, *blocks.shape[1:])
    blocks = jnp.stack([blocks[0], blocks[3], blocks[2], blocks[1]])
    return tuple(blocks[:, index & 1, index >> 1] for index in range(4))


def gather_whole(values, axis):
    values = lax.all_gather(values.astype(bf16), "dp", axis=axis, tiled=True)
    return lax.all_gather(values, "section", axis=0, tiled=True)


def split_rows(matrix, cols):
    rows, width = matrix.shape[0] // PARTS, matrix.shape[1] // cols
    return matrix.reshape(PARTS, rows, cols, width).transpose(0, 2, 1, 3).reshape(PARTS, cols * rows, width)


def merge_rows(blocks, cols):
    rows, width = blocks.shape[1] // cols, blocks.shape[2]
    return blocks.reshape(PARTS, cols, rows, width).transpose(0, 2, 1, 3).reshape(PARTS * rows, cols * width)


def weights_whole(w_qkv, w_out, w_gates, w_up, w_down, gains, biases):
    w_qkv, w_out, w_up, w_down = (gather_whole(w, 1) for w in (w_qkv, w_out, w_up, w_down))
    w_gates, gains, biases = (gather_whole(w, 2) for w in (w_gates, gains, biases))
    heads, tails = [], []
    for layer in range(2):
        lines = jnp.concatenate([gains[layer], biases[layer], jnp.zeros((12, gains.shape[2]), bf16)], axis=0)
        lines = jnp.concatenate([lines[None], jnp.zeros((PARTS - 1, *lines.shape), bf16)], axis=0)
        heads.append(spread_whole(jnp.concatenate([split_rows(w_qkv[layer], 3), lines], axis=1)))
        parts = [w_out[layer], w_gates[layer, 0], w_gates[layer, 1]]
        parts = [split_rows(part, 1) for part in parts] + [split_rows(w_up[layer], 4), split_rows(w_down[layer], 1)]
        tails.append(jnp.concatenate(parts, axis=1))
    return heads, tails


def joined(pieces):
    return jnp.stack(pieces).transpose(2, 1, 0, 3, 4).reshape(PARTS, *pieces[0].shape[2:])


def collect_whole(early, rest):
    early = joined(early)
    parts = [merge_rows(early, 3), merge_rows(rest[:, :UNIT], 1)]
    parts += [jnp.stack([merge_rows(rest[:, at * UNIT : (at + 1) * UNIT], 1) for at in (1, 2)])]
    parts += [merge_rows(rest[:, 3 * UNIT : 7 * UNIT], 4), merge_rows(rest[:, 7 * UNIT : REST], 1), rest[0, REST : REST + 2]]
    axes = (0, 0, 1, 0, 0, 1)
    parts = [lax.psum_scatter(part.astype(f32), "dp", scatter_dimension=axis, tiled=True) for part, axis in zip(parts, axes)]
    return [lax.psum(part, "section") for part in parts]


def fold_core(keep, got):
    away = (keep[1].astype(f32) + got[1].astype(f32)).astype(bf16)
    return away, keep[0].astype(f32) + got[0].astype(f32)


def fold_y(near, got):
    near = near + got.astype(f32)
    return near[0], [near[k].astype(bf16) for k in (1, 2, 3)]


def fold_z(total, gots):
    for got in gots:
        total = total + got.astype(f32)
    return total


def pack_kernel(place, qkv_ref, out_ref, gates_ref, up_ref, down_ref, lines_ref, head_ref, tail_ref):
    width = out_ref.shape[2]
    for at in range(3):
        head_ref[at * UNIT : (at + 1) * UNIT, :] = qkv_ref[0, :, at * width : (at + 1) * width].astype(bf16)
    head_ref[3 * UNIT :, :] = lines_ref[...].astype(bf16)
    tail_ref[:UNIT, :] = out_ref[0].astype(bf16)
    for at in range(2):
        tail_ref[(1 + at) * UNIT : (2 + at) * UNIT, :] = gates_ref[0, at].astype(bf16)
    for at in range(4):
        tail_ref[(3 + at) * UNIT : (4 + at) * UNIT, :] = up_ref[0, :, at * width : (at + 1) * width].astype(bf16)
    tail_ref[7 * UNIT :, :] = down_ref[0].astype(bf16)


def pack(place, index, w_qkv, w_out, w_gates, w_up, w_down, gains, biases):
    width = w_out.shape[2]
    lines = jnp.concatenate([gains[0], biases[0]], axis=0)
    mine = jnp.arange(width)[None, :] // UNIT == index
    lines = jnp.concatenate([jnp.where(mine, jnp.tile(lines, (1, PARTS)), 0.0), jnp.zeros((12, width), f32)], axis=0)
    arrays = (w_qkv, w_out, w_gates, w_up, w_down, lines)
    return call(
        pack_kernel,
        (1,),
        [whole(*array.shape) for array in arrays],
        [whole(FIRST, width), whole(REST, width)],
        [struct((FIRST, width), bf16), struct((REST, width), bf16)],
        moved=3_000_000,
    )(place, *arrays)


def after(value, *others):
    return lax.optimization_barrier((value, *others))[0]


def gain_grads(grads, w_qkv, w_gates, w_up, gains):
    d_qkv, _, d_gates, d_up = grads[:4]
    w_qkv, w_gates, w_up, gains = (w[0].astype(bf16).astype(f32) for w in (w_qkv, w_gates, w_up, gains))
    first = jnp.sum(w_qkv * d_qkv, axis=1) + jnp.sum(w_gates[0] * d_gates[0], axis=1)
    second = jnp.sum(w_up * d_up, axis=1) + jnp.sum(w_gates[1] * d_gates[1], axis=1)
    return jnp.stack([first, second]) / gains


def layer_forward(place, layer, x, head, rest):
    n1, q, k, v, vec = qkv_forward(place, x, head)
    o, s = attend_forward(place, q, k, v, 2, onto=attend_forward(place, q, k, v, 0))
    middle, n2, scale, ga, ta = gate_forward(place, layer, x, n1, o, vec, rest)
    y, h, slope, gf, tf = feed_forward(place, layer, middle, n2, vec, rest)
    return y, (x, n1, q, k, v, vec, o, s, n2, scale, ga, ta, h, slope, gf, tf)


def layer_backward(place, layer, grads, kept, head, rest):
    x, n1, q, k, v, vec, o, s, n2, scale, ga, ta, h, slope, gf, tf = kept
    dm, df, dzf, du, da, dza, do, small = feed_back(place, layer, grads, n2, scale, ga, ta, slope, gf, tf, vec, rest)
    later = rest_grad(place, o, n1, n2, h, da, dza, dzf, du, df, small)
    dqkv = attend_back(place, q, k, v, o, s, do, 2, onto=attend_back(place, q, k, v, o, s, do, 0))
    early = first_grad(place, (n1, *dqkv))
    dx, low = qkv_back(place, layer, x, dm, *dqkv, dza, vec, head, rest)
    return dx, low, collect_whole(early, later)


def per_device(tokens, cotangent, w_qkv, w_out, w_gates, w_up, w_down, norm_gains, gate_biases):
    section = lax.axis_index("section")
    index = lax.axis_index("dp")
    fast = lax.axis_size("dp") == PARTS
    first = section == 0
    masters = (w_qkv, w_out, w_gates, w_up, w_down, norm_gains, gate_biases)

    def pick(own, other):
        return jnp.where(first, own, other), jnp.where(first, other, own)

    x = jnp.where(first, tokens[0, 0], tokens[1, 0])
    seeds = [cotangent[0, m, 0] for m in range(2)]
    own_seed, other_seed = jnp.where(first, seeds[0], seeds[1]), jnp.where(first, seeds[1], seeds[0])
    if fast:
        y0, y1, theirs, dxs, lows, grads = run(x, own_seed, other_seed, masters, index, first, pick)
    else:
        place = jnp.zeros((3,), jnp.int32)
        heads, rest = weights_whole(*masters)
        y0, kept0 = layer_forward(place, 0, x, heads[0], rest[0])
        y1, kept1 = layer_forward(place, 1, y0, heads[1], rest[1])
        seeds = pick(own_seed, crossed(other_seed))
        dx1, low1, grads1 = layer_backward(place, 1, [seeds[1]], kept1, heads[1], rest[1])
        dx0, low0, grads0 = layer_backward(place, 0, [seeds[0], low1], kept0, heads[0], rest[0])
        dxs, lows = (dx0, dx1), (crossed(low0, (1,)), crossed(low1, (0,)))
        theirs = crossed(jnp.where(first, y1, y0))
        grads = [jnp.where(first, *pair) for pair in zip(grads0, grads1)]

    mine = jnp.where(first, y0, y1)
    block = jnp.stack([jnp.where(first, mine, theirs), jnp.where(first, theirs, mine)])[None, :, None]
    dx = jnp.where(first, *dxs)
    other = jnp.where(first, *lows).astype(f32)
    in_grads = jnp.stack([jnp.where(first, dx, other), jnp.where(first, other, dx)])[None, :, None]
    grads.insert(5, gain_grads(grads, w_qkv, w_gates, w_up, norm_gains))
    return (block, in_grads, *(grad[None] for grad in grads))


def run(x, own_seed, other_seed, masters, index, first, pick):
    width = x.shape[1]
    place = jnp.stack([index // 4, (index // 2) & 1, index & 1]).astype(jnp.int32)
    head, tail = pack(place, index, *masters)
    heads = pick(head, crossed(head))
    tails = pick(tail, crossed(after(tail, heads[0])))
    tail0 = lax.all_gather(tails[0], "dp", axis=0)

    def cores(z, y):
        return z, y, swapped(z, 1), swapped(y, 1)

    zh0 = jnp.stack(along_z(heads[0]))
    yh0 = swapped(zh0, 2)
    zh1 = along_z(after(heads[1], yh0))
    head0 = cores(zh0, yh0)
    n1, q, k, v, vec = qkv_forward(place, x, head0)
    zh1 = jnp.stack([after(part, n1) for part in zh1])
    yh1 = swapped(zh1, 2)
    o, s = attend_forward(place, q, k, v, 0, waits=(zh1,))
    o, s = attend_forward(place, q, k, v, 2, onto=(o, s))
    tail0 = after(tail0, o)
    tail1 = lax.all_gather(after(tails[1], tail0), "dp", axis=0)
    middle, n2, scale, ga, ta = gate_forward(place, 0, x, n1, o, vec, tail0)
    head1 = cores(after(zh1, n2), after(yh1, n2))
    y0, h, slope, gf, tf = feed_forward(place, 0, middle, n2, vec, tail0)
    other_seed = crossed(after(other_seed, n2))
    kept0 = (x, n1, q, k, v, vec, o, s, n2, scale, ga, ta, h, slope, gf, tf)

    n1, q, k, v, vec = qkv_forward(place, y0, head1)
    o, s = attend_forward(place, q, k, v, 0)
    o, s = attend_forward(place, q, k, v, 2, onto=(o, s))
    middle, n2, scale, ga, ta = gate_forward(place, 1, y0, n1, o, vec, tail1)
    y1, h, slope, gf, tf = feed_forward(place, 1, middle, n2, vec, tail1)
    theirs = crossed(jnp.where(first, y1, y0))

    seeds = pick(own_seed, after(other_seed, y1))
    dm1, df, dzf, du, da, dza1, do, small = feed_back(place, 1, [seeds[1]], n2, scale, ga, ta, slope, gf, tf, vec, tail1)
    rest1 = lax.psum_scatter(rest_grad(place, o, n1, n2, h, da, dza1, dzf, du, df, small), "dp", scatter_dimension=0)
    dqkv = attend_back(place, q, k, v, o, s, do, 0)
    dqkv = attend_back(place, q, k, v, o, s, do, 2, onto=dqkv)
    dx1, low1 = qkv_back(place, 1, y0, dm1, *dqkv, dza1, vec, head1, tail1, waits=(theirs,))
    early1 = (n1, *dqkv)
    other1 = crossed(low1, (0,))

    x, n1, q, k, v, vec, o, s, n2, scale, ga, ta, h, slope, gf, tf = kept0
    dm, df, dzf, du, da, dza, do, small = feed_back(
        place, 0, [seeds[0], low1], n2, scale, ga, ta, slope, gf, tf, vec, tail0
    )
    grad0 = rest_grad(place, o, n1, n2, h, da, dza, dzf, du, df, small, waits=(other1,))
    rest0 = lax.psum_scatter(grad0, "dp", scatter_dimension=0)
    dqkv = attend_back(place, q, k, v, o, s, do, 0)
    rest1 = after(rest1, dqkv[0])
    last1 = crossed(rest1, (0,))
    dqkv = attend_back(place, q, k, v, o, s, do, 2, onto=dqkv)
    keep, send = first_grad(place, (n1, *dqkv), early1, waits=(last1,))
    got = swapped(send, 1)
    dx0, low0 = qkv_back(place, 0, x, dm, *dqkv, dza, vec, head0, tail0, waits=(keep,))
    rest1 = rest1.astype(f32) + last1.astype(f32)
    away, near = fold_core(keep, after(got, low0))
    got = swapped(away, 2)
    other0 = crossed(after(low0, away), (1,))
    own, sends = fold_y(near, got)
    own = fold_z(own, [moved_z(part, at + 1) for at, part in enumerate(sends)])
    half = 3 * UNIT
    mine, theirs_early = jnp.where(first, own[:half], own[half:]), jnp.where(first, own[half:], own[:half])
    early = mine + crossed(theirs_early.astype(bf16)).astype(f32)
    rest0 = after(rest0, own)
    rest0 = rest0.astype(f32) + crossed(rest0, (1,)).astype(f32)
    later = jnp.where(first, rest0, rest1)
    grads = [
        jnp.concatenate([early[at * UNIT : (at + 1) * UNIT] for at in range(3)], axis=1),
        later[:UNIT],
        later[UNIT : 3 * UNIT].reshape(2, UNIT, width),
        jnp.concatenate([later[(3 + at) * UNIT : (4 + at) * UNIT] for at in range(4)], axis=1),
        later[7 * UNIT : REST],
        lax.dynamic_slice(later, (REST, index * UNIT), (2, UNIT)),
    ]
    return y0, y1, theirs, (dx0, dx1), (other0, other1), grads


def solution(mesh):
    placed = (
        P(None, "dp", None, None),
        P("section", None, "dp", None, None),
        P("section", "dp", None),
        P("section", "dp", None),
        P("section", None, "dp", None),
        P("section", "dp", None),
        P("section", "dp", None),
        P("section", None, "dp"),
        P("section", None, "dp"),
    )
    return jax.shard_map(
        per_device,
        mesh=mesh,
        in_specs=placed,
        out_specs=(P("section", None, "dp", None, None), P("section", None, "dp", None, None)) + placed[2:],
        check_vma=False,
    )
```

```python
import functools

import jax
import jax.numpy as jnp
from jax import lax
from jax.experimental import pallas as pl
from jax.experimental.pallas import tpu as pltpu
from jax.sharding import PartitionSpec as P

HD = 64
ROWS = 256
bf16 = jnp.bfloat16
f32 = jnp.float32
root_term = 0.7978845608
cube_term = 0.044715
VMEM = 56 * 1024 * 1024
PARTS = 16
UNIT = 32
FIRST = 3 * UNIT + 16
REST = 11 * UNIT


def dense(left, right):
    return jnp.dot(left, right, preferred_element_type=f32)


def cross(left, right):
    return lax.dot_general(left, right, (((0,), (0,)), ((), ())), preferred_element_type=f32)


def against(left, right):
    return lax.dot_general(left, right, (((1,), (1,)), ((), ())), preferred_element_type=f32)


def normalise(values):
    centred = values - jnp.mean(values, axis=-1, keepdims=True)
    spread = jnp.mean(centred * centred, axis=-1, keepdims=True)
    scale = lax.rsqrt(spread + 1e-05)
    return centred * scale, scale


def norm_back(grad, hat, scale, gain):
    spread = grad * gain
    first = jnp.mean(spread, axis=-1, keepdims=True)
    second = jnp.mean(spread * hat, axis=-1, keepdims=True)
    return scale * (spread - first - hat * second)


ANY = pl.BlockSpec(memory_space=pl.ANY)


def struct(shape, dtype):
    return jax.ShapeDtypeStruct(shape, dtype)


def rows_of(width):
    return pl.BlockSpec((ROWS, width), lambda i, place: (i, 0))


def whole(*shape):
    return pl.BlockSpec(shape, lambda i, place: (0,) * len(shape))


def call(kernel, grid, in_specs, out_specs, out_shape, scratch=(), flops=0, moved=0, waits=(), onto=()):
    extra = len(onto) + len(waits)
    count = len(in_specs)

    def run(*args):
        def body(*refs):
            kernel(*refs[: 1 + count], *refs[1 + count + extra :])

        return pl.pallas_call(
            body,
            grid_spec=pltpu.PrefetchScalarGridSpec(
                num_scalar_prefetch=1, grid=grid, in_specs=in_specs + [ANY] * extra, out_specs=out_specs, scratch_shapes=list(scratch)
            ),
            out_shape=out_shape,
            input_output_aliases={1 + count + at: at for at in range(len(onto))},
            compiler_params=pltpu.CompilerParams(dimension_semantics=("arbitrary",), vmem_limit_bytes=VMEM),
            cost_estimate=pl.CostEstimate(flops=flops, bytes_accessed=moved, transcendentals=0),
        )(*args, *onto, *waits)

    return run


def fetches(place, sources, target, sems, cuts, base=0):
    copies = []
    for number, (start, stop) in enumerate(cuts):
        group = []
        for index, source in enumerate(sources):
            for slot in range(4):
                part = ((place[0] - slot) & 3) * 4 + (place[1] ^ (index & 1)) * 2 + (place[2] ^ (index >> 1))
                group.append(
                    pltpu.make_async_copy(
                        source.at[slot, pl.ds(start, stop - start)],
                        target.at[part, pl.ds(start - base, stop - start)],
                        sems.at[number],
                    )
                )
        copies.append(group)
    return copies


def unit(ref, at):
    return ref[:, at * UNIT : (at + 1) * UNIT, :].reshape(PARTS * UNIT, ref.shape[2])


def down_part(ref, at, start=7):
    return ref[at * 4 : at * 4 + 4, start * UNIT : (start + 4) * UNIT, :].reshape(16 * UNIT, ref.shape[2])


def rest_copy(source, target, sem, start, stop, base):
    cut, goal = pl.ds(start, stop - start), pl.ds(start - base, stop - start)
    return pltpu.make_async_copy(source.at[:, cut], target.at[:, goal], sem)


def at_start(copies):
    @pl.when(pl.program_id(0) == 0)
    def _():
        for copy in copies:
            copy.start()
        for copy in copies:
            copy.wait()


def qkv_kernel(many, place, x_ref, *refs):
    n_ref, q_ref, k_ref, v_ref, vec_ref, buf, sems = refs[many:]
    copies = fetches(place, refs[:many], buf, sems, ((0, FIRST),))[0]

    @pl.when(pl.program_id(0) == 0)
    def _():
        for copy in copies:
            copy.start()
        for copy in copies:
            copy.wait()
        vec_ref[...] = jnp.sum(buf[:, 3 * UNIT : 3 * UNIT + 16, :].astype(f32), axis=0)

    hat, _ = normalise(x_ref[...].astype(f32))
    n1 = (hat * vec_ref[0:1, :]).astype(bf16)
    n_ref[...] = n1
    q_ref[...] = (dense(n1, unit(buf, 0)).astype(bf16) * 0.125).astype(bf16)
    k_ref[...] = dense(n1, unit(buf, 1)).astype(bf16)
    v_ref[...] = dense(n1, unit(buf, 2)).astype(bf16)


def qkv_forward(place, x, weights, waits=()):
    length, width = x.shape
    row = rows_of(width)
    return call(
        functools.partial(qkv_kernel, len(weights)),
        (length // ROWS,),
        [row] + [ANY] * len(weights),
        [row] * 4 + [whole(16, width)],
        [struct((length, width), bf16)] * 4 + [struct((16, width), f32)],
        [pltpu.VMEM((PARTS, FIRST, width), bf16), pltpu.SemaphoreType.DMA((1,))],
        flops=2 * length * width * 3 * width,
        moved=8_000_000,
        waits=waits,
    )(place, x, *weights)


def attend_kernel(block, place, q_ref, k_ref, v_ref, o_ref, s_ref):
    length = q_ref.shape[0]
    lane = lax.broadcasted_iota(jnp.int32, (block, 128), 1)
    row = lax.broadcasted_iota(jnp.int32, (block, block), 0)
    col = lax.broadcasted_iota(jnp.int32, (block, block), 1)
    for index in range(length // block):
        start, stop = index * block, (index + 1) * block
        q = q_ref[start:stop, :]
        outs, logs = [], []
        for head in range(2):
            mine = (lane >= head * HD) & (lane < (head + 1) * HD)
            own = jnp.where(mine, q, jnp.zeros_like(q))
            scores = against(own, k_ref[:stop, :])
            last = jnp.where(row >= col, scores[:, start:], -1e30)
            scores = jnp.concatenate([scores[:, :start], last], axis=1) if start else last
            highest = jnp.max(scores, axis=1, keepdims=True)
            weights = jnp.exp(scores - highest)
            total = jnp.sum(weights, axis=1, keepdims=True)
            outs.append(dense(weights.astype(bf16), v_ref[:stop, :]) * (1.0 / total))
            logs.append(highest + jnp.log(total))
        o_ref[start:stop, :] = jnp.where(lane < HD, outs[0], outs[1]).astype(bf16)
        s_ref[start:stop, :] = jnp.where(lane < HD, logs[0], logs[1])


def attend_forward(place, q, k, v, start, onto=(), waits=(), block=256):
    length, width = q.shape
    pair = pl.BlockSpec((length, 128), lambda i, place: (0, i + start))
    return call(
        functools.partial(attend_kernel, block),
        (width // 256,),
        [pair] * 3,
        [pair, pair],
        [struct((length, width), bf16), struct((length, width), f32)],
        flops=6_000_000_000,
        moved=3_000_000,
        onto=onto,
        waits=waits,
    )(place, q, k, v)


def gelu(u):
    square = u * u
    inner = jnp.tanh(u * (root_term + (root_term * cube_term) * square))
    half = 0.5 + 0.5 * inner
    slope = half + (0.5 * root_term) * u * (1.0 - inner * inner) * (1.0 + (3.0 * cube_term) * square)
    return u * half, slope


def gated_rows(x, n1, o, vec, buf):
    branch = dense(o, unit(buf, 0))
    opening = jax.nn.sigmoid(dense(n1, unit(buf, 1)) + vec[2:3, :])
    gated = opening * branch
    middle = x.astype(f32) + gated
    hat, scale = normalise(middle)
    n2 = (hat * vec[1:2, :]).astype(bf16)
    return middle, n2, hat, scale, opening, gated * (1.0 - opening)


def feed_rows(middle, n2, vec, buf, h_ref, slope_ref, at_rows):
    feed = None
    for at in range(4):
        cut = slice(at * 512, at * 512 + 512)
        active, slope = gelu(dense(n2, unit(buf, 3 + at)))
        active = active.astype(bf16)
        h_ref[at_rows, cut] = active
        slope_ref[:, cut] = slope.astype(bf16)
        part = dense(active, down_part(buf, at))
        feed = part if feed is None else feed + part
    closing = jax.nn.sigmoid(dense(n2, unit(buf, 2)) + vec[3:4, :])
    gated = closing * feed
    return middle + gated, closing, gated * (1.0 - closing)


def feed_kernel(place, x_ref, n1_ref, o_ref, vec_ref, rest_ref,
                y_ref, n2_ref, scale_ref, ga_ref, ta_ref, h_ref, slope_ref, gf_ref, tf_ref, buf, sems):
    at_start([rest_copy(rest_ref, buf, sems.at[0], 0, REST, 0)])
    vec = vec_ref[...]
    middle, n2, _, scale, ga, ta = gated_rows(x_ref[...], n1_ref[...], o_ref[...], vec, buf)
    ga_ref[...] = ga.astype(bf16)
    ta_ref[...] = ta.astype(bf16)
    n2_ref[...] = n2
    scale_ref[...] = jnp.broadcast_to(scale, scale_ref.shape)
    y, gf, tf = feed_rows(middle, n2, vec, buf, h_ref, slope_ref, slice(None))
    gf_ref[...] = gf.astype(bf16)
    tf_ref[...] = tf.astype(bf16)
    y_ref[...] = y.astype(bf16)


def feed_forward(place, x, n1, o, vec, rest, waits=()):
    length, width = x.shape
    wide = 4 * width
    row, half = rows_of(width), struct((length, width), bf16)
    big, bigs = rows_of(wide), struct((length, wide), bf16)
    return call(
        feed_kernel,
        (length // ROWS,),
        [row, row, row, whole(16, width), ANY],
        [row, row, rows_of(128), row, row, big, big, row, row],
        [half, half, struct((length, 128), f32), half, half, bigs, bigs, half, half],
        [pltpu.VMEM((PARTS, REST, width), bf16), pltpu.SemaphoreType.DMA((1,))],
        flops=2 * length * width * (3 * width + 2 * wide),
        moved=24_000_000,
        waits=waits,
    )(place, x, n1, o, vec, rest)


def back_rows(e, hat, scale, ga, ta, slope_ref, gf, tf, gain, buf, du_ref, at_rows):
    df = (e * gf).astype(bf16)
    dzf = (e * tf).astype(bf16)
    dn2 = against(dzf, unit(buf, 2))
    for at in range(4):
        cut = slice(at * 512, at * 512 + 512)
        du = (against(df, down_part(buf, at)) * slope_ref[:, cut].astype(f32)).astype(bf16)
        du_ref[at_rows, cut] = du
        dn2 = dn2 + against(du, unit(buf, 3 + at))
    dm = e + norm_back(dn2, hat, scale, gain)
    da = (dm * ga).astype(bf16)
    dza = (dm * ta).astype(bf16)
    return dm, df, dzf, da, dza, against(da, unit(buf, 0)).astype(bf16)


def put_lanes(swap, keep, send, values, rows, first):
    for y in range(2):
        low, high = (values[(y * 2 + c) * rows : (y * 2 + c + 1) * rows] for c in range(2))
        keep[y, first : first + rows, :] = jnp.where(swap, high, low)
        send[y, first : first + rows, :] = jnp.where(swap, low, high)


def rest_grads(place, keep, send, o, n1, n2, h, da, dza, dzf, du_ref, df, sums):
    put = functools.partial(put_lanes, place[2] == 1, keep, send)
    put(cross(o, da).astype(bf16), UNIT, 0)
    put(cross(n1, dza).astype(bf16), UNIT, UNIT)
    put(cross(n2, dzf).astype(bf16), UNIT, 2 * UNIT)
    for at in range(4):
        put(cross(n2, du_ref[:, at * 512 : at * 512 + 512]).astype(bf16), UNIT, (3 + at) * UNIT)
    put(cross(h, df).astype(bf16), 4 * UNIT, 7 * UNIT)
    small = jnp.concatenate([sums, jnp.zeros((8, sums.shape[1]), f32)], axis=0).astype(bf16)
    for ref in (keep, send):
        for y in range(2):
            ref[y, REST:, :] = small


def keep_rows(at_rows, refs, values):
    for ref, value in zip(refs, values):
        ref[at_rows, :] = value


def add_sums(sums, dza, dzf):
    rows = [jnp.sum(part.astype(f32), axis=0, keepdims=True) for part in (dza, dzf)]
    new = jnp.concatenate(rows + [jnp.zeros((6, dza.shape[1]), f32)], axis=0)
    sums[...] = jnp.where(pl.program_id(0) == 0, new, sums[...] + new)


def turn_kernel(count, place, x_ref, n1_ref, o_ref, e_ref, vec_ref, o_cols, n1_cols, rest_ref,
                y_ref, dm_ref, dza_ref, do_ref, keep, send, buf, h, du, slope, n2, df, dzf, da, dza, sums, sems):
    step = pl.program_id(0)
    at_start([rest_copy(rest_ref, buf, sems.at[0], 0, REST, 0)])

    @pl.when(step < count)
    def _():
        at_rows = pl.ds(pl.multiple_of(step * ROWS, ROWS), ROWS)
        vec = vec_ref[...]
        middle, low, hat, scale, ga, ta = gated_rows(x_ref[...], n1_ref[...], o_ref[...], vec, buf)
        y, gf, tf = feed_rows(middle, low, vec, buf, h, slope, at_rows)
        y_ref[...] = y.astype(bf16)
        e = e_ref[...].astype(f32)
        dm, *parts, grad_o = back_rows(e, hat, scale, ga, ta, slope, gf, tf, vec[1:2, :], buf, du, at_rows)
        dm_ref[...] = dm
        do_ref[...] = grad_o
        keep_rows(at_rows, (n2, df, dzf, da, dza), (low, *parts))
        dza_ref[...] = parts[3]
        add_sums(sums, parts[3], parts[1])

    @pl.when(step >= count)
    def _():
        at = step - count
        narrow, wide = pl.ds(pl.multiple_of(at * 128, 128), 128), pl.ds(pl.multiple_of(at * 512, 512), 512)
        lefts = (o_cols[...], n1_cols[...], n2[:, narrow], h[:, wide])
        rest_grads(place, keep, send, *lefts, da[...], dza[...], dzf[...], du, df[...], sums[...])


def late_specs(length, width, count):
    row = pl.BlockSpec((ROWS, width), lambda i, place: (jnp.minimum(i, count - 1), 0))
    cols = pl.BlockSpec((length, width // 4), lambda i, place: (0, jnp.maximum(i - count, 0)))
    grad = pl.BlockSpec((2, REST + 16, width), lambda i, place: (jnp.maximum(i - count, 0), 0, 0))
    return row, cols, grad


def turn(place, x, n1, o, e, vec, rest, waits=()):
    length, width = x.shape
    wide, count = 4 * width, length // ROWS
    row, cols, grad = late_specs(length, width, count)
    half, tall = struct((length, width), bf16), pltpu.VMEM((length, width), bf16)
    return call(
        functools.partial(turn_kernel, count),
        (count + 4,),
        [row] * 4 + [whole(16, width), cols, cols, ANY],
        [row] * 4 + [grad] * 2,
        [half, struct((length, width), f32), half, half] + [struct((PARTS // 2, REST + 16, width), bf16)] * 2,
        [pltpu.VMEM((PARTS, REST, width), bf16)]
        + [pltpu.VMEM((length, wide), bf16)] * 2
        + [pltpu.VMEM((ROWS, wide), bf16)]
        + [tall] * 5
        + [pltpu.VMEM((8, width), f32), pltpu.SemaphoreType.DMA((1,))],
        flops=6 * length * width * (3 * width + 2 * wide),
        moved=24_000_000,
        waits=waits,
    )(place, x, n1, o, e, vec, o, n1, rest)


def dx_rows(x, dm, dqkv, dza, gain, buf, gate):
    width = x.shape[1]
    dn = against(dza, gate[...].reshape(PARTS * UNIT, width))
    for at, part in enumerate(dqkv):
        dn = dn + against(part, unit(buf, at))
    hat, scale = normalise(x.astype(f32))
    return dm + norm_back(dn, hat, scale, gain)


def joint_kernel(count, many, place, x_ref, dm1_ref, dq_ref, dk_ref, dv_ref, dza1_ref, e_ref,
                 n2_ref, scale_ref, ga_ref, ta_ref, slope_ref, gf_ref, tf_ref, vec1_ref, vec_ref,
                 o_cols, n1_cols, n2_cols, h_cols, rest1_ref, rest_ref, *refs):
    dx_ref, low_ref, dm_ref, dza_ref, do_ref, keep, send, head, gate, buf, du, df, dzf, da, dza, sums, sems = refs[many:]
    step = pl.program_id(0)
    copies = fetches(place, refs[:many], head, sems, ((0, 3 * UNIT),))[0]
    copies.append(rest_copy(rest1_ref, gate, sems.at[1], UNIT, 2 * UNIT, UNIT))
    copies.append(rest_copy(rest_ref, buf, sems.at[2], 0, REST, 0))
    at_start(copies)

    @pl.when(step < count)
    def _():
        at_rows = pl.ds(pl.multiple_of(step * ROWS, ROWS), ROWS)
        dqkv = (dq_ref[...], dk_ref[...], dv_ref[...])
        dx = dx_rows(x_ref[...], dm1_ref[...], dqkv, dza1_ref[...], vec1_ref[0:1, :], head, gate)
        dx_ref[...] = dx
        low = dx.astype(bf16)
        low_ref[...] = low
        e = e_ref[...].astype(f32) + low.astype(f32)
        gain = vec_ref[1:2, :]
        hat = n2_ref[...].astype(f32) * (1.0 / gain)
        ga, ta, gf, tf = (ref[...].astype(f32) for ref in (ga_ref, ta_ref, gf_ref, tf_ref))
        dm, *parts, grad_o = back_rows(e, hat, scale_ref[:, 0:1], ga, ta, slope_ref, gf, tf, gain, buf, du, at_rows)
        dm_ref[...] = dm
        do_ref[...] = grad_o
        keep_rows(at_rows, (df, dzf, da, dza), parts)
        dza_ref[...] = parts[3]
        add_sums(sums, parts[3], parts[1])

    @pl.when(step >= count)
    def _():
        lefts = (o_cols[...], n1_cols[...], n2_cols[...], h_cols[...])
        rest_grads(place, keep, send, *lefts, da[...], dza[...], dzf[...], du, df[...], sums[...])


def joint_back(place, x, dm1, dqkv, dza1, vec1, head, rest1, e, kept, rest, waits=()):
    n1, o, vec, n2, scale, ga, ta, h, slope, gf, tf = kept
    length, width = x.shape
    wide, count = 4 * width, length // ROWS
    row, cols, grad = late_specs(length, width, count)
    lanes = pl.BlockSpec((ROWS, 128), lambda i, place: (jnp.minimum(i, count - 1), 0))
    big = pl.BlockSpec((ROWS, wide), lambda i, place: (jnp.minimum(i, count - 1), 0))
    wides = pl.BlockSpec((length, wide // 4), lambda i, place: (0, jnp.maximum(i - count, 0)))
    half, tall = struct((length, width), bf16), pltpu.VMEM((length, width), bf16)
    floats = struct((length, width), f32)
    return call(
        functools.partial(joint_kernel, count, len(head)),
        (count + 4,),
        [row] * 8 + [lanes, row, row, big, row, row, whole(16, width), whole(16, width), cols, cols, cols, wides, ANY, ANY]
        + [ANY] * len(head),
        [row] * 5 + [grad] * 2,
        [floats, half, floats, half, half] + [struct((PARTS // 2, REST + 16, width), bf16)] * 2,
        [pltpu.VMEM((PARTS, 3 * UNIT, width), bf16), pltpu.VMEM((PARTS, UNIT, width), bf16), pltpu.VMEM((PARTS, REST, width), bf16)]
        + [pltpu.VMEM((length, wide), bf16)]
        + [tall] * 4
        + [pltpu.VMEM((8, width), f32), pltpu.SemaphoreType.DMA((3,))],
        flops=4 * length * width * (5 * width + 2 * wide),
        moved=40_000_000,
        waits=waits,
    )(place, x, dm1, *dqkv, dza1, e, n2, scale, ga, ta, slope, gf, tf, vec1, vec, o, n1, n2, h, rest1, rest, *head)


def split3(value):
    first = value.astype(bf16)
    rest = value - first.astype(f32)
    second = rest.astype(bf16)
    third = (rest - second.astype(f32)).astype(bf16)
    return first, second, third


def attend_back_kernel(block, place, q_ref, k_ref, v_ref, o_ref, s_ref, do_ref, dq_ref, dk_ref, dv_ref,
                       q_s, k_s, v_s, do_s, acc):
    length = q_ref.shape[0]
    lane = lax.broadcasted_iota(jnp.int32, (length, 128), 1)
    row = lax.broadcasted_iota(jnp.int32, (block, block), 0)
    col = lax.broadcasted_iota(jnp.int32, (block, block), 1)
    q, k, v, do = q_ref[...], k_ref[...], v_ref[...], do_ref[...]
    zero = jnp.zeros_like(q)
    product = do.astype(f32) * o_ref[...].astype(f32)
    for head in range(2):
        low = head * HD
        other = (1 - head) * HD
        mine = (lane >= low) & (lane < low + HD)
        logs = -s_ref[:, low : low + 1]
        delta = -jnp.sum(jnp.where(mine, product, 0.0), axis=1, keepdims=True)
        one = jnp.where((lane >= other) & (lane < other + 3), jnp.ones_like(q), zero)
        q_aug, do_aug = jnp.where(mine, q, zero), jnp.where(mine, do, zero)
        for at, (part, piece) in enumerate(zip(split3(logs), split3(delta))):
            here = lane == other + at
            q_aug = jnp.where(here, part, q_aug)
            do_aug = jnp.where(here, piece, do_aug)
        q_s[head] = q_aug
        do_s[head] = do_aug
        k_s[head] = jnp.where(mine, k, one)
        v_s[head] = jnp.where(mine, v, one)
    for index in range(length // block):
        start, stop = index * block, (index + 1) * block
        kgrads, vgrads = [], []
        for head in range(2):
            kb, vb = k_s[head, start:stop, :], v_s[head, start:stop, :]
            scores = against(kb, q_s[head, start:, :])
            first = jnp.where(row <= col, scores[:, :block], -1e30)
            scores = jnp.concatenate([first, scores[:, block:]], axis=1) if stop < length else first
            probs = jnp.exp(scores)
            grads = (probs * against(vb, do_s[head, start:, :])).astype(bf16)
            vgrads.append(dense(probs.astype(bf16), do_ref[start:, :]))
            kgrads.append(dense(grads, q_ref[start:, :]))
            part = cross(grads, kb)
            if index == 0:
                acc[head] = part
            else:
                acc[head, start:, :] += part
        half = lane[:block] < HD
        dk_ref[start:stop, :] = jnp.where(half, kgrads[0], kgrads[1]).astype(bf16)
        dv_ref[start:stop, :] = jnp.where(half, vgrads[0], vgrads[1]).astype(bf16)
    dq_ref[...] = (jnp.where(lane < HD, acc[0], acc[1]) * 0.125).astype(bf16)


def attend_back(place, q, k, v, o, s, do, start, count=2, onto=(), waits=(), block=256):
    length, width = q.shape
    pair = pl.BlockSpec((length, 128), lambda i, place: (0, i + start))
    return call(
        functools.partial(attend_back_kernel, block),
        (count,),
        [pair] * 6,
        [pair] * 3,
        [struct((length, width), bf16)] * 3,
        [pltpu.VMEM((2, length, 128), bf16)] * 4 + [pltpu.VMEM((2, length, 128), f32)],
        flops=5_000_000_000 * count,
        moved=5_000_000,
        onto=onto,
        waits=waits,
    )(place, q, k, v, o, s, do)


def qkv_back_kernel(many, place, x_ref, dm_ref, dq_ref, dk_ref, dv_ref, dza_ref, vec_ref, rest_ref, *refs):
    dx_ref, low_ref, buf, gate, sems = refs[many:]
    copies = fetches(place, refs[:many], buf, sems, ((0, 3 * UNIT),))[0]
    at_start(copies + [rest_copy(rest_ref, gate, sems.at[1], UNIT, 2 * UNIT, UNIT)])
    dqkv = (dq_ref[...], dk_ref[...], dv_ref[...])
    dx = dx_rows(x_ref[...], dm_ref[...], dqkv, dza_ref[...], vec_ref[0:1, :], buf, gate)
    dx_ref[...] = dx
    low_ref[...] = dx.astype(bf16)


def qkv_back(place, x, dm, dq, dk, dv, dza, vec, weights, rest, waits=()):
    length, width = x.shape
    row = rows_of(width)
    return call(
        functools.partial(qkv_back_kernel, len(weights)),
        (length // ROWS,),
        [row] * 6 + [whole(16, width), ANY] + [ANY] * len(weights),
        [row, row],
        [struct((length, width), f32), struct((length, width), bf16)],
        [pltpu.VMEM((PARTS, 3 * UNIT, width), bf16), pltpu.VMEM((PARTS, UNIT, width), bf16), pltpu.SemaphoreType.DMA((2,))],
        flops=2 * length * width * 4 * width,
        moved=12_000_000,
        waits=waits,
    )(place, x, dm, dq, dk, dv, dza, vec, rest, *weights)


def put(place, outs, values, rows, first):
    keep, send = outs
    for y in range(2):
        low, high = (values[(y * 2 + c) * rows : (y * 2 + c + 1) * rows] for c in range(2))
        at = place[1] ^ y
        swap = place[2] == 1
        keep[at, 0, first : first + rows, :] = jnp.where(swap, high, low)
        send[at, 0, first : first + rows, :] = jnp.where(swap, low, high)


def grad_outs(rows, width):
    out = pl.BlockSpec((2, 1, rows, width), lambda i, place: (0, (i - place[0]) & 3, 0, 0))
    return [out, out], [struct((2, 4, rows, width), bf16)] * 2


def first_grad_kernel(place, *refs):
    outs = refs[-2:]
    for layer in range(len(refs) // 4):
        n1_ref = refs[4 * layer]
        for at, ref in enumerate(refs[4 * layer + 1 : 4 * layer + 4]):
            put(place, outs, cross(n1_ref[...], ref[...]).astype(bf16), UNIT, (3 * layer + at) * UNIT)


def first_grad(place, *layers, waits=()):
    length, width = layers[0][0].shape
    cols = pl.BlockSpec((length, width // 4), lambda i, place: (0, i))
    specs, shapes = grad_outs(3 * UNIT * len(layers), width)
    return call(
        first_grad_kernel,
        (4,),
        ([cols] + [whole(length, width)] * 3) * len(layers),
        specs,
        shapes,
        flops=2 * length * width * 3 * width * len(layers),
        moved=9_000_000 * len(layers),
        waits=waits,
    )(place, *(value for layer in layers for value in layer))


def moved_z(value, steps):
    count = lax.axis_size("dp")
    return lax.ppermute(value, "dp", [(d, (d + 4 * steps) % count) for d in range(count)])


def swapped(value, bit):
    return lax.ppermute(value, "dp", [(d, d ^ bit) for d in range(lax.axis_size("dp"))])


def crossed(value, sources=(0, 1)):
    return lax.ppermute(value, "section", [(s, 1 - s) for s in sources])


def along_z(block):
    return [block] + [moved_z(block, k) for k in (1, 2, 3)]


def across(own):
    beside = swapped(own, 2)
    return own, beside, swapped(own, 1), swapped(beside, 1)


def spread_whole(blocks):
    blocks = blocks.reshape(4, 2, 2, *blocks.shape[1:])
    blocks = jnp.stack([blocks[0], blocks[3], blocks[2], blocks[1]])
    return tuple(blocks[:, index & 1, index >> 1] for index in range(4))


def gather_whole(values, axis):
    values = lax.all_gather(values.astype(bf16), "dp", axis=axis, tiled=True)
    return lax.all_gather(values, "section", axis=0, tiled=True)


def split_rows(matrix, cols):
    rows, width = matrix.shape[0] // PARTS, matrix.shape[1] // cols
    return matrix.reshape(PARTS, rows, cols, width).transpose(0, 2, 1, 3).reshape(PARTS, cols * rows, width)


def merge_rows(blocks, cols):
    rows, width = blocks.shape[1] // cols, blocks.shape[2]
    return blocks.reshape(PARTS, cols, rows, width).transpose(0, 2, 1, 3).reshape(PARTS * rows, cols * width)


def weights_whole(w_qkv, w_out, w_gates, w_up, w_down, gains, biases):
    w_qkv, w_out, w_up, w_down = (gather_whole(w, 1) for w in (w_qkv, w_out, w_up, w_down))
    w_gates, gains, biases = (gather_whole(w, 2) for w in (w_gates, gains, biases))
    heads, tails = [], []
    for layer in range(2):
        lines = jnp.concatenate([gains[layer], biases[layer], jnp.zeros((12, gains.shape[2]), bf16)], axis=0)
        lines = jnp.concatenate([lines[None], jnp.zeros((PARTS - 1, *lines.shape), bf16)], axis=0)
        heads.append(spread_whole(jnp.concatenate([split_rows(w_qkv[layer], 3), lines], axis=1)))
        parts = [w_out[layer], w_gates[layer, 0], w_gates[layer, 1]]
        parts = [split_rows(part, 1) for part in parts] + [split_rows(w_up[layer], 4), split_rows(w_down[layer], 1)]
        tails.append(jnp.concatenate(parts, axis=1))
    return heads, tails


def joined(pieces):
    return jnp.stack(pieces).transpose(2, 1, 0, 3, 4).reshape(PARTS, *pieces[0].shape[2:])


def collect_whole(early, rest):
    early, rest = joined(early), jnp.stack(rest, axis=1).reshape(PARTS, *rest[0].shape[1:])
    parts = [merge_rows(early, 3), merge_rows(rest[:, :UNIT], 1)]
    parts += [jnp.stack([merge_rows(rest[:, at * UNIT : (at + 1) * UNIT], 1) for at in (1, 2)])]
    parts += [merge_rows(rest[:, 3 * UNIT : 7 * UNIT], 4), merge_rows(rest[:, 7 * UNIT : REST], 1), rest[0, REST : REST + 2]]
    axes = (0, 0, 1, 0, 0, 1)
    parts = [lax.psum_scatter(part.astype(f32), "dp", scatter_dimension=axis, tiled=True) for part, axis in zip(parts, axes)]
    return [lax.psum(part, "section") for part in parts]


def fold_core(keep, got):
    away = (keep[1].astype(f32) + got[1].astype(f32)).astype(bf16)
    return away, keep[0].astype(f32) + got[0].astype(f32)


def scattered(keep, got):
    lanes = [[d for d in range(PARTS) if d % 2 == c] for c in range(2)]
    both = (keep.astype(f32) + got.astype(f32)).astype(bf16)
    return lax.psum_scatter(both, "dp", scatter_dimension=0, axis_index_groups=lanes)


def fold_y(near, got):
    near = near + got.astype(f32)
    return near[0], [near[k].astype(bf16) for k in (1, 2, 3)]


def fold_z(total, gots):
    for got in gots:
        total = total + got.astype(f32)
    return total


def pack_kernel(place, qkv_ref, out_ref, gates_ref, up_ref, down_ref, lines_ref, head_ref, tail_ref):
    width = out_ref.shape[2]
    for at in range(3):
        head_ref[at * UNIT : (at + 1) * UNIT, :] = qkv_ref[0, :, at * width : (at + 1) * width].astype(bf16)
    head_ref[3 * UNIT :, :] = lines_ref[...].astype(bf16)
    tail_ref[:UNIT, :] = out_ref[0].astype(bf16)
    for at in range(2):
        tail_ref[(1 + at) * UNIT : (2 + at) * UNIT, :] = gates_ref[0, at].astype(bf16)
    for at in range(4):
        tail_ref[(3 + at) * UNIT : (4 + at) * UNIT, :] = up_ref[0, :, at * width : (at + 1) * width].astype(bf16)
    tail_ref[7 * UNIT :, :] = down_ref[0].astype(bf16)


def pack(place, index, w_qkv, w_out, w_gates, w_up, w_down, gains, biases):
    width = w_out.shape[2]
    lines = jnp.concatenate([gains[0], biases[0]], axis=0)
    mine = jnp.arange(width)[None, :] // UNIT == index
    lines = jnp.concatenate([jnp.where(mine, jnp.tile(lines, (1, PARTS)), 0.0), jnp.zeros((12, width), f32)], axis=0)
    arrays = (w_qkv, w_out, w_gates, w_up, w_down, lines)
    return call(
        pack_kernel,
        (1,),
        [whole(*array.shape) for array in arrays],
        [whole(FIRST, width), whole(REST, width)],
        [struct((FIRST, width), bf16), struct((REST, width), bf16)],
        moved=3_000_000,
    )(place, *arrays)


def after(value, *others):
    return lax.optimization_barrier((value, *others))[0]


def gain_grads(grads, w_qkv, w_gates, w_up, gains):
    d_qkv, _, d_gates, d_up = grads[:4]
    w_qkv, w_gates, w_up, gains = (w[0].astype(bf16).astype(f32) for w in (w_qkv, w_gates, w_up, gains))
    first = jnp.sum(w_qkv * d_qkv, axis=1) + jnp.sum(w_gates[0] * d_gates[0], axis=1)
    second = jnp.sum(w_up * d_up, axis=1) + jnp.sum(w_gates[1] * d_gates[1], axis=1)
    return jnp.stack([first, second]) / gains


def per_device(tokens, cotangent, w_qkv, w_out, w_gates, w_up, w_down, norm_gains, gate_biases):
    section = lax.axis_index("section")
    index = lax.axis_index("dp")
    fast = lax.axis_size("dp") == PARTS
    first = section == 0
    masters = (w_qkv, w_out, w_gates, w_up, w_down, norm_gains, gate_biases)

    def pick(own, other):
        return jnp.where(first, own, other), jnp.where(first, other, own)

    x = jnp.where(first, tokens[0, 0], tokens[1, 0])
    seeds = [cotangent[0, m, 0] for m in range(2)]
    own_seed, other_seed = jnp.where(first, seeds[0], seeds[1]), jnp.where(first, seeds[1], seeds[0])
    if fast:
        y0, y1, theirs, dxs, lows, grads = run(x, own_seed, other_seed, masters, index, first, pick)
    else:
        place = jnp.zeros((3,), jnp.int32)
        heads, rest = weights_whole(*masters)
        n0, q0, k0, v0, vec0 = qkv_forward(place, x, heads[0])
        o0, s0 = attend_forward(place, q0, k0, v0, 2, onto=attend_forward(place, q0, k0, v0, 0))
        y0, *kept = feed_forward(place, x, n0, o0, vec0, rest[0])
        n1, q1, k1, v1, vec1 = qkv_forward(place, y0, heads[1])
        o1, s1 = attend_forward(place, q1, k1, v1, 2, onto=attend_forward(place, q1, k1, v1, 0))
        seeds = pick(own_seed, crossed(other_seed))
        y1, dm, dza, do, *later1 = turn(place, y0, n1, o1, seeds[1], vec1, rest[1])
        dqkv = attend_back(place, q1, k1, v1, o1, s1, do, 2, onto=attend_back(place, q1, k1, v1, o1, s1, do, 0))
        early1 = first_grad(place, (n1, *dqkv))
        dx1, low1, dm, dza, do, *later0 = joint_back(
            place, y0, dm, dqkv, dza, vec1, heads[1], rest[1], seeds[0], (n0, o0, vec0, *kept), rest[0]
        )
        dqkv = attend_back(place, q0, k0, v0, o0, s0, do, 2, onto=attend_back(place, q0, k0, v0, o0, s0, do, 0))
        early0 = first_grad(place, (n0, *dqkv))
        dx0, low0 = qkv_back(place, x, dm, *dqkv, dza, vec0, heads[0], rest[0])
        grads0, grads1 = collect_whole(early0, later0), collect_whole(early1, later1)
        dxs, lows = (dx0, dx1), (crossed(low0, (1,)), crossed(low1, (0,)))
        theirs = crossed(jnp.where(first, y1, y0))
        grads = [jnp.where(first, *pair) for pair in zip(grads0, grads1)]

    mine = jnp.where(first, y0, y1)
    block = jnp.stack([jnp.where(first, mine, theirs), jnp.where(first, theirs, mine)])[None, :, None]
    in_grads = jnp.stack([jnp.where(first, dxs[0], lows[1].astype(f32)), dxs[1]])
    last = jnp.where(first, lows[0].astype(f32), dxs[1])
    in_grads = lax.dynamic_update_slice(in_grads, last[None], (1, 0, 0))[None, :, None]
    grads.insert(5, gain_grads(grads, w_qkv, w_gates, w_up, norm_gains))
    return (block, in_grads, *(grad[None] for grad in grads))


def run(x, own_seed, other_seed, masters, index, first, pick):
    width = x.shape[1]
    place = jnp.stack([index // 4, (index // 2) & 1, index & 1]).astype(jnp.int32)
    head, tail = pack(place, index, *masters)
    heads = pick(head, crossed(head))
    tails = pick(tail, crossed(tail))
    tail0 = lax.all_gather(tails[0], "dp", axis=0)

    def cores(z, y):
        return z, y, swapped(z, 1), swapped(y, 1)

    zh0 = jnp.stack(along_z(heads[0]))
    yh0 = swapped(zh0, 2)
    zh1 = along_z(after(heads[1], yh0))
    head0 = cores(zh0, yh0)
    n1, q, k, v, vec = qkv_forward(place, x, head0)
    o, s = attend_forward(place, q, k, v, 0)
    zh1 = jnp.stack([after(part, o) for part in zh1])
    yh1 = swapped(zh1, 2)
    o, s = attend_forward(place, q, k, v, 2, onto=(o, s), waits=(zh1,))
    tail0 = after(tail0, o)
    tail1 = lax.all_gather(after(tails[1], tail0), "dp", axis=0)
    other_seed = crossed(after(other_seed, o))
    y0, *held = feed_forward(place, x, n1, o, vec, tail0)
    head1 = cores(after(zh1, y0), after(yh1, y0))
    kept0 = (n1, o, vec, *held)
    layer0 = (q, k, v, o, s)

    n1, q, k, v, vec = qkv_forward(place, y0, head1)
    o, s = attend_forward(place, q, k, v, 0)
    o, s = attend_forward(place, q, k, v, 2, onto=(o, s))
    seeds = pick(own_seed, after(other_seed, o))
    y1, dm, dza, do, keep, send = turn(place, y0, n1, o, seeds[1], vec, tail1)
    got = swapped(send, 1)
    theirs = crossed(jnp.where(first, y1, y0))
    dqkv = attend_back(place, q, k, v, o, s, do, 0)
    rest1 = scattered(keep, after(got, dqkv[0]))
    dqkv = attend_back(place, q, k, v, o, s, do, 2, onto=dqkv)
    keep_b, send_b = first_grad(place, (n1, *dqkv))
    got_b = swapped(send_b, 1)
    dx1, low1, dm, dza, do, keep, send = joint_back(
        place, y0, dm, dqkv, dza, vec, head1, tail1, seeds[0], kept0, tail0, waits=(keep_b,)
    )
    n1, o, vec = kept0[:3]
    q, k, v, o, s = layer0
    got = swapped(send, 1)
    away, near = fold_core(keep_b, after(got_b, low1))
    got_b = swapped(away, 2)
    other1 = crossed(low1, (0,))
    dqkv = attend_back(place, q, k, v, o, s, do, 0, 1, waits=(away,))
    rest1 = after(rest1, dqkv[0])
    rest0 = scattered(keep, after(got, dqkv[0]))
    own, sends = fold_y(near, after(got_b, dqkv[0]))
    gots = [moved_z(part, at + 1) for at, part in enumerate(sends)]
    dqkv = attend_back(place, q, k, v, o, s, do, 1, 3, onto=dqkv, waits=(theirs, *sends))
    early1 = fold_z(own, [after(got, dqkv[0]) for got in gots])
    low = jnp.concatenate([rest1, early1.astype(bf16)])
    last1 = crossed(low, (0,))
    keep, send = first_grad(place, (n1, *dqkv), waits=(other1, low))
    got = swapped(send, 1)
    away, near = fold_core(keep, got)
    got = swapped(away, 2)
    dx0, low0 = qkv_back(place, x, dm, *dqkv, dza, vec, head0, tail0, waits=(away,))
    last1 = after(last1, low0).astype(f32)
    rest1, early1 = rest1.astype(f32) + last1[: REST + 16], early1 + last1[REST + 16 :]
    other0 = crossed(low0, (1,))
    own, sends = fold_y(near, after(got, low0))
    gots = [moved_z(part, at + 1) for at, part in enumerate(sends)]
    early0 = fold_z(own, gots)
    early0 = early0 + crossed(early0.astype(bf16), (1,)).astype(f32)
    early = jnp.where(first, early0, early1)
    rest0 = after(rest0, gots[0])
    rest0 = rest0.astype(f32) + crossed(rest0, (1,)).astype(f32)
    later = jnp.where(first, rest0, rest1)
    grads = [
        jnp.concatenate([early[at * UNIT : (at + 1) * UNIT] for at in range(3)], axis=1),
        later[:UNIT],
        later[UNIT : 3 * UNIT].reshape(2, UNIT, width),
        jnp.concatenate([later[(3 + at) * UNIT : (4 + at) * UNIT] for at in range(4)], axis=1),
        later[7 * UNIT : REST],
        lax.dynamic_slice(later, (REST, index * UNIT), (2, UNIT)),
    ]
    return y0, y1, theirs, (dx0, dx1), (other0, other1), grads


def solution(mesh):
    placed = (
        P(None, "dp", None, None),
        P("section", None, "dp", None, None),
        P("section", "dp", None),
        P("section", "dp", None),
        P("section", None, "dp", None),
        P("section", "dp", None),
        P("section", "dp", None),
        P("section", None, "dp"),
        P("section", None, "dp"),
    )
    return jax.shard_map(
        per_device,
        mesh=mesh,
        in_specs=placed,
        out_specs=(P("section", None, "dp", None, None), P("section", None, "dp", None, None)) + placed[2:],
        check_vma=False,
    )
```

```python
import functools

import jax
import jax.numpy as jnp
from jax import lax
from jax.experimental import pallas as pl
from jax.experimental.pallas import tpu as pltpu
from jax.sharding import PartitionSpec as P

HD = 64
ROWS = 512
bf16 = jnp.bfloat16
f32 = jnp.float32
root_term = 0.7978845608
cube_term = 0.044715
VMEM = 56 * 1024 * 1024
PARTS = 16
UNIT = 32
FIRST = 3 * UNIT + 16
REST = 11 * UNIT


def dense(left, right):
    return jnp.dot(left, right, preferred_element_type=f32)


def cross(left, right):
    return lax.dot_general(left, right, (((0,), (0,)), ((), ())), preferred_element_type=f32)


def against(left, right):
    return lax.dot_general(left, right, (((1,), (1,)), ((), ())), preferred_element_type=f32)


def normalise(values):
    centred = values - jnp.mean(values, axis=-1, keepdims=True)
    spread = jnp.mean(centred * centred, axis=-1, keepdims=True)
    scale = lax.rsqrt(spread + 1e-05)
    return centred * scale, scale


def norm_back(grad, hat, scale, gain):
    spread = grad * gain
    first = jnp.mean(spread, axis=-1, keepdims=True)
    second = jnp.mean(spread * hat, axis=-1, keepdims=True)
    return scale * (spread - first - hat * second)


ANY = pl.BlockSpec(memory_space=pl.ANY)


def struct(shape, dtype):
    return jax.ShapeDtypeStruct(shape, dtype)


def rows_of(width):
    return pl.BlockSpec((ROWS, width), lambda i, place: (i, 0))


def whole(*shape):
    return pl.BlockSpec(shape, lambda i, place: (0,) * len(shape))


def call(kernel, grid, in_specs, out_specs, out_shape, scratch=(), flops=0, moved=0, waits=(), onto=()):
    extra = len(onto) + len(waits)
    count = len(in_specs)

    def run(*args):
        def body(*refs):
            kernel(*refs[: 1 + count], *refs[1 + count + extra :])

        return pl.pallas_call(
            body,
            grid_spec=pltpu.PrefetchScalarGridSpec(
                num_scalar_prefetch=1, grid=grid, in_specs=in_specs + [ANY] * extra, out_specs=out_specs, scratch_shapes=list(scratch)
            ),
            out_shape=out_shape,
            input_output_aliases={1 + count + at: at for at in range(len(onto))},
            compiler_params=pltpu.CompilerParams(dimension_semantics=("arbitrary",), vmem_limit_bytes=VMEM),
            cost_estimate=pl.CostEstimate(flops=flops, bytes_accessed=moved, transcendentals=0),
        )(*args, *onto, *waits)

    return run


def fetches(place, sources, target, sems, cuts, base=0):
    copies = []
    for number, (start, stop) in enumerate(cuts):
        group = []
        for index, source in enumerate(sources):
            for slot in range(4):
                part = ((place[0] - slot) & 3) * 4 + (place[1] ^ (index & 1)) * 2 + (place[2] ^ (index >> 1))
                group.append(
                    pltpu.make_async_copy(
                        source.at[slot, pl.ds(start, stop - start)],
                        target.at[part, pl.ds(start - base, stop - start)],
                        sems.at[number],
                    )
                )
        copies.append(group)
    return copies


def unit(ref, at):
    return ref[:, at * UNIT : (at + 1) * UNIT, :].reshape(PARTS * UNIT, ref.shape[2])


def down_part(ref, at, start=7):
    return ref[at * 4 : at * 4 + 4, start * UNIT : (start + 4) * UNIT, :].reshape(16 * UNIT, ref.shape[2])


def rest_copy(source, target, sem, start, stop, base):
    cut, goal = pl.ds(start, stop - start), pl.ds(start - base, stop - start)
    return pltpu.make_async_copy(source.at[:, cut], target.at[:, goal], sem)


def at_start(copies):
    @pl.when(pl.program_id(0) == 0)
    def _():
        for copy in copies:
            copy.start()
        for copy in copies:
            copy.wait()


def qkv_kernel(many, place, x_ref, *refs):
    n_ref, q_ref, k_ref, v_ref, vec_ref, buf, sems = refs[many:]
    copies = fetches(place, refs[:many], buf, sems, ((0, FIRST),))[0]

    @pl.when(pl.program_id(0) == 0)
    def _():
        for copy in copies:
            copy.start()
        for copy in copies:
            copy.wait()
        vec_ref[...] = jnp.sum(buf[:, 3 * UNIT : 3 * UNIT + 16, :].astype(f32), axis=0)

    hat, _ = normalise(x_ref[...].astype(f32))
    n1 = (hat * vec_ref[0:1, :]).astype(bf16)
    n_ref[...] = n1
    q_ref[...] = (dense(n1, unit(buf, 0)).astype(bf16) * 0.125).astype(bf16)
    k_ref[...] = dense(n1, unit(buf, 1)).astype(bf16)
    v_ref[...] = dense(n1, unit(buf, 2)).astype(bf16)


def qkv_forward(place, x, weights, waits=()):
    length, width = x.shape
    row = rows_of(width)
    return call(
        functools.partial(qkv_kernel, len(weights)),
        (length // ROWS,),
        [row] + [ANY] * len(weights),
        [row] * 4 + [whole(16, width)],
        [struct((length, width), bf16)] * 4 + [struct((16, width), f32)],
        [pltpu.VMEM((PARTS, FIRST, width), bf16), pltpu.SemaphoreType.DMA((1,))],
        flops=2 * length * width * 3 * width,
        moved=8_000_000,
        waits=waits,
    )(place, x, *weights)


def attend_kernel(block, place, q_ref, k_ref, v_ref, o_ref, s_ref):
    length = q_ref.shape[0]
    lane = lax.broadcasted_iota(jnp.int32, (block, 128), 1)
    row = lax.broadcasted_iota(jnp.int32, (block, block), 0)
    col = lax.broadcasted_iota(jnp.int32, (block, block), 1)
    for index in range(length // block):
        start, stop = index * block, (index + 1) * block
        q = q_ref[start:stop, :]
        outs, logs = [], []
        for head in range(2):
            mine = (lane >= head * HD) & (lane < (head + 1) * HD)
            own = jnp.where(mine, q, jnp.zeros_like(q))
            scores = against(own, k_ref[:stop, :])
            last = jnp.where(row >= col, scores[:, start:], -1e30)
            scores = jnp.concatenate([scores[:, :start], last], axis=1) if start else last
            highest = jnp.max(scores, axis=1, keepdims=True)
            weights = jnp.exp(scores - highest)
            total = jnp.sum(weights, axis=1, keepdims=True)
            outs.append(dense(weights.astype(bf16), v_ref[:stop, :]) * (1.0 / total))
            logs.append(highest + jnp.log(total))
        o_ref[start:stop, :] = jnp.where(lane < HD, outs[0], outs[1]).astype(bf16)
        s_ref[start:stop, :] = jnp.where(lane < HD, logs[0], logs[1])


def attend_forward(place, q, k, v, start, onto=(), waits=(), block=256):
    length, width = q.shape
    pair = pl.BlockSpec((length, 128), lambda i, place: (0, i + start))
    return call(
        functools.partial(attend_kernel, block),
        (width // 256,),
        [pair] * 3,
        [pair, pair],
        [struct((length, width), bf16), struct((length, width), f32)],
        flops=6_000_000_000,
        moved=3_000_000,
        onto=onto,
        waits=waits,
    )(place, q, k, v)


def gelu(u):
    square = u * u
    inner = jnp.tanh(u * (root_term + (root_term * cube_term) * square))
    half = 0.5 + 0.5 * inner
    slope = half + (0.5 * root_term) * u * (1.0 - inner * inner) * (1.0 + (3.0 * cube_term) * square)
    return u * half, slope


def gated_rows(x, n1, o, vec, buf):
    branch = dense(o, unit(buf, 0))
    opening = jax.nn.sigmoid(dense(n1, unit(buf, 1)) + vec[2:3, :])
    gated = opening * branch
    middle = x.astype(f32) + gated
    hat, scale = normalise(middle)
    n2 = (hat * vec[1:2, :]).astype(bf16)
    return middle, n2, hat, scale, opening, gated * (1.0 - opening)


def feed_rows(middle, n2, vec, buf, h_ref, slope_ref, at_rows):
    feed = None
    for at in range(4):
        cut = slice(at * 512, at * 512 + 512)
        active, slope = gelu(dense(n2, unit(buf, 3 + at)))
        active = active.astype(bf16)
        h_ref[at_rows, cut] = active
        slope_ref[:, cut] = slope.astype(bf16)
        part = dense(active, down_part(buf, at))
        feed = part if feed is None else feed + part
    closing = jax.nn.sigmoid(dense(n2, unit(buf, 2)) + vec[3:4, :])
    gated = closing * feed
    return middle + gated, closing, gated * (1.0 - closing)


def feed_kernel(place, x_ref, n1_ref, o_ref, vec_ref, rest_ref,
                y_ref, n2_ref, scale_ref, ga_ref, ta_ref, h_ref, slope_ref, gf_ref, tf_ref, buf, sems):
    at_start([rest_copy(rest_ref, buf, sems.at[0], 0, REST, 0)])
    vec = vec_ref[...]
    middle, n2, _, scale, ga, ta = gated_rows(x_ref[...], n1_ref[...], o_ref[...], vec, buf)
    ga_ref[...] = ga.astype(bf16)
    ta_ref[...] = ta.astype(bf16)
    n2_ref[...] = n2
    scale_ref[...] = jnp.broadcast_to(scale, scale_ref.shape)
    y, gf, tf = feed_rows(middle, n2, vec, buf, h_ref, slope_ref, slice(None))
    gf_ref[...] = gf.astype(bf16)
    tf_ref[...] = tf.astype(bf16)
    y_ref[...] = y.astype(bf16)


def feed_forward(place, x, n1, o, vec, rest, waits=()):
    length, width = x.shape
    wide = 4 * width
    row, half = rows_of(width), struct((length, width), bf16)
    big, bigs = rows_of(wide), struct((length, wide), bf16)
    return call(
        feed_kernel,
        (length // ROWS,),
        [row, row, row, whole(16, width), ANY],
        [row, row, rows_of(128), row, row, big, big, row, row],
        [half, half, struct((length, 128), f32), half, half, bigs, bigs, half, half],
        [pltpu.VMEM((PARTS, REST, width), bf16), pltpu.SemaphoreType.DMA((1,))],
        flops=2 * length * width * (3 * width + 2 * wide),
        moved=24_000_000,
        waits=waits,
    )(place, x, n1, o, vec, rest)


def back_rows(e, hat, scale, ga, ta, slope_ref, gf, tf, gain, buf, du_ref, at_rows):
    df = (e * gf).astype(bf16)
    dzf = (e * tf).astype(bf16)
    dn2 = against(dzf, unit(buf, 2))
    for at in range(4):
        cut = slice(at * 512, at * 512 + 512)
        du = (against(df, down_part(buf, at)) * slope_ref[:, cut].astype(f32)).astype(bf16)
        du_ref[at_rows, cut] = du
        dn2 = dn2 + against(du, unit(buf, 3 + at))
    dm = e + norm_back(dn2, hat, scale, gain)
    da = (dm * ga).astype(bf16)
    dza = (dm * ta).astype(bf16)
    return dm, df, dzf, da, dza, against(da, unit(buf, 0)).astype(bf16)


def put_lanes(swap, keep, send, values, rows, first):
    for y in range(2):
        low, high = (values[(y * 2 + c) * rows : (y * 2 + c + 1) * rows] for c in range(2))
        keep[y, first : first + rows, :] = jnp.where(swap, high, low)
        send[y, first : first + rows, :] = jnp.where(swap, low, high)


def rest_grads(place, keep, send, o, n1, n2, h, da, dza, dzf, du_ref, df, sums):
    put = functools.partial(put_lanes, place[2] == 1, keep, send)
    put(cross(o, da).astype(bf16), UNIT, 0)
    put(cross(n1, dza).astype(bf16), UNIT, UNIT)
    put(cross(n2, dzf).astype(bf16), UNIT, 2 * UNIT)
    for at in range(4):
        put(cross(n2, du_ref[:, at * 512 : at * 512 + 512]).astype(bf16), UNIT, (3 + at) * UNIT)
    put(cross(h, df).astype(bf16), 4 * UNIT, 7 * UNIT)
    small = jnp.concatenate([sums, jnp.zeros((8, sums.shape[1]), f32)], axis=0).astype(bf16)
    for ref in (keep, send):
        for y in range(2):
            ref[y, REST:, :] = small


def keep_rows(at_rows, refs, values):
    for ref, value in zip(refs, values):
        ref[at_rows, :] = value


def add_sums(sums, dza, dzf):
    rows = [jnp.sum(part.astype(f32), axis=0, keepdims=True) for part in (dza, dzf)]
    new = jnp.concatenate(rows + [jnp.zeros((6, dza.shape[1]), f32)], axis=0)
    sums[...] = jnp.where(pl.program_id(0) == 0, new, sums[...] + new)


def turn_kernel(count, place, x_ref, n1_ref, o_ref, e_ref, vec_ref, o_cols, n1_cols, rest_ref,
                y_ref, dm_ref, dza_ref, do_ref, keep, send, buf, h, du, slope, n2, df, dzf, da, dza, sums, sems):
    step = pl.program_id(0)
    at_start([rest_copy(rest_ref, buf, sems.at[0], 0, REST, 0)])

    @pl.when(step < count)
    def _():
        at_rows = pl.ds(pl.multiple_of(step * ROWS, ROWS), ROWS)
        vec = vec_ref[...]
        middle, low, hat, scale, ga, ta = gated_rows(x_ref[...], n1_ref[...], o_ref[...], vec, buf)
        y, gf, tf = feed_rows(middle, low, vec, buf, h, slope, at_rows)
        y_ref[...] = y.astype(bf16)
        e = e_ref[...].astype(f32)
        dm, *parts, grad_o = back_rows(e, hat, scale, ga, ta, slope, gf, tf, vec[1:2, :], buf, du, at_rows)
        dm_ref[...] = dm
        do_ref[...] = grad_o
        keep_rows(at_rows, (n2, df, dzf, da, dza), (low, *parts))
        dza_ref[...] = parts[3]
        add_sums(sums, parts[3], parts[1])

    @pl.when(step >= count)
    def _():
        at = step - count
        narrow, wide = pl.ds(pl.multiple_of(at * 128, 128), 128), pl.ds(pl.multiple_of(at * 512, 512), 512)
        lefts = (o_cols[...], n1_cols[...], n2[:, narrow], h[:, wide])
        rest_grads(place, keep, send, *lefts, da[...], dza[...], dzf[...], du, df[...], sums[...])


def late_specs(length, width, count):
    row = pl.BlockSpec((ROWS, width), lambda i, place: (jnp.minimum(i, count - 1), 0))
    cols = pl.BlockSpec((length, width // 4), lambda i, place: (0, jnp.maximum(i - count, 0)))
    grad = pl.BlockSpec((2, REST + 16, width), lambda i, place: (jnp.maximum(i - count, 0), 0, 0))
    return row, cols, grad


def turn(place, x, n1, o, e, vec, rest, waits=()):
    length, width = x.shape
    wide, count = 4 * width, length // ROWS
    row, cols, grad = late_specs(length, width, count)
    half, tall = struct((length, width), bf16), pltpu.VMEM((length, width), bf16)
    return call(
        functools.partial(turn_kernel, count),
        (count + 4,),
        [row] * 4 + [whole(16, width), cols, cols, ANY],
        [row] * 4 + [grad] * 2,
        [half, struct((length, width), f32), half, half] + [struct((PARTS // 2, REST + 16, width), bf16)] * 2,
        [pltpu.VMEM((PARTS, REST, width), bf16)]
        + [pltpu.VMEM((length, wide), bf16)] * 2
        + [pltpu.VMEM((ROWS, wide), bf16)]
        + [tall] * 5
        + [pltpu.VMEM((8, width), f32), pltpu.SemaphoreType.DMA((1,))],
        flops=6 * length * width * (3 * width + 2 * wide),
        moved=24_000_000,
        waits=waits,
    )(place, x, n1, o, e, vec, o, n1, rest)


def dx_rows(x, dm, dqkv, dza, gain, buf, gate):
    width = x.shape[1]
    dn = against(dza, gate[...].reshape(PARTS * UNIT, width))
    for at, part in enumerate(dqkv):
        dn = dn + against(part, unit(buf, at))
    hat, scale = normalise(x.astype(f32))
    return dm + norm_back(dn, hat, scale, gain)


def joint_kernel(count, many, place, x_ref, dm1_ref, dq_ref, dk_ref, dv_ref, dza1_ref, e_ref,
                 n2_ref, scale_ref, ga_ref, ta_ref, slope_ref, gf_ref, tf_ref, vec1_ref, vec_ref,
                 o_cols, n1_cols, n2_cols, h_cols, rest1_ref, rest_ref, *refs):
    dx_ref, low_ref, dm_ref, dza_ref, do_ref, keep, send, head, gate, buf, du, df, dzf, da, dza, sums, sems = refs[many:]
    step = pl.program_id(0)
    copies = fetches(place, refs[:many], head, sems, ((0, 3 * UNIT),))[0]
    copies.append(rest_copy(rest1_ref, gate, sems.at[1], UNIT, 2 * UNIT, UNIT))
    copies.append(rest_copy(rest_ref, buf, sems.at[2], 0, REST, 0))
    at_start(copies)

    @pl.when(step < count)
    def _():
        at_rows = pl.ds(pl.multiple_of(step * ROWS, ROWS), ROWS)
        dqkv = (dq_ref[...], dk_ref[...], dv_ref[...])
        dx = dx_rows(x_ref[...], dm1_ref[...], dqkv, dza1_ref[...], vec1_ref[0:1, :], head, gate)
        dx_ref[...] = dx
        low = dx.astype(bf16)
        low_ref[...] = low
        e = e_ref[...].astype(f32) + low.astype(f32)
        gain = vec_ref[1:2, :]
        hat = n2_ref[...].astype(f32) * (1.0 / gain)
        ga, ta, gf, tf = (ref[...].astype(f32) for ref in (ga_ref, ta_ref, gf_ref, tf_ref))
        dm, *parts, grad_o = back_rows(e, hat, scale_ref[:, 0:1], ga, ta, slope_ref, gf, tf, gain, buf, du, at_rows)
        dm_ref[...] = dm
        do_ref[...] = grad_o
        keep_rows(at_rows, (df, dzf, da, dza), parts)
        dza_ref[...] = parts[3]
        add_sums(sums, parts[3], parts[1])

    @pl.when(step >= count)
    def _():
        lefts = (o_cols[...], n1_cols[...], n2_cols[...], h_cols[...])
        rest_grads(place, keep, send, *lefts, da[...], dza[...], dzf[...], du, df[...], sums[...])


def joint_back(place, x, dm1, dqkv, dza1, vec1, head, rest1, e, kept, rest, waits=()):
    n1, o, vec, n2, scale, ga, ta, h, slope, gf, tf = kept
    length, width = x.shape
    wide, count = 4 * width, length // ROWS
    row, cols, grad = late_specs(length, width, count)
    lanes = pl.BlockSpec((ROWS, 128), lambda i, place: (jnp.minimum(i, count - 1), 0))
    big = pl.BlockSpec((ROWS, wide), lambda i, place: (jnp.minimum(i, count - 1), 0))
    wides = pl.BlockSpec((length, wide // 4), lambda i, place: (0, jnp.maximum(i - count, 0)))
    half, tall = struct((length, width), bf16), pltpu.VMEM((length, width), bf16)
    floats = struct((length, width), f32)
    return call(
        functools.partial(joint_kernel, count, len(head)),
        (count + 4,),
        [row] * 8 + [lanes, row, row, big, row, row, whole(16, width), whole(16, width), cols, cols, cols, wides, ANY, ANY]
        + [ANY] * len(head),
        [row] * 5 + [grad] * 2,
        [floats, half, floats, half, half] + [struct((PARTS // 2, REST + 16, width), bf16)] * 2,
        [pltpu.VMEM((PARTS, 3 * UNIT, width), bf16), pltpu.VMEM((PARTS, UNIT, width), bf16), pltpu.VMEM((PARTS, REST, width), bf16)]
        + [pltpu.VMEM((length, wide), bf16)]
        + [tall] * 4
        + [pltpu.VMEM((8, width), f32), pltpu.SemaphoreType.DMA((3,))],
        flops=4 * length * width * (5 * width + 2 * wide),
        moved=40_000_000,
        waits=waits,
    )(place, x, dm1, *dqkv, dza1, e, n2, scale, ga, ta, slope, gf, tf, vec1, vec, o, n1, n2, h, rest1, rest, *head)


def split3(value):
    first = value.astype(bf16)
    rest = value - first.astype(f32)
    second = rest.astype(bf16)
    third = (rest - second.astype(f32)).astype(bf16)
    return first, second, third


def attend_back_kernel(block, place, q_ref, k_ref, v_ref, o_ref, s_ref, do_ref, dq_ref, dk_ref, dv_ref,
                       q_s, k_s, v_s, do_s, acc):
    length = q_ref.shape[0]
    lane = lax.broadcasted_iota(jnp.int32, (length, 128), 1)
    row = lax.broadcasted_iota(jnp.int32, (block, block), 0)
    col = lax.broadcasted_iota(jnp.int32, (block, block), 1)
    q, k, v, do = q_ref[...], k_ref[...], v_ref[...], do_ref[...]
    zero = jnp.zeros_like(q)
    product = do.astype(f32) * o_ref[...].astype(f32)
    for head in range(2):
        low = head * HD
        other = (1 - head) * HD
        mine = (lane >= low) & (lane < low + HD)
        logs = -s_ref[:, low : low + 1]
        delta = -jnp.sum(jnp.where(mine, product, 0.0), axis=1, keepdims=True)
        one = jnp.where((lane >= other) & (lane < other + 3), jnp.ones_like(q), zero)
        q_aug, do_aug = jnp.where(mine, q, zero), jnp.where(mine, do, zero)
        for at, (part, piece) in enumerate(zip(split3(logs), split3(delta))):
            here = lane == other + at
            q_aug = jnp.where(here, part, q_aug)
            do_aug = jnp.where(here, piece, do_aug)
        q_s[head] = q_aug
        do_s[head] = do_aug
        k_s[head] = jnp.where(mine, k, one)
        v_s[head] = jnp.where(mine, v, one)
    for index in range(length // block):
        start, stop = index * block, (index + 1) * block
        kgrads, vgrads = [], []
        for head in range(2):
            kb, vb = k_s[head, start:stop, :], v_s[head, start:stop, :]
            scores = against(kb, q_s[head, start:, :])
            first = jnp.where(row <= col, scores[:, :block], -1e30)
            scores = jnp.concatenate([first, scores[:, block:]], axis=1) if stop < length else first
            probs = jnp.exp(scores)
            grads = (probs * against(vb, do_s[head, start:, :])).astype(bf16)
            vgrads.append(dense(probs.astype(bf16), do_ref[start:, :]))
            kgrads.append(dense(grads, q_ref[start:, :]))
            part = cross(grads, kb)
            if index == 0:
                acc[head] = part
            else:
                acc[head, start:, :] += part
        half = lane[:block] < HD
        dk_ref[start:stop, :] = jnp.where(half, kgrads[0], kgrads[1]).astype(bf16)
        dv_ref[start:stop, :] = jnp.where(half, vgrads[0], vgrads[1]).astype(bf16)
    dq_ref[...] = (jnp.where(lane < HD, acc[0], acc[1]) * 0.125).astype(bf16)


def attend_back(place, q, k, v, o, s, do, start, count=2, onto=(), waits=(), block=256):
    length, width = q.shape
    pair = pl.BlockSpec((length, 128), lambda i, place: (0, i + start))
    return call(
        functools.partial(attend_back_kernel, block),
        (count,),
        [pair] * 6,
        [pair] * 3,
        [struct((length, width), bf16)] * 3,
        [pltpu.VMEM((2, length, 128), bf16)] * 4 + [pltpu.VMEM((2, length, 128), f32)],
        flops=5_000_000_000 * count,
        moved=5_000_000,
        onto=onto,
        waits=waits,
    )(place, q, k, v, o, s, do)


def qkv_back_kernel(many, place, x_ref, dm_ref, dq_ref, dk_ref, dv_ref, dza_ref, vec_ref, rest_ref, *refs):
    dx_ref, low_ref, buf, gate, sems = refs[many:]
    copies = fetches(place, refs[:many], buf, sems, ((0, 3 * UNIT),))[0]
    at_start(copies + [rest_copy(rest_ref, gate, sems.at[1], UNIT, 2 * UNIT, UNIT)])
    dqkv = (dq_ref[...], dk_ref[...], dv_ref[...])
    dx = dx_rows(x_ref[...], dm_ref[...], dqkv, dza_ref[...], vec_ref[0:1, :], buf, gate)
    dx_ref[...] = dx
    low_ref[...] = dx.astype(bf16)


def qkv_back(place, x, dm, dq, dk, dv, dza, vec, weights, rest, waits=()):
    length, width = x.shape
    row = rows_of(width)
    return call(
        functools.partial(qkv_back_kernel, len(weights)),
        (length // ROWS,),
        [row] * 6 + [whole(16, width), ANY] + [ANY] * len(weights),
        [row, row],
        [struct((length, width), f32), struct((length, width), bf16)],
        [pltpu.VMEM((PARTS, 3 * UNIT, width), bf16), pltpu.VMEM((PARTS, UNIT, width), bf16), pltpu.SemaphoreType.DMA((2,))],
        flops=2 * length * width * 4 * width,
        moved=12_000_000,
        waits=waits,
    )(place, x, dm, dq, dk, dv, dza, vec, rest, *weights)


def put(place, outs, values, rows, first):
    keep, send = outs
    for y in range(2):
        low, high = (values[(y * 2 + c) * rows : (y * 2 + c + 1) * rows] for c in range(2))
        at = place[1] ^ y
        swap = place[2] == 1
        keep[at, 0, first : first + rows, :] = jnp.where(swap, high, low)
        send[at, 0, first : first + rows, :] = jnp.where(swap, low, high)


def grad_outs(rows, width):
    out = pl.BlockSpec((2, 1, rows, width), lambda i, place: (0, (i - place[0]) & 3, 0, 0))
    return [out, out], [struct((2, 4, rows, width), bf16)] * 2


def first_grad_kernel(place, *refs):
    outs = refs[-2:]
    for layer in range(len(refs) // 4):
        n1_ref = refs[4 * layer]
        for at, ref in enumerate(refs[4 * layer + 1 : 4 * layer + 4]):
            put(place, outs, cross(n1_ref[...], ref[...]).astype(bf16), UNIT, (3 * layer + at) * UNIT)


def first_grad(place, *layers, waits=()):
    length, width = layers[0][0].shape
    cols = pl.BlockSpec((length, width // 4), lambda i, place: (0, i))
    specs, shapes = grad_outs(3 * UNIT * len(layers), width)
    return call(
        first_grad_kernel,
        (4,),
        ([cols] + [whole(length, width)] * 3) * len(layers),
        specs,
        shapes,
        flops=2 * length * width * 3 * width * len(layers),
        moved=9_000_000 * len(layers),
        waits=waits,
    )(place, *(value for layer in layers for value in layer))


def moved_z(value, steps):
    count = lax.axis_size("dp")
    return lax.ppermute(value, "dp", [(d, (d + 4 * steps) % count) for d in range(count)])


def swapped(value, bit):
    return lax.ppermute(value, "dp", [(d, d ^ bit) for d in range(lax.axis_size("dp"))])


def crossed(value, sources=(0, 1)):
    return lax.ppermute(value, "section", [(s, 1 - s) for s in sources])


def along_z(block):
    return [block] + [moved_z(block, k) for k in (1, 2, 3)]


def across(own):
    beside = swapped(own, 2)
    return own, beside, swapped(own, 1), swapped(beside, 1)


def spread_whole(blocks):
    blocks = blocks.reshape(4, 2, 2, *blocks.shape[1:])
    blocks = jnp.stack([blocks[0], blocks[3], blocks[2], blocks[1]])
    return tuple(blocks[:, index & 1, index >> 1] for index in range(4))


def gather_whole(values, axis):
    values = lax.all_gather(values.astype(bf16), "dp", axis=axis, tiled=True)
    return lax.all_gather(values, "section", axis=0, tiled=True)


def split_rows(matrix, cols):
    rows, width = matrix.shape[0] // PARTS, matrix.shape[1] // cols
    return matrix.reshape(PARTS, rows, cols, width).transpose(0, 2, 1, 3).reshape(PARTS, cols * rows, width)


def merge_rows(blocks, cols):
    rows, width = blocks.shape[1] // cols, blocks.shape[2]
    return blocks.reshape(PARTS, cols, rows, width).transpose(0, 2, 1, 3).reshape(PARTS * rows, cols * width)


def weights_whole(w_qkv, w_out, w_gates, w_up, w_down, gains, biases):
    w_qkv, w_out, w_up, w_down = (gather_whole(w, 1) for w in (w_qkv, w_out, w_up, w_down))
    w_gates, gains, biases = (gather_whole(w, 2) for w in (w_gates, gains, biases))
    heads, tails = [], []
    for layer in range(2):
        lines = jnp.concatenate([gains[layer], biases[layer], jnp.zeros((12, gains.shape[2]), bf16)], axis=0)
        lines = jnp.concatenate([lines[None], jnp.zeros((PARTS - 1, *lines.shape), bf16)], axis=0)
        heads.append(spread_whole(jnp.concatenate([split_rows(w_qkv[layer], 3), lines], axis=1)))
        parts = [w_out[layer], w_gates[layer, 0], w_gates[layer, 1]]
        parts = [split_rows(part, 1) for part in parts] + [split_rows(w_up[layer], 4), split_rows(w_down[layer], 1)]
        tails.append(jnp.concatenate(parts, axis=1))
    return heads, tails


def joined(pieces):
    return jnp.stack(pieces).transpose(2, 1, 0, 3, 4).reshape(PARTS, *pieces[0].shape[2:])


def collect_whole(early, rest):
    early, rest = joined(early), jnp.stack(rest, axis=1).reshape(PARTS, *rest[0].shape[1:])
    parts = [merge_rows(early, 3), merge_rows(rest[:, :UNIT], 1)]
    parts += [jnp.stack([merge_rows(rest[:, at * UNIT : (at + 1) * UNIT], 1) for at in (1, 2)])]
    parts += [merge_rows(rest[:, 3 * UNIT : 7 * UNIT], 4), merge_rows(rest[:, 7 * UNIT : REST], 1), rest[0, REST : REST + 2]]
    axes = (0, 0, 1, 0, 0, 1)
    parts = [lax.psum_scatter(part.astype(f32), "dp", scatter_dimension=axis, tiled=True) for part, axis in zip(parts, axes)]
    return [lax.psum(part, "section") for part in parts]


def fold_core(keep, got):
    away = (keep[1].astype(f32) + got[1].astype(f32)).astype(bf16)
    return away, keep[0].astype(f32) + got[0].astype(f32)


def scattered(keep, got):
    lanes = [[d for d in range(PARTS) if d % 2 == c] for c in range(2)]
    both = (keep.astype(f32) + got.astype(f32)).astype(bf16)
    return lax.psum_scatter(both, "dp", scatter_dimension=0, axis_index_groups=lanes)


def fold_y(near, got):
    near = near + got.astype(f32)
    return near[0], [near[k].astype(bf16) for k in (1, 2, 3)]


def fold_z(total, gots):
    for got in gots:
        total = total + got.astype(f32)
    return total


def pack_kernel(place, qkv_ref, out_ref, gates_ref, up_ref, down_ref, lines_ref, head_ref, tail_ref):
    width = out_ref.shape[2]
    for at in range(3):
        head_ref[at * UNIT : (at + 1) * UNIT, :] = qkv_ref[0, :, at * width : (at + 1) * width].astype(bf16)
    head_ref[3 * UNIT :, :] = lines_ref[...].astype(bf16)
    tail_ref[:UNIT, :] = out_ref[0].astype(bf16)
    for at in range(2):
        tail_ref[(1 + at) * UNIT : (2 + at) * UNIT, :] = gates_ref[0, at].astype(bf16)
    for at in range(4):
        tail_ref[(3 + at) * UNIT : (4 + at) * UNIT, :] = up_ref[0, :, at * width : (at + 1) * width].astype(bf16)
    tail_ref[7 * UNIT :, :] = down_ref[0].astype(bf16)


def pack(place, index, w_qkv, w_out, w_gates, w_up, w_down, gains, biases):
    width = w_out.shape[2]
    lines = jnp.concatenate([gains[0], biases[0]], axis=0)
    mine = jnp.arange(width)[None, :] // UNIT == index
    lines = jnp.concatenate([jnp.where(mine, jnp.tile(lines, (1, PARTS)), 0.0), jnp.zeros((12, width), f32)], axis=0)
    arrays = (w_qkv, w_out, w_gates, w_up, w_down, lines)
    return call(
        pack_kernel,
        (1,),
        [whole(*array.shape) for array in arrays],
        [whole(FIRST, width), whole(REST, width)],
        [struct((FIRST, width), bf16), struct((REST, width), bf16)],
        moved=3_000_000,
    )(place, *arrays)


def after(value, *others):
    return lax.optimization_barrier((value, *others))[0]


def gain_grads(grads, w_qkv, w_gates, w_up, gains):
    d_qkv, _, d_gates, d_up = grads[:4]
    w_qkv, w_gates, w_up, gains = (w[0].astype(bf16).astype(f32) for w in (w_qkv, w_gates, w_up, gains))
    first = jnp.sum(w_qkv * d_qkv, axis=1) + jnp.sum(w_gates[0] * d_gates[0], axis=1)
    second = jnp.sum(w_up * d_up, axis=1) + jnp.sum(w_gates[1] * d_gates[1], axis=1)
    return jnp.stack([first, second]) / gains


def finish_kernel(place, own0, got0, own1, got1, own2, got2, own3, got3, w_qkv, w_gates, w_up, gains,
                  g_qkv, g_out, g_gates, g_up, g_down, g_gains, g_biases):
    width = own0.shape[1]
    first = place[3] == 0

    def total(start, stop):
        early = own0[start:stop, :] + got0[start:stop, :].astype(f32), own1[start:stop, :] + got1[start:stop, :].astype(f32)
        return jnp.where(first, *early)

    def rest(start, stop):
        return jnp.where(
            first,
            own2[start:stop, :].astype(f32) + got2[start:stop, :].astype(f32),
            own3[start:stop, :].astype(f32) + got3[start:stop, :].astype(f32),
        )

    def against_weight(weight, grad):
        return jnp.sum(weight.astype(bf16).astype(f32) * grad, axis=1, keepdims=True)

    rows = lax.broadcasted_iota(jnp.int32, (UNIT, UNIT), 0)
    diagonal = rows == lax.broadcasted_iota(jnp.int32, (UNIT, UNIT), 1)
    lines = [None, None]
    for at in range(2):
        part = rest((1 + at) * UNIT, (2 + at) * UNIT)
        g_gates[0, at] = part
        lines[at] = against_weight(w_gates[0, at], part)
    for at in range(3):
        cut = slice(at * width, at * width + width)
        part = total(at * UNIT, (at + 1) * UNIT)
        g_qkv[0, :, cut] = part
        lines[0] += against_weight(w_qkv[0, :, cut], part)
    for at in range(4):
        cut = slice(at * width, at * width + width)
        part = rest((3 + at) * UNIT, (4 + at) * UNIT)
        g_up[0, :, cut] = part
        lines[1] += against_weight(w_up[0, :, cut], part)
    g_out[0] = rest(0, UNIT)
    g_down[0] = rest(7 * UNIT, REST)
    sums = rest(REST, REST + 16)
    index = (place[0] * 2 + place[1]) * 2 + place[2]
    for at in range(2):
        line = jnp.sum(jnp.where(diagonal, lines[at], 0.0), axis=0, keepdims=True)
        g_gains[0, at : at + 1, :] = line / gains[0, at : at + 1, :].astype(bf16).astype(f32)
        mine = jnp.zeros((1, UNIT), f32)
        for part in range(PARTS):
            mine = jnp.where(index == part, sums[at : at + 1, part * UNIT : (part + 1) * UNIT], mine)
        g_biases[0, at : at + 1, :] = mine


def finish(place, sums, masters):
    w_qkv, w_out, w_gates, w_up, w_down, gains, biases = masters
    inputs = (*sums, w_qkv, w_gates, w_up, gains)
    shapes = [struct(master.shape, f32) for master in (w_qkv, w_out, w_gates, w_up, w_down, gains, biases)]
    return call(
        finish_kernel,
        (1,),
        [whole(*value.shape) for value in inputs],
        [whole(*shape.shape) for shape in shapes],
        shapes,
        moved=6_000_000,
    )(place, *inputs)


def per_device(tokens, cotangent, w_qkv, w_out, w_gates, w_up, w_down, norm_gains, gate_biases):
    section = lax.axis_index("section")
    index = lax.axis_index("dp")
    fast = lax.axis_size("dp") == PARTS
    first = section == 0
    masters = (w_qkv, w_out, w_gates, w_up, w_down, norm_gains, gate_biases)

    def pick(own, other):
        return jnp.where(first, own, other), jnp.where(first, other, own)

    x = jnp.where(first, tokens[0, 0], tokens[1, 0])
    seeds = [cotangent[0, m, 0] for m in range(2)]
    own_seed, other_seed = jnp.where(first, seeds[0], seeds[1]), jnp.where(first, seeds[1], seeds[0])
    if fast:
        y0, y1, theirs, dxs, lows, grads = run(x, own_seed, other_seed, masters, index, section, pick)
    else:
        place = jnp.zeros((3,), jnp.int32)
        heads, rest = weights_whole(*masters)
        n0, q0, k0, v0, vec0 = qkv_forward(place, x, heads[0])
        o0, s0 = attend_forward(place, q0, k0, v0, 2, onto=attend_forward(place, q0, k0, v0, 0))
        y0, *kept = feed_forward(place, x, n0, o0, vec0, rest[0])
        n1, q1, k1, v1, vec1 = qkv_forward(place, y0, heads[1])
        o1, s1 = attend_forward(place, q1, k1, v1, 2, onto=attend_forward(place, q1, k1, v1, 0))
        seeds = pick(own_seed, crossed(other_seed))
        y1, dm, dza, do, *later1 = turn(place, y0, n1, o1, seeds[1], vec1, rest[1])
        dqkv = attend_back(place, q1, k1, v1, o1, s1, do, 2, onto=attend_back(place, q1, k1, v1, o1, s1, do, 0))
        early1 = first_grad(place, (n1, *dqkv))
        dx1, low1, dm, dza, do, *later0 = joint_back(
            place, y0, dm, dqkv, dza, vec1, heads[1], rest[1], seeds[0], (n0, o0, vec0, *kept), rest[0]
        )
        dqkv = attend_back(place, q0, k0, v0, o0, s0, do, 2, onto=attend_back(place, q0, k0, v0, o0, s0, do, 0))
        early0 = first_grad(place, (n0, *dqkv))
        dx0, low0 = qkv_back(place, x, dm, *dqkv, dza, vec0, heads[0], rest[0])
        grads0, grads1 = collect_whole(early0, later0), collect_whole(early1, later1)
        dxs, lows = (dx0, dx1), (crossed(low0, (1,)), crossed(low1, (0,)))
        theirs = crossed(jnp.where(first, y1, y0))
        grads = [jnp.where(first, *pair) for pair in zip(grads0, grads1)]
        grads.insert(5, gain_grads(grads, w_qkv, w_gates, w_up, norm_gains))
        grads = [grad[None] for grad in grads]

    mine = jnp.where(first, y0, y1)
    block = jnp.stack([jnp.where(first, mine, theirs), jnp.where(first, theirs, mine)])[None, :, None]
    in_grads = jnp.stack([jnp.where(first, dxs[0], lows[1].astype(f32)), dxs[1]])
    last = jnp.where(first, lows[0].astype(f32), dxs[1])
    in_grads = lax.dynamic_update_slice(in_grads, last[None], (1, 0, 0))[None, :, None]
    return (block, in_grads, *grads)


def run(x, own_seed, other_seed, masters, index, section, pick):
    first = section == 0
    width = x.shape[1]
    place = jnp.stack([index // 4, (index // 2) & 1, index & 1, section]).astype(jnp.int32)
    head, tail = pack(place, index, *masters)
    heads = pick(head, crossed(head))
    tails = pick(tail, crossed(tail))
    tail0 = lax.all_gather(tails[0], "dp", axis=0)

    def cores(z, y):
        return z, y, swapped(z, 1), swapped(y, 1)

    zh0 = jnp.stack(along_z(heads[0]))
    yh0 = swapped(zh0, 2)
    zh1 = along_z(after(heads[1], yh0))
    head0 = cores(zh0, yh0)
    n1, q, k, v, vec = qkv_forward(place, x, head0)
    o, s = attend_forward(place, q, k, v, 0)
    zh1 = jnp.stack([after(part, o) for part in zh1])
    yh1 = swapped(zh1, 2)
    o, s = attend_forward(place, q, k, v, 2, onto=(o, s), waits=(zh1,))
    tail0 = after(tail0, o)
    tail1 = lax.all_gather(after(tails[1], tail0), "dp", axis=0)
    other_seed = crossed(after(other_seed, o))
    y0, *held = feed_forward(place, x, n1, o, vec, tail0)
    head1 = cores(after(zh1, y0), after(yh1, y0))
    kept0 = (n1, o, vec, *held)
    layer0 = (q, k, v, o, s)

    n1, q, k, v, vec = qkv_forward(place, y0, head1)
    o, s = attend_forward(place, q, k, v, 0)
    o, s = attend_forward(place, q, k, v, 2, onto=(o, s))
    seeds = pick(own_seed, after(other_seed, o))
    y1, dm, dza, do, keep, send = turn(place, y0, n1, o, seeds[1], vec, tail1)
    got = swapped(send, 1)
    theirs = crossed(jnp.where(first, y1, y0))
    dqkv = attend_back(place, q, k, v, o, s, do, 0, 1)
    rest1 = scattered(keep, after(got, dqkv[0]))
    dqkv = attend_back(place, q, k, v, o, s, do, 1, 3, onto=dqkv)
    keep_b, send_b = first_grad(place, (n1, *dqkv))
    got_b = swapped(send_b, 1)
    dx1, low1, dm, dza, do, keep, send = joint_back(
        place, y0, dm, dqkv, dza, vec, head1, tail1, seeds[0], kept0, tail0, waits=(keep_b, theirs)
    )
    n1, o, vec = kept0[:3]
    q, k, v, o, s = layer0
    got = swapped(send, 1)
    away, near = fold_core(keep_b, after(got_b, low1))
    got_b = swapped(away, 2)
    other1 = crossed(low1, (0,))
    dqkv = attend_back(place, q, k, v, o, s, do, 0, 1, waits=(away,))
    rest0 = scattered(keep, after(got, dqkv[0]))
    dqkv = attend_back(place, q, k, v, o, s, do, 1, 3, onto=dqkv)
    own, sends = fold_y(near, after(got_b, dqkv[0]))
    gots = [moved_z(part, at + 1) for at, part in enumerate(sends)]
    keep, send = first_grad(place, (n1, *dqkv), waits=(other1, *sends))
    got = swapped(send, 1)
    away, near = fold_core(keep, got)
    got = swapped(away, 2)
    dx0, low0 = qkv_back(place, x, dm, *dqkv, dza, vec, head0, tail0, waits=(away,))
    early1 = fold_z(own, [after(part, low0) for part in gots])
    rest1 = after(rest1, low0)
    last1 = crossed(jnp.concatenate([rest1, early1.astype(bf16)]), (0,))
    other0 = crossed(low0, (1,))
    own, sends = fold_y(near, after(got, low0))
    gots = [moved_z(part, at + 1) for at, part in enumerate(sends)]
    early0 = fold_z(own, gots)
    last0 = crossed(early0.astype(bf16), (1,))
    rest0 = after(rest0, last0, last1, other0)
    later0 = crossed(rest0, (1,))
    sums = (early0, last0, early1, last1[REST + 16 :], rest0, later0, rest1, last1[: REST + 16])
    grads = finish(place, sums, masters)
    return y0, y1, theirs, (dx0, dx1), (other0, other1), grads


def solution(mesh):
    placed = (
        P(None, "dp", None, None),
        P("section", None, "dp", None, None),
        P("section", "dp", None),
        P("section", "dp", None),
        P("section", None, "dp", None),
        P("section", "dp", None),
        P("section", "dp", None),
        P("section", None, "dp"),
        P("section", None, "dp"),
    )
    return jax.shard_map(
        per_device,
        mesh=mesh,
        in_specs=placed,
        out_specs=(P("section", None, "dp", None, None), P("section", None, "dp", None, None)) + placed[2:],
        check_vma=False,
    )
```

```python
import functools

import jax
import jax.numpy as jnp
from jax import lax
from jax.experimental import pallas as pl
from jax.experimental.pallas import tpu as pltpu
from jax.sharding import PartitionSpec as P

HD = 64
ROWS = 512
bf16 = jnp.bfloat16
f32 = jnp.float32
root_term = 0.7978845608
cube_term = 0.044715
VMEM = 56 * 1024 * 1024
PARTS = 16
UNIT = 32
FIRST = 3 * UNIT + 16
REST = 11 * UNIT


def dense(left, right):
    return jnp.dot(left, right, preferred_element_type=f32)


def cross(left, right):
    return lax.dot_general(left, right, (((0,), (0,)), ((), ())), preferred_element_type=f32)


def against(left, right):
    return lax.dot_general(left, right, (((1,), (1,)), ((), ())), preferred_element_type=f32)


def normalise(values):
    centred = values - jnp.mean(values, axis=-1, keepdims=True)
    spread = jnp.mean(centred * centred, axis=-1, keepdims=True)
    scale = lax.rsqrt(spread + 1e-05)
    return centred * scale, scale


def norm_back(grad, hat, scale, gain):
    spread = grad * gain
    first = jnp.mean(spread, axis=-1, keepdims=True)
    second = jnp.mean(spread * hat, axis=-1, keepdims=True)
    return scale * (spread - first - hat * second)


ANY = pl.BlockSpec(memory_space=pl.ANY)


def struct(shape, dtype):
    return jax.ShapeDtypeStruct(shape, dtype)


def rows_of(width):
    return pl.BlockSpec((ROWS, width), lambda i, place: (i, 0))


def whole(*shape):
    return pl.BlockSpec(shape, lambda i, place: (0,) * len(shape))


def call(kernel, grid, in_specs, out_specs, out_shape, scratch=(), flops=0, moved=0, waits=(), onto=()):
    extra = len(onto) + len(waits)
    count = len(in_specs)

    def run(*args):
        def body(*refs):
            kernel(*refs[: 1 + count], *refs[1 + count + extra :])

        return pl.pallas_call(
            body,
            grid_spec=pltpu.PrefetchScalarGridSpec(
                num_scalar_prefetch=1, grid=grid, in_specs=in_specs + [ANY] * extra, out_specs=out_specs, scratch_shapes=list(scratch)
            ),
            out_shape=out_shape,
            input_output_aliases={1 + count + at: at for at in range(len(onto))},
            compiler_params=pltpu.CompilerParams(dimension_semantics=("arbitrary",), vmem_limit_bytes=VMEM),
            cost_estimate=pl.CostEstimate(flops=flops, bytes_accessed=moved, transcendentals=0),
        )(*args, *onto, *waits)

    return run


def fetches(place, sources, target, sems, cuts, base=0):
    copies = []
    for number, (start, stop) in enumerate(cuts):
        group = []
        for index, source in enumerate(sources):
            for slot in range(4):
                part = ((place[0] - slot) & 3) * 4 + (place[1] ^ (index & 1)) * 2 + (place[2] ^ (index >> 1))
                group.append(
                    pltpu.make_async_copy(
                        source.at[slot, pl.ds(start, stop - start)],
                        target.at[part, pl.ds(start - base, stop - start)],
                        sems.at[number],
                    )
                )
        copies.append(group)
    return copies


def unit(ref, at):
    return ref[:, at * UNIT : (at + 1) * UNIT, :].reshape(PARTS * UNIT, ref.shape[2])


def down_part(ref, at, start=7):
    return ref[at * 4 : at * 4 + 4, start * UNIT : (start + 4) * UNIT, :].reshape(16 * UNIT, ref.shape[2])


def rest_copy(source, target, sem, start, stop, base):
    cut, goal = pl.ds(start, stop - start), pl.ds(start - base, stop - start)
    return pltpu.make_async_copy(source.at[:, cut], target.at[:, goal], sem)


def at_start(copies):
    @pl.when(pl.program_id(0) == 0)
    def _():
        for copy in copies:
            copy.start()
        for copy in copies:
            copy.wait()


def qkv_kernel(many, place, x_ref, *refs):
    n_ref, q_ref, k_ref, v_ref, vec_ref, buf, sems = refs[many:]
    copies = fetches(place, refs[:many], buf, sems, ((0, FIRST),))[0]

    @pl.when(pl.program_id(0) == 0)
    def _():
        for copy in copies:
            copy.start()
        for copy in copies:
            copy.wait()
        vec_ref[...] = jnp.sum(buf[:, 3 * UNIT : 3 * UNIT + 16, :].astype(f32), axis=0)

    hat, _ = normalise(x_ref[...].astype(f32))
    n1 = (hat * vec_ref[0:1, :]).astype(bf16)
    n_ref[...] = n1
    q_ref[...] = (dense(n1, unit(buf, 0)).astype(bf16) * 0.125).astype(bf16)
    k_ref[...] = dense(n1, unit(buf, 1)).astype(bf16)
    v_ref[...] = dense(n1, unit(buf, 2)).astype(bf16)


def qkv_forward(place, x, weights, waits=()):
    length, width = x.shape
    row = rows_of(width)
    return call(
        functools.partial(qkv_kernel, len(weights)),
        (length // ROWS,),
        [row] + [ANY] * len(weights),
        [row] * 4 + [whole(16, width)],
        [struct((length, width), bf16)] * 4 + [struct((16, width), f32)],
        [pltpu.VMEM((PARTS, FIRST, width), bf16), pltpu.SemaphoreType.DMA((1,))],
        flops=2 * length * width * 3 * width,
        moved=8_000_000,
        waits=waits,
    )(place, x, *weights)


def attend_kernel(block, place, q_ref, k_ref, v_ref, o_ref, s_ref):
    length = q_ref.shape[0]
    lane = lax.broadcasted_iota(jnp.int32, (block, 128), 1)
    row = lax.broadcasted_iota(jnp.int32, (block, block), 0)
    col = lax.broadcasted_iota(jnp.int32, (block, block), 1)
    for index in range(length // block):
        start, stop = index * block, (index + 1) * block
        q = q_ref[start:stop, :]
        outs, logs = [], []
        for head in range(2):
            mine = (lane >= head * HD) & (lane < (head + 1) * HD)
            own = jnp.where(mine, q, jnp.zeros_like(q))
            scores = against(own, k_ref[:stop, :])
            last = jnp.where(row >= col, scores[:, start:], -1e30)
            scores = jnp.concatenate([scores[:, :start], last], axis=1) if start else last
            highest = jnp.max(scores, axis=1, keepdims=True)
            weights = jnp.exp(scores - highest)
            total = jnp.sum(weights, axis=1, keepdims=True)
            outs.append(dense(weights.astype(bf16), v_ref[:stop, :]) * (1.0 / total))
            logs.append(highest + jnp.log(total))
        o_ref[start:stop, :] = jnp.where(lane < HD, outs[0], outs[1]).astype(bf16)
        s_ref[start:stop, :] = jnp.where(lane < HD, logs[0], logs[1])


def attend_forward(place, q, k, v, start, onto=(), waits=(), block=256):
    length, width = q.shape
    pair = pl.BlockSpec((length, 128), lambda i, place: (0, i + start))
    return call(
        functools.partial(attend_kernel, block),
        (width // 256,),
        [pair] * 3,
        [pair, pair],
        [struct((length, width), bf16), struct((length, width), f32)],
        flops=6_000_000_000,
        moved=3_000_000,
        onto=onto,
        waits=waits,
    )(place, q, k, v)


def gelu(u):
    square = u * u
    inner = jnp.tanh(u * (root_term + (root_term * cube_term) * square))
    half = 0.5 + 0.5 * inner
    slope = half + (0.5 * root_term) * u * (1.0 - inner * inner) * (1.0 + (3.0 * cube_term) * square)
    return u * half, slope


def gated_rows(x, n1, o, vec, buf):
    branch = dense(o, unit(buf, 0))
    opening = jax.nn.sigmoid(dense(n1, unit(buf, 1)) + vec[2:3, :])
    gated = opening * branch
    middle = x.astype(f32) + gated
    hat, scale = normalise(middle)
    n2 = (hat * vec[1:2, :]).astype(bf16)
    return middle, n2, hat, scale, opening, gated * (1.0 - opening)


def feed_rows(middle, n2, vec, buf, h_ref, slope_ref, at_rows):
    feed = None
    for at in range(4):
        cut = slice(at * 512, at * 512 + 512)
        active, slope = gelu(dense(n2, unit(buf, 3 + at)))
        active = active.astype(bf16)
        h_ref[at_rows, cut] = active
        slope_ref[:, cut] = slope.astype(bf16)
        part = dense(active, down_part(buf, at))
        feed = part if feed is None else feed + part
    closing = jax.nn.sigmoid(dense(n2, unit(buf, 2)) + vec[3:4, :])
    gated = closing * feed
    return middle + gated, closing, gated * (1.0 - closing)


def feed_kernel(place, x_ref, n1_ref, o_ref, vec_ref, rest_ref,
                y_ref, n2_ref, scale_ref, ga_ref, ta_ref, h_ref, slope_ref, gf_ref, tf_ref, buf, sems):
    at_start([rest_copy(rest_ref, buf, sems.at[0], 0, REST, 0)])
    vec = vec_ref[...]
    middle, n2, _, scale, ga, ta = gated_rows(x_ref[...], n1_ref[...], o_ref[...], vec, buf)
    ga_ref[...] = ga.astype(bf16)
    ta_ref[...] = ta.astype(bf16)
    n2_ref[...] = n2
    scale_ref[...] = jnp.broadcast_to(scale, scale_ref.shape)
    y, gf, tf = feed_rows(middle, n2, vec, buf, h_ref, slope_ref, slice(None))
    gf_ref[...] = gf.astype(bf16)
    tf_ref[...] = tf.astype(bf16)
    y_ref[...] = y.astype(bf16)


def feed_forward(place, x, n1, o, vec, rest, waits=()):
    length, width = x.shape
    wide = 4 * width
    row, half = rows_of(width), struct((length, width), bf16)
    big, bigs = rows_of(wide), struct((length, wide), bf16)
    return call(
        feed_kernel,
        (length // ROWS,),
        [row, row, row, whole(16, width), ANY],
        [row, row, rows_of(128), row, row, big, big, row, row],
        [half, half, struct((length, 128), f32), half, half, bigs, bigs, half, half],
        [pltpu.VMEM((PARTS, REST, width), bf16), pltpu.SemaphoreType.DMA((1,))],
        flops=2 * length * width * (3 * width + 2 * wide),
        moved=24_000_000,
        waits=waits,
    )(place, x, n1, o, vec, rest)


def back_rows(e, hat, scale, ga, ta, slope_ref, gf, tf, gain, buf, du_ref, at_rows):
    df = (e * gf).astype(bf16)
    dzf = (e * tf).astype(bf16)
    dn2 = against(dzf, unit(buf, 2))
    for at in range(4):
        cut = slice(at * 512, at * 512 + 512)
        du = (against(df, down_part(buf, at)) * slope_ref[:, cut].astype(f32)).astype(bf16)
        du_ref[at_rows, cut] = du
        dn2 = dn2 + against(du, unit(buf, 3 + at))
    dm = e + norm_back(dn2, hat, scale, gain)
    da = (dm * ga).astype(bf16)
    dza = (dm * ta).astype(bf16)
    return dm, df, dzf, da, dza, against(da, unit(buf, 0)).astype(bf16)


def put_lanes(swap, keep, send, values, rows, first):
    for y in range(2):
        low, high = (values[(y * 2 + c) * rows : (y * 2 + c + 1) * rows] for c in range(2))
        keep[y, first : first + rows, :] = jnp.where(swap, high, low)
        send[y, first : first + rows, :] = jnp.where(swap, low, high)


def rest_grads(place, keep, send, o, n1, n2, h, da, dza, dzf, du_ref, df, sums):
    put = functools.partial(put_lanes, place[2] == 1, keep, send)
    put(cross(o, da).astype(bf16), UNIT, 0)
    put(cross(n1, dza).astype(bf16), UNIT, UNIT)
    put(cross(n2, dzf).astype(bf16), UNIT, 2 * UNIT)
    for at in range(4):
        put(cross(n2, du_ref[:, at * 512 : at * 512 + 512]).astype(bf16), UNIT, (3 + at) * UNIT)
    put(cross(h, df).astype(bf16), 4 * UNIT, 7 * UNIT)
    small = jnp.concatenate([sums, jnp.zeros((8, sums.shape[1]), f32)], axis=0).astype(bf16)
    for ref in (keep, send):
        for y in range(2):
            ref[y, REST:, :] = small


def keep_rows(at_rows, refs, values):
    for ref, value in zip(refs, values):
        ref[at_rows, :] = value


def add_sums(sums, dza, dzf):
    rows = [jnp.sum(part.astype(f32), axis=0, keepdims=True) for part in (dza, dzf)]
    new = jnp.concatenate(rows + [jnp.zeros((6, dza.shape[1]), f32)], axis=0)
    sums[...] = jnp.where(pl.program_id(0) == 0, new, sums[...] + new)


def turn_kernel(count, place, x_ref, n1_ref, o_ref, e_ref, vec_ref, o_cols, n1_cols, rest_ref,
                y_ref, dm_ref, dza_ref, do_ref, keep, send, buf, h, du, slope, n2, df, dzf, da, dza, sums, sems):
    step = pl.program_id(0)
    at_start([rest_copy(rest_ref, buf, sems.at[0], 0, REST, 0)])

    @pl.when(step < count)
    def _():
        at_rows = pl.ds(pl.multiple_of(step * ROWS, ROWS), ROWS)
        vec = vec_ref[...]
        middle, low, hat, scale, ga, ta = gated_rows(x_ref[...], n1_ref[...], o_ref[...], vec, buf)
        y, gf, tf = feed_rows(middle, low, vec, buf, h, slope, at_rows)
        y_ref[...] = y.astype(bf16)
        e = e_ref[...].astype(f32)
        dm, *parts, grad_o = back_rows(e, hat, scale, ga, ta, slope, gf, tf, vec[1:2, :], buf, du, at_rows)
        dm_ref[...] = dm
        do_ref[...] = grad_o
        keep_rows(at_rows, (n2, df, dzf, da, dza), (low, *parts))
        dza_ref[...] = parts[3]
        add_sums(sums, parts[3], parts[1])

    @pl.when(step >= count)
    def _():
        at = step - count
        narrow, wide = pl.ds(pl.multiple_of(at * 128, 128), 128), pl.ds(pl.multiple_of(at * 512, 512), 512)
        lefts = (o_cols[...], n1_cols[...], n2[:, narrow], h[:, wide])
        rest_grads(place, keep, send, *lefts, da[...], dza[...], dzf[...], du, df[...], sums[...])


def late_specs(length, width, count):
    row = pl.BlockSpec((ROWS, width), lambda i, place: (jnp.minimum(i, count - 1), 0))
    cols = pl.BlockSpec((length, width // 4), lambda i, place: (0, jnp.maximum(i - count, 0)))
    grad = pl.BlockSpec((2, REST + 16, width), lambda i, place: (jnp.maximum(i - count, 0), 0, 0))
    return row, cols, grad


def turn(place, x, n1, o, e, vec, rest, waits=()):
    length, width = x.shape
    wide, count = 4 * width, length // ROWS
    row, cols, grad = late_specs(length, width, count)
    half, tall = struct((length, width), bf16), pltpu.VMEM((length, width), bf16)
    return call(
        functools.partial(turn_kernel, count),
        (count + 4,),
        [row] * 4 + [whole(16, width), cols, cols, ANY],
        [row] * 4 + [grad] * 2,
        [half, struct((length, width), f32), half, half] + [struct((PARTS // 2, REST + 16, width), bf16)] * 2,
        [pltpu.VMEM((PARTS, REST, width), bf16)]
        + [pltpu.VMEM((length, wide), bf16)] * 2
        + [pltpu.VMEM((ROWS, wide), bf16)]
        + [tall] * 5
        + [pltpu.VMEM((8, width), f32), pltpu.SemaphoreType.DMA((1,))],
        flops=6 * length * width * (3 * width + 2 * wide),
        moved=24_000_000,
        waits=waits,
    )(place, x, n1, o, e, vec, o, n1, rest)


def dx_rows(x, dm, dqkv, dza, gain, buf, gate):
    width = x.shape[1]
    dn = against(dza, gate[...].reshape(PARTS * UNIT, width))
    for at, part in enumerate(dqkv):
        dn = dn + against(part, unit(buf, at))
    hat, scale = normalise(x.astype(f32))
    return dm + norm_back(dn, hat, scale, gain)


def joint_kernel(count, many, place, x_ref, dm1_ref, dq_ref, dk_ref, dv_ref, dza1_ref, e_ref,
                 n2_ref, scale_ref, ga_ref, ta_ref, slope_ref, gf_ref, tf_ref, vec1_ref, vec_ref,
                 o_cols, n1_cols, n2_cols, h_cols, rest1_ref, rest_ref, *refs):
    dx_ref, low_ref, dm_ref, dza_ref, do_ref, keep, send, head, gate, buf, du, df, dzf, da, dza, sums, sems = refs[many:]
    step = pl.program_id(0)
    copies = fetches(place, refs[:many], head, sems, ((0, 3 * UNIT),))[0]
    copies.append(rest_copy(rest1_ref, gate, sems.at[1], UNIT, 2 * UNIT, UNIT))
    copies.append(rest_copy(rest_ref, buf, sems.at[2], 0, REST, 0))
    at_start(copies)

    @pl.when(step < count)
    def _():
        at_rows = pl.ds(pl.multiple_of(step * ROWS, ROWS), ROWS)
        dqkv = (dq_ref[...], dk_ref[...], dv_ref[...])
        dx = dx_rows(x_ref[...], dm1_ref[...], dqkv, dza1_ref[...], vec1_ref[0:1, :], head, gate)
        dx_ref[...] = dx
        low = dx.astype(bf16)
        low_ref[...] = low
        e = e_ref[...].astype(f32) + low.astype(f32)
        gain = vec_ref[1:2, :]
        hat = n2_ref[...].astype(f32) * (1.0 / gain)
        ga, ta, gf, tf = (ref[...].astype(f32) for ref in (ga_ref, ta_ref, gf_ref, tf_ref))
        dm, *parts, grad_o = back_rows(e, hat, scale_ref[:, 0:1], ga, ta, slope_ref, gf, tf, gain, buf, du, at_rows)
        dm_ref[...] = dm
        do_ref[...] = grad_o
        keep_rows(at_rows, (df, dzf, da, dza), parts)
        dza_ref[...] = parts[3]
        add_sums(sums, parts[3], parts[1])

    @pl.when(step >= count)
    def _():
        lefts = (o_cols[...], n1_cols[...], n2_cols[...], h_cols[...])
        rest_grads(place, keep, send, *lefts, da[...], dza[...], dzf[...], du, df[...], sums[...])


def joint_back(place, x, dm1, dqkv, dza1, vec1, head, rest1, e, kept, rest, waits=()):
    n1, o, vec, n2, scale, ga, ta, h, slope, gf, tf = kept
    length, width = x.shape
    wide, count = 4 * width, length // ROWS
    row, cols, grad = late_specs(length, width, count)
    lanes = pl.BlockSpec((ROWS, 128), lambda i, place: (jnp.minimum(i, count - 1), 0))
    big = pl.BlockSpec((ROWS, wide), lambda i, place: (jnp.minimum(i, count - 1), 0))
    wides = pl.BlockSpec((length, wide // 4), lambda i, place: (0, jnp.maximum(i - count, 0)))
    half, tall = struct((length, width), bf16), pltpu.VMEM((length, width), bf16)
    floats = struct((length, width), f32)
    return call(
        functools.partial(joint_kernel, count, len(head)),
        (count + 4,),
        [row] * 8 + [lanes, row, row, big, row, row, whole(16, width), whole(16, width), cols, cols, cols, wides, ANY, ANY]
        + [ANY] * len(head),
        [row] * 5 + [grad] * 2,
        [floats, half, floats, half, half] + [struct((PARTS // 2, REST + 16, width), bf16)] * 2,
        [pltpu.VMEM((PARTS, 3 * UNIT, width), bf16), pltpu.VMEM((PARTS, UNIT, width), bf16), pltpu.VMEM((PARTS, REST, width), bf16)]
        + [pltpu.VMEM((length, wide), bf16)]
        + [tall] * 4
        + [pltpu.VMEM((8, width), f32), pltpu.SemaphoreType.DMA((3,))],
        flops=4 * length * width * (5 * width + 2 * wide),
        moved=40_000_000,
        waits=waits,
    )(place, x, dm1, *dqkv, dza1, e, n2, scale, ga, ta, slope, gf, tf, vec1, vec, o, n1, n2, h, rest1, rest, *head)


def split3(value):
    first = value.astype(bf16)
    rest = value - first.astype(f32)
    second = rest.astype(bf16)
    third = (rest - second.astype(f32)).astype(bf16)
    return first, second, third


def attend_back_kernel(block, place, q_ref, k_ref, v_ref, o_ref, s_ref, do_ref, dq_ref, dk_ref, dv_ref,
                       q_s, k_s, v_s, do_s, acc):
    length = q_ref.shape[0]
    lane = lax.broadcasted_iota(jnp.int32, (length, 128), 1)
    row = lax.broadcasted_iota(jnp.int32, (block, block), 0)
    col = lax.broadcasted_iota(jnp.int32, (block, block), 1)
    q, k, v, do = q_ref[...], k_ref[...], v_ref[...], do_ref[...]
    zero = jnp.zeros_like(q)
    product = do.astype(f32) * o_ref[...].astype(f32)
    for head in range(2):
        low = head * HD
        other = (1 - head) * HD
        mine = (lane >= low) & (lane < low + HD)
        logs = -s_ref[:, low : low + 1]
        delta = -jnp.sum(jnp.where(mine, product, 0.0), axis=1, keepdims=True)
        one = jnp.where((lane >= other) & (lane < other + 3), jnp.ones_like(q), zero)
        q_aug, do_aug = jnp.where(mine, q, zero), jnp.where(mine, do, zero)
        for at, (part, piece) in enumerate(zip(split3(logs), split3(delta))):
            here = lane == other + at
            q_aug = jnp.where(here, part, q_aug)
            do_aug = jnp.where(here, piece, do_aug)
        q_s[head] = q_aug
        do_s[head] = do_aug
        k_s[head] = jnp.where(mine, k, one)
        v_s[head] = jnp.where(mine, v, one)
    for index in range(length // block):
        start, stop = index * block, (index + 1) * block
        kgrads, vgrads = [], []
        for head in range(2):
            kb, vb = k_s[head, start:stop, :], v_s[head, start:stop, :]
            scores = against(kb, q_s[head, start:, :])
            first = jnp.where(row <= col, scores[:, :block], -1e30)
            scores = jnp.concatenate([first, scores[:, block:]], axis=1) if stop < length else first
            probs = jnp.exp(scores)
            grads = (probs * against(vb, do_s[head, start:, :])).astype(bf16)
            vgrads.append(dense(probs.astype(bf16), do_ref[start:, :]))
            kgrads.append(dense(grads, q_ref[start:, :]))
            part = cross(grads, kb)
            if index == 0:
                acc[head] = part
            else:
                acc[head, start:, :] += part
        half = lane[:block] < HD
        dk_ref[start:stop, :] = jnp.where(half, kgrads[0], kgrads[1]).astype(bf16)
        dv_ref[start:stop, :] = jnp.where(half, vgrads[0], vgrads[1]).astype(bf16)
    dq_ref[...] = (jnp.where(lane < HD, acc[0], acc[1]) * 0.125).astype(bf16)


def attend_back(place, q, k, v, o, s, do, start, count=2, onto=(), waits=(), block=256):
    length, width = q.shape
    pair = pl.BlockSpec((length, 128), lambda i, place: (0, i + start))
    return call(
        functools.partial(attend_back_kernel, block),
        (count,),
        [pair] * 6,
        [pair] * 3,
        [struct((length, width), bf16)] * 3,
        [pltpu.VMEM((2, length, 128), bf16)] * 4 + [pltpu.VMEM((2, length, 128), f32)],
        flops=5_000_000_000 * count,
        moved=5_000_000,
        onto=onto,
        waits=waits,
    )(place, q, k, v, o, s, do)


def qkv_back_kernel(many, place, x_ref, dm_ref, dq_ref, dk_ref, dv_ref, dza_ref, vec_ref, rest_ref, *refs):
    dx_ref, low_ref, buf, gate, sems = refs[many:]
    copies = fetches(place, refs[:many], buf, sems, ((0, 3 * UNIT),))[0]
    at_start(copies + [rest_copy(rest_ref, gate, sems.at[1], UNIT, 2 * UNIT, UNIT)])
    dqkv = (dq_ref[...], dk_ref[...], dv_ref[...])
    dx = dx_rows(x_ref[...], dm_ref[...], dqkv, dza_ref[...], vec_ref[0:1, :], buf, gate)
    dx_ref[...] = dx
    low_ref[...] = dx.astype(bf16)


def qkv_back(place, x, dm, dq, dk, dv, dza, vec, weights, rest, waits=()):
    length, width = x.shape
    row = rows_of(width)
    return call(
        functools.partial(qkv_back_kernel, len(weights)),
        (length // ROWS,),
        [row] * 6 + [whole(16, width), ANY] + [ANY] * len(weights),
        [row, row],
        [struct((length, width), f32), struct((length, width), bf16)],
        [pltpu.VMEM((PARTS, 3 * UNIT, width), bf16), pltpu.VMEM((PARTS, UNIT, width), bf16), pltpu.SemaphoreType.DMA((2,))],
        flops=2 * length * width * 4 * width,
        moved=12_000_000,
        waits=waits,
    )(place, x, dm, dq, dk, dv, dza, vec, rest, *weights)


def put(place, outs, values, rows, first):
    keep, send = outs
    for y in range(2):
        low, high = (values[(y * 2 + c) * rows : (y * 2 + c + 1) * rows] for c in range(2))
        at = place[1] ^ y
        swap = place[2] == 1
        keep[at, 0, first : first + rows, :] = jnp.where(swap, high, low)
        send[at, 0, first : first + rows, :] = jnp.where(swap, low, high)


def grad_outs(rows, width):
    out = pl.BlockSpec((2, 1, rows, width), lambda i, place: (0, (i - place[0]) & 3, 0, 0))
    return [out, out], [struct((2, 4, rows, width), bf16)] * 2


def first_grad_kernel(place, *refs):
    outs = refs[-2:]
    for layer in range(len(refs) // 4):
        n1_ref = refs[4 * layer]
        for at, ref in enumerate(refs[4 * layer + 1 : 4 * layer + 4]):
            put(place, outs, cross(n1_ref[...], ref[...]).astype(bf16), UNIT, (3 * layer + at) * UNIT)


def first_grad(place, *layers, waits=()):
    length, width = layers[0][0].shape
    cols = pl.BlockSpec((length, width // 4), lambda i, place: (0, i))
    specs, shapes = grad_outs(3 * UNIT * len(layers), width)
    return call(
        first_grad_kernel,
        (4,),
        ([cols] + [whole(length, width)] * 3) * len(layers),
        specs,
        shapes,
        flops=2 * length * width * 3 * width * len(layers),
        moved=9_000_000 * len(layers),
        waits=waits,
    )(place, *(value for layer in layers for value in layer))


def moved_z(value, steps):
    count = lax.axis_size("dp")
    return lax.ppermute(value, "dp", [(d, (d + 4 * steps) % count) for d in range(count)])


def swapped(value, bit):
    return lax.ppermute(value, "dp", [(d, d ^ bit) for d in range(lax.axis_size("dp"))])


def crossed(value, sources=(0, 1)):
    return lax.ppermute(value, "section", [(s, 1 - s) for s in sources])


def along_z(block):
    return [block] + [moved_z(block, k) for k in (1, 2, 3)]


def across(own):
    beside = swapped(own, 2)
    return own, beside, swapped(own, 1), swapped(beside, 1)


def spread_whole(blocks):
    blocks = blocks.reshape(4, 2, 2, *blocks.shape[1:])
    blocks = jnp.stack([blocks[0], blocks[3], blocks[2], blocks[1]])
    return tuple(blocks[:, index & 1, index >> 1] for index in range(4))


def gather_whole(values, axis):
    values = lax.all_gather(values.astype(bf16), "dp", axis=axis, tiled=True)
    return lax.all_gather(values, "section", axis=0, tiled=True)


def split_rows(matrix, cols):
    rows, width = matrix.shape[0] // PARTS, matrix.shape[1] // cols
    return matrix.reshape(PARTS, rows, cols, width).transpose(0, 2, 1, 3).reshape(PARTS, cols * rows, width)


def merge_rows(blocks, cols):
    rows, width = blocks.shape[1] // cols, blocks.shape[2]
    return blocks.reshape(PARTS, cols, rows, width).transpose(0, 2, 1, 3).reshape(PARTS * rows, cols * width)


def weights_whole(w_qkv, w_out, w_gates, w_up, w_down, gains, biases):
    w_qkv, w_out, w_up, w_down = (gather_whole(w, 1) for w in (w_qkv, w_out, w_up, w_down))
    w_gates, gains, biases = (gather_whole(w, 2) for w in (w_gates, gains, biases))
    heads, tails = [], []
    for layer in range(2):
        lines = jnp.concatenate([gains[layer], biases[layer], jnp.zeros((12, gains.shape[2]), bf16)], axis=0)
        lines = jnp.concatenate([lines[None], jnp.zeros((PARTS - 1, *lines.shape), bf16)], axis=0)
        heads.append(spread_whole(jnp.concatenate([split_rows(w_qkv[layer], 3), lines], axis=1)))
        parts = [w_out[layer], w_gates[layer, 0], w_gates[layer, 1]]
        parts = [split_rows(part, 1) for part in parts] + [split_rows(w_up[layer], 4), split_rows(w_down[layer], 1)]
        tails.append(jnp.concatenate(parts, axis=1))
    return heads, tails


def joined(pieces):
    return jnp.stack(pieces).transpose(2, 1, 0, 3, 4).reshape(PARTS, *pieces[0].shape[2:])


def collect_whole(early, rest):
    early, rest = joined(early), jnp.stack(rest, axis=1).reshape(PARTS, *rest[0].shape[1:])
    parts = [merge_rows(early, 3), merge_rows(rest[:, :UNIT], 1)]
    parts += [jnp.stack([merge_rows(rest[:, at * UNIT : (at + 1) * UNIT], 1) for at in (1, 2)])]
    parts += [merge_rows(rest[:, 3 * UNIT : 7 * UNIT], 4), merge_rows(rest[:, 7 * UNIT : REST], 1), rest[0, REST : REST + 2]]
    axes = (0, 0, 1, 0, 0, 1)
    parts = [lax.psum_scatter(part.astype(f32), "dp", scatter_dimension=axis, tiled=True) for part, axis in zip(parts, axes)]
    return [lax.psum(part, "section") for part in parts]


def fold_core(keep, got):
    away = (keep[1].astype(f32) + got[1].astype(f32)).astype(bf16)
    return away, keep[0].astype(f32) + got[0].astype(f32)


def scattered(keep, got):
    lanes = [[d for d in range(PARTS) if d % 2 == c] for c in range(2)]
    both = (keep.astype(f32) + got.astype(f32)).astype(bf16)
    return lax.psum_scatter(both, "dp", scatter_dimension=0, axis_index_groups=lanes)


def fold_y(near, got):
    near = near + got.astype(f32)
    return near[0], [near[k].astype(bf16) for k in (1, 2, 3)]


def fold_z(total, gots):
    for got in gots:
        total = total + got.astype(f32)
    return total


def pack_kernel(place, qkv_ref, out_ref, gates_ref, up_ref, down_ref, lines_ref, head_ref, tail_ref):
    width = out_ref.shape[2]
    for at in range(3):
        head_ref[at * UNIT : (at + 1) * UNIT, :] = qkv_ref[0, :, at * width : (at + 1) * width].astype(bf16)
    head_ref[3 * UNIT :, :] = lines_ref[...].astype(bf16)
    tail_ref[:UNIT, :] = out_ref[0].astype(bf16)
    for at in range(2):
        tail_ref[(1 + at) * UNIT : (2 + at) * UNIT, :] = gates_ref[0, at].astype(bf16)
    for at in range(4):
        tail_ref[(3 + at) * UNIT : (4 + at) * UNIT, :] = up_ref[0, :, at * width : (at + 1) * width].astype(bf16)
    tail_ref[7 * UNIT :, :] = down_ref[0].astype(bf16)


def pack(place, index, w_qkv, w_out, w_gates, w_up, w_down, gains, biases):
    width = w_out.shape[2]
    lines = jnp.concatenate([gains[0], biases[0]], axis=0)
    mine = jnp.arange(width)[None, :] // UNIT == index
    lines = jnp.concatenate([jnp.where(mine, jnp.tile(lines, (1, PARTS)), 0.0), jnp.zeros((12, width), f32)], axis=0)
    arrays = (w_qkv, w_out, w_gates, w_up, w_down, lines)
    return call(
        pack_kernel,
        (1,),
        [whole(*array.shape) for array in arrays],
        [whole(FIRST, width), whole(REST, width)],
        [struct((FIRST, width), bf16), struct((REST, width), bf16)],
        moved=3_000_000,
    )(place, *arrays)


def after(value, *others):
    return lax.optimization_barrier((value, *others))[0]


def gain_grads(grads, w_qkv, w_gates, w_up, gains):
    d_qkv, _, d_gates, d_up = grads[:4]
    w_qkv, w_gates, w_up, gains = (w[0].astype(bf16).astype(f32) for w in (w_qkv, w_gates, w_up, gains))
    first = jnp.sum(w_qkv * d_qkv, axis=1) + jnp.sum(w_gates[0] * d_gates[0], axis=1)
    second = jnp.sum(w_up * d_up, axis=1) + jnp.sum(w_gates[1] * d_gates[1], axis=1)
    return jnp.stack([first, second]) / gains


def finish_kernel(place, own0, got0, own1, got1, own2, got2, own3, got3, w_qkv, w_gates, w_up, gains,
                  g_qkv, g_out, g_gates, g_up, g_down, g_gains, g_biases):
    width = own0.shape[1]
    first = place[3] == 0

    def total(start, stop):
        early = own0[start:stop, :] + got0[start:stop, :].astype(f32), own1[start:stop, :] + got1[start:stop, :].astype(f32)
        return jnp.where(first, *early)

    def rest(start, stop):
        return jnp.where(
            first,
            own2[start:stop, :].astype(f32) + got2[start:stop, :].astype(f32),
            own3[start:stop, :].astype(f32) + got3[start:stop, :].astype(f32),
        )

    def against_weight(weight, grad):
        return jnp.sum(weight.astype(bf16).astype(f32) * grad, axis=1, keepdims=True)

    rows = lax.broadcasted_iota(jnp.int32, (UNIT, UNIT), 0)
    diagonal = rows == lax.broadcasted_iota(jnp.int32, (UNIT, UNIT), 1)
    lines = [None, None]
    for at in range(2):
        part = rest((1 + at) * UNIT, (2 + at) * UNIT)
        g_gates[0, at] = part
        lines[at] = against_weight(w_gates[0, at], part)
    for at in range(3):
        cut = slice(at * width, at * width + width)
        part = total(at * UNIT, (at + 1) * UNIT)
        g_qkv[0, :, cut] = part
        lines[0] += against_weight(w_qkv[0, :, cut], part)
    for at in range(4):
        cut = slice(at * width, at * width + width)
        part = rest((3 + at) * UNIT, (4 + at) * UNIT)
        g_up[0, :, cut] = part
        lines[1] += against_weight(w_up[0, :, cut], part)
    g_out[0] = rest(0, UNIT)
    g_down[0] = rest(7 * UNIT, REST)
    sums = rest(REST, REST + 16)
    index = (place[0] * 2 + place[1]) * 2 + place[2]
    for at in range(2):
        line = jnp.sum(jnp.where(diagonal, lines[at], 0.0), axis=0, keepdims=True)
        g_gains[0, at : at + 1, :] = line / gains[0, at : at + 1, :].astype(bf16).astype(f32)
        mine = jnp.zeros((1, UNIT), f32)
        for part in range(PARTS):
            mine = jnp.where(index == part, sums[at : at + 1, part * UNIT : (part + 1) * UNIT], mine)
        g_biases[0, at : at + 1, :] = mine


def finish(place, sums, masters):
    w_qkv, w_out, w_gates, w_up, w_down, gains, biases = masters
    inputs = (*sums, w_qkv, w_gates, w_up, gains)
    shapes = [struct(master.shape, f32) for master in (w_qkv, w_out, w_gates, w_up, w_down, gains, biases)]
    return call(
        finish_kernel,
        (1,),
        [whole(*value.shape) for value in inputs],
        [whole(*shape.shape) for shape in shapes],
        shapes,
        moved=6_000_000,
    )(place, *inputs)


def per_device(tokens, cotangent, w_qkv, w_out, w_gates, w_up, w_down, norm_gains, gate_biases):
    section = lax.axis_index("section")
    index = lax.axis_index("dp")
    fast = lax.axis_size("dp") == PARTS
    first = section == 0
    masters = (w_qkv, w_out, w_gates, w_up, w_down, norm_gains, gate_biases)

    def pick(own, other):
        return jnp.where(first, own, other), jnp.where(first, other, own)

    x = jnp.where(first, tokens[0, 0], tokens[1, 0])
    seeds = [cotangent[0, m, 0] for m in range(2)]
    own_seed, other_seed = jnp.where(first, seeds[0], seeds[1]), jnp.where(first, seeds[1], seeds[0])
    if fast:
        y0, y1, theirs, dxs, lows, grads = run(x, own_seed, other_seed, masters, index, section, pick)
    else:
        place = jnp.zeros((3,), jnp.int32)
        heads, rest = weights_whole(*masters)
        n0, q0, k0, v0, vec0 = qkv_forward(place, x, heads[0])
        o0, s0 = attend_forward(place, q0, k0, v0, 2, onto=attend_forward(place, q0, k0, v0, 0))
        y0, *kept = feed_forward(place, x, n0, o0, vec0, rest[0])
        n1, q1, k1, v1, vec1 = qkv_forward(place, y0, heads[1])
        o1, s1 = attend_forward(place, q1, k1, v1, 2, onto=attend_forward(place, q1, k1, v1, 0))
        seeds = pick(own_seed, crossed(other_seed))
        y1, dm, dza, do, *later1 = turn(place, y0, n1, o1, seeds[1], vec1, rest[1])
        dqkv = attend_back(place, q1, k1, v1, o1, s1, do, 2, onto=attend_back(place, q1, k1, v1, o1, s1, do, 0))
        early1 = first_grad(place, (n1, *dqkv))
        dx1, low1, dm, dza, do, *later0 = joint_back(
            place, y0, dm, dqkv, dza, vec1, heads[1], rest[1], seeds[0], (n0, o0, vec0, *kept), rest[0]
        )
        dqkv = attend_back(place, q0, k0, v0, o0, s0, do, 2, onto=attend_back(place, q0, k0, v0, o0, s0, do, 0))
        early0 = first_grad(place, (n0, *dqkv))
        dx0, low0 = qkv_back(place, x, dm, *dqkv, dza, vec0, heads[0], rest[0])
        grads0, grads1 = collect_whole(early0, later0), collect_whole(early1, later1)
        dxs, lows = (dx0, dx1), (crossed(low0, (1,)), crossed(low1, (0,)))
        theirs = crossed(jnp.where(first, y1, y0))
        grads = [jnp.where(first, *pair) for pair in zip(grads0, grads1)]
        grads.insert(5, gain_grads(grads, w_qkv, w_gates, w_up, norm_gains))
        grads = [grad[None] for grad in grads]

    mine = jnp.where(first, y0, y1)
    block = jnp.stack([jnp.where(first, mine, theirs), jnp.where(first, theirs, mine)])[None, :, None]
    in_grads = jnp.stack([jnp.where(first, dxs[0], lows[1].astype(f32)), dxs[1]])
    last = jnp.where(first, lows[0].astype(f32), dxs[1])
    in_grads = lax.dynamic_update_slice(in_grads, last[None], (1, 0, 0))[None, :, None]
    return (block, in_grads, *grads)


def run(x, own_seed, other_seed, masters, index, section, pick):
    first = section == 0
    width = x.shape[1]
    place = jnp.stack([index // 4, (index // 2) & 1, index & 1, section]).astype(jnp.int32)
    head, tail = pack(place, index, *masters)
    heads = pick(head, crossed(head))
    tails = pick(tail, crossed(tail))
    tail0 = lax.all_gather(tails[0], "dp", axis=0)

    def cores(z, y):
        return z, y, swapped(z, 1), swapped(y, 1)

    zh0 = jnp.stack(along_z(heads[0]))
    yh0 = swapped(zh0, 2)
    head0 = cores(zh0, yh0)
    n1, q, k, v, vec = qkv_forward(place, x, head0)
    zh1 = along_z(after(heads[1], n1))
    o, s = attend_forward(place, q, k, v, 0)
    zh1 = jnp.stack([after(part, o) for part in zh1])
    yh1 = swapped(zh1, 2)
    o, s = attend_forward(place, q, k, v, 2, onto=(o, s), waits=(zh1,))
    tail0 = after(tail0, o)
    tail1 = lax.all_gather(after(tails[1], tail0), "dp", axis=0)
    other_seed = crossed(after(other_seed, o))
    y0, *held = feed_forward(place, x, n1, o, vec, tail0)
    head1 = cores(after(zh1, y0), after(yh1, y0))
    kept0 = (n1, o, vec, *held)
    layer0 = (q, k, v, o, s)

    n1, q, k, v, vec = qkv_forward(place, y0, head1)
    o, s = attend_forward(place, q, k, v, 0)
    o, s = attend_forward(place, q, k, v, 2, onto=(o, s))
    seeds = pick(own_seed, after(other_seed, o))
    y1, dm, dza, do, keep, send = turn(place, y0, n1, o, seeds[1], vec, tail1)
    got = swapped(send, 1)
    theirs = crossed(jnp.where(first, y1, y0))
    dqkv = attend_back(place, q, k, v, o, s, do, 0, 1)
    rest1 = scattered(keep, after(got, dqkv[0]))
    dqkv = attend_back(place, q, k, v, o, s, do, 1, 3, onto=dqkv)
    keep_b, send_b = first_grad(place, (n1, *dqkv))
    got_b = swapped(send_b, 1)
    dx1, low1, dm, dza, do, keep, send = joint_back(
        place, y0, dm, dqkv, dza, vec, head1, tail1, seeds[0], kept0, tail0, waits=(keep_b, theirs)
    )
    n1, o, vec = kept0[:3]
    q, k, v, o, s = layer0
    got = swapped(send, 1)
    away, near = fold_core(keep_b, after(got_b, low1))
    got_b = swapped(away, 2)
    other1 = crossed(low1, (0,))
    dqkv = attend_back(place, q, k, v, o, s, do, 0, 1, waits=(away,))
    rest0 = scattered(keep, after(got, dqkv[0]))
    dqkv = attend_back(place, q, k, v, o, s, do, 1, 3, onto=dqkv)
    own, sends = fold_y(near, after(got_b, dqkv[0]))
    gots = [moved_z(part, at + 1) for at, part in enumerate(sends)]
    keep, send = first_grad(place, (n1, *dqkv), waits=(other1, *sends))
    got = swapped(send, 1)
    away, near = fold_core(keep, got)
    got = swapped(away, 2)
    dx0, low0 = qkv_back(place, x, dm, *dqkv, dza, vec, head0, tail0, waits=(away,))
    early1 = fold_z(own, [after(part, low0) for part in gots])
    rest1 = after(rest1, low0)
    last1 = crossed(jnp.concatenate([rest1, early1.astype(bf16)]), (0,))
    other0 = crossed(low0, (1,))
    own, sends = fold_y(near, after(got, low0))
    gots = [moved_z(part, at + 1) for at, part in enumerate(sends)]
    early0 = fold_z(own, gots)
    last0 = crossed(early0.astype(bf16), (1,))
    rest0 = after(rest0, last0, last1, other0)
    later0 = crossed(rest0, (1,))
    sums = (early0, last0, early1, last1[REST + 16 :], rest0, later0, rest1, last1[: REST + 16])
    grads = finish(place, sums, masters)
    return y0, y1, theirs, (dx0, dx1), (other0, other1), grads


def solution(mesh):
    placed = (
        P(None, "dp", None, None),
        P("section", None, "dp", None, None),
        P("section", "dp", None),
        P("section", "dp", None),
        P("section", None, "dp", None),
        P("section", "dp", None),
        P("section", "dp", None),
        P("section", None, "dp"),
        P("section", None, "dp"),
    )
    return jax.shard_map(
        per_device,
        mesh=mesh,
        in_specs=placed,
        out_specs=(P("section", None, "dp", None, None), P("section", None, "dp", None, None)) + placed[2:],
        check_vma=False,
    )
```

```python
import functools

import jax
import jax.numpy as jnp
from jax import lax
from jax.experimental import pallas as pl
from jax.experimental.pallas import tpu as pltpu
from jax.sharding import PartitionSpec as P

HD = 64
ROWS = 512
bf16 = jnp.bfloat16
f32 = jnp.float32
root_term = 0.7978845608
cube_term = 0.044715
VMEM = 56 * 1024 * 1024
PARTS = 16
UNIT = 32
FIRST = 3 * UNIT + 16
REST = 11 * UNIT


def dense(left, right):
    return jnp.dot(left, right, preferred_element_type=f32)


def cross(left, right):
    return lax.dot_general(left, right, (((0,), (0,)), ((), ())), preferred_element_type=f32)


def against(left, right):
    return lax.dot_general(left, right, (((1,), (1,)), ((), ())), preferred_element_type=f32)


def normalise(values):
    centred = values - jnp.mean(values, axis=-1, keepdims=True)
    spread = jnp.mean(centred * centred, axis=-1, keepdims=True)
    scale = lax.rsqrt(spread + 1e-05)
    return centred * scale, scale


def norm_back(grad, hat, scale, gain):
    spread = grad * gain
    first = jnp.mean(spread, axis=-1, keepdims=True)
    second = jnp.mean(spread * hat, axis=-1, keepdims=True)
    return scale * (spread - first - hat * second)


ANY = pl.BlockSpec(memory_space=pl.ANY)


def struct(shape, dtype):
    return jax.ShapeDtypeStruct(shape, dtype)


def rows_of(width):
    return pl.BlockSpec((ROWS, width), lambda i, place: (i, 0))


def whole(*shape):
    return pl.BlockSpec(shape, lambda i, place: (0,) * len(shape))


def call(kernel, grid, in_specs, out_specs, out_shape, scratch=(), flops=0, moved=0, waits=(), onto=()):
    extra = len(onto) + len(waits)
    count = len(in_specs)

    def run(*args):
        def body(*refs):
            kernel(*refs[: 1 + count], *refs[1 + count + extra :])

        return pl.pallas_call(
            body,
            grid_spec=pltpu.PrefetchScalarGridSpec(
                num_scalar_prefetch=1, grid=grid, in_specs=in_specs + [ANY] * extra, out_specs=out_specs, scratch_shapes=list(scratch)
            ),
            out_shape=out_shape,
            input_output_aliases={1 + count + at: at for at in range(len(onto))},
            compiler_params=pltpu.CompilerParams(dimension_semantics=("arbitrary",), vmem_limit_bytes=VMEM),
            cost_estimate=pl.CostEstimate(flops=flops, bytes_accessed=moved, transcendentals=0),
        )(*args, *onto, *waits)

    return run


def fetches(place, sources, target, sems, cuts, base=0):
    copies = []
    for number, (start, stop) in enumerate(cuts):
        group = []
        for index, source in enumerate(sources):
            for slot in range(4):
                part = ((place[0] - slot) & 3) * 4 + (place[1] ^ (index & 1)) * 2 + (place[2] ^ (index >> 1))
                group.append(
                    pltpu.make_async_copy(
                        source.at[slot, pl.ds(start, stop - start)],
                        target.at[part, pl.ds(start - base, stop - start)],
                        sems.at[number],
                    )
                )
        copies.append(group)
    return copies


def unit(ref, at):
    return ref[:, at * UNIT : (at + 1) * UNIT, :].reshape(PARTS * UNIT, ref.shape[2])


def down_part(ref, at, start=7):
    return ref[at * 4 : at * 4 + 4, start * UNIT : (start + 4) * UNIT, :].reshape(16 * UNIT, ref.shape[2])


def rest_copy(source, target, sem, start, stop, base):
    cut, goal = pl.ds(start, stop - start), pl.ds(start - base, stop - start)
    return pltpu.make_async_copy(source.at[:, cut], target.at[:, goal], sem)


def at_start(copies):
    @pl.when(pl.program_id(0) == 0)
    def _():
        for copy in copies:
            copy.start()
        for copy in copies:
            copy.wait()


def qkv_kernel(many, place, x_ref, *refs):
    n_ref, q_ref, k_ref, v_ref, vec_ref, buf, sems = refs[many:]
    copies = fetches(place, refs[:many], buf, sems, ((0, FIRST),))[0]

    @pl.when(pl.program_id(0) == 0)
    def _():
        for copy in copies:
            copy.start()
        for copy in copies:
            copy.wait()
        vec_ref[...] = jnp.sum(buf[:, 3 * UNIT : 3 * UNIT + 16, :].astype(f32), axis=0)

    hat, _ = normalise(x_ref[...].astype(f32))
    n1 = (hat * vec_ref[0:1, :]).astype(bf16)
    n_ref[...] = n1
    q_ref[...] = (dense(n1, unit(buf, 0)).astype(bf16) * 0.125).astype(bf16)
    k_ref[...] = dense(n1, unit(buf, 1)).astype(bf16)
    v_ref[...] = dense(n1, unit(buf, 2)).astype(bf16)


def qkv_forward(place, x, weights, waits=()):
    length, width = x.shape
    row = rows_of(width)
    return call(
        functools.partial(qkv_kernel, len(weights)),
        (length // ROWS,),
        [row] + [ANY] * len(weights),
        [row] * 4 + [whole(16, width)],
        [struct((length, width), bf16)] * 4 + [struct((16, width), f32)],
        [pltpu.VMEM((PARTS, FIRST, width), bf16), pltpu.SemaphoreType.DMA((1,))],
        flops=2 * length * width * 3 * width,
        moved=8_000_000,
        waits=waits,
    )(place, x, *weights)


def attend_kernel(block, place, q_ref, k_ref, v_ref, o_ref, s_ref):
    length = q_ref.shape[0]
    lane = lax.broadcasted_iota(jnp.int32, (block, 128), 1)
    row = lax.broadcasted_iota(jnp.int32, (block, block), 0)
    col = lax.broadcasted_iota(jnp.int32, (block, block), 1)
    for index in range(length // block):
        start, stop = index * block, (index + 1) * block
        q = q_ref[start:stop, :]
        outs, logs = [], []
        for head in range(2):
            mine = (lane >= head * HD) & (lane < (head + 1) * HD)
            own = jnp.where(mine, q, jnp.zeros_like(q))
            scores = against(own, k_ref[:stop, :])
            last = jnp.where(row >= col, scores[:, start:], -1e30)
            scores = jnp.concatenate([scores[:, :start], last], axis=1) if start else last
            highest = jnp.max(scores, axis=1, keepdims=True)
            weights = jnp.exp(scores - highest)
            total = jnp.sum(weights, axis=1, keepdims=True)
            outs.append(dense(weights.astype(bf16), v_ref[:stop, :]) * (1.0 / total))
            logs.append(highest + jnp.log(total))
        o_ref[start:stop, :] = jnp.where(lane < HD, outs[0], outs[1]).astype(bf16)
        s_ref[start:stop, :] = jnp.where(lane < HD, logs[0], logs[1])


def attend_forward(place, q, k, v, start, onto=(), waits=(), block=256):
    length, width = q.shape
    pair = pl.BlockSpec((length, 128), lambda i, place: (0, i + start))
    return call(
        functools.partial(attend_kernel, block),
        (width // 256,),
        [pair] * 3,
        [pair, pair],
        [struct((length, width), bf16), struct((length, width), f32)],
        flops=6_000_000_000,
        moved=3_000_000,
        onto=onto,
        waits=waits,
    )(place, q, k, v)


def gelu(u):
    square = u * u
    inner = jnp.tanh(u * (root_term + (root_term * cube_term) * square))
    half = 0.5 + 0.5 * inner
    slope = half + (0.5 * root_term) * u * (1.0 - inner * inner) * (1.0 + (3.0 * cube_term) * square)
    return u * half, slope


def gated_rows(x, n1, o, vec, buf):
    branch = dense(o, unit(buf, 0))
    opening = jax.nn.sigmoid(dense(n1, unit(buf, 1)) + vec[2:3, :])
    gated = opening * branch
    middle = x.astype(f32) + gated
    hat, scale = normalise(middle)
    n2 = (hat * vec[1:2, :]).astype(bf16)
    return middle, n2, hat, scale, opening, gated * (1.0 - opening)


def feed_rows(middle, n2, vec, buf, h_ref, slope_ref, at_rows):
    feed = None
    for at in range(4):
        cut = slice(at * 512, at * 512 + 512)
        active, slope = gelu(dense(n2, unit(buf, 3 + at)))
        active = active.astype(bf16)
        h_ref[at_rows, cut] = active
        slope_ref[:, cut] = slope.astype(bf16)
        part = dense(active, down_part(buf, at))
        feed = part if feed is None else feed + part
    closing = jax.nn.sigmoid(dense(n2, unit(buf, 2)) + vec[3:4, :])
    gated = closing * feed
    return middle + gated, closing, gated * (1.0 - closing)


def feed_kernel(place, x_ref, n1_ref, o_ref, vec_ref, rest_ref,
                y_ref, n2_ref, scale_ref, ga_ref, ta_ref, h_ref, slope_ref, gf_ref, tf_ref, buf, sems):
    at_start([rest_copy(rest_ref, buf, sems.at[0], 0, REST, 0)])
    vec = vec_ref[...]
    middle, n2, _, scale, ga, ta = gated_rows(x_ref[...], n1_ref[...], o_ref[...], vec, buf)
    ga_ref[...] = ga.astype(bf16)
    ta_ref[...] = ta.astype(bf16)
    n2_ref[...] = n2
    scale_ref[...] = jnp.broadcast_to(scale, scale_ref.shape)
    y, gf, tf = feed_rows(middle, n2, vec, buf, h_ref, slope_ref, slice(None))
    gf_ref[...] = gf.astype(bf16)
    tf_ref[...] = tf.astype(bf16)
    y_ref[...] = y.astype(bf16)


def feed_forward(place, x, n1, o, vec, rest, waits=()):
    length, width = x.shape
    wide = 4 * width
    row, half = rows_of(width), struct((length, width), bf16)
    big, bigs = rows_of(wide), struct((length, wide), bf16)
    return call(
        feed_kernel,
        (length // ROWS,),
        [row, row, row, whole(16, width), ANY],
        [row, row, rows_of(128), row, row, big, big, row, row],
        [half, half, struct((length, 128), f32), half, half, bigs, bigs, half, half],
        [pltpu.VMEM((PARTS, REST, width), bf16), pltpu.SemaphoreType.DMA((1,))],
        flops=2 * length * width * (3 * width + 2 * wide),
        moved=24_000_000,
        waits=waits,
    )(place, x, n1, o, vec, rest)


def back_rows(e, hat, scale, ga, ta, slope_ref, gf, tf, gain, buf, du_ref, at_rows):
    df = (e * gf).astype(bf16)
    dzf = (e * tf).astype(bf16)
    dn2 = against(dzf, unit(buf, 2))
    for at in range(4):
        cut = slice(at * 512, at * 512 + 512)
        du = (against(df, down_part(buf, at)) * slope_ref[:, cut].astype(f32)).astype(bf16)
        du_ref[at_rows, cut] = du
        dn2 = dn2 + against(du, unit(buf, 3 + at))
    dm = e + norm_back(dn2, hat, scale, gain)
    da = (dm * ga).astype(bf16)
    dza = (dm * ta).astype(bf16)
    return dm, df, dzf, da, dza, against(da, unit(buf, 0)).astype(bf16)


def put_lanes(swap, keep, send, values, rows, first):
    for y in range(2):
        low, high = (values[(y * 2 + c) * rows : (y * 2 + c + 1) * rows] for c in range(2))
        keep[y, first : first + rows, :] = jnp.where(swap, high, low)
        send[y, first : first + rows, :] = jnp.where(swap, low, high)


def rest_grads(place, keep, send, o, n1, n2, h, da, dza, dzf, du_ref, df, sums):
    put = functools.partial(put_lanes, place[2] == 1, keep, send)
    put(cross(o, da).astype(bf16), UNIT, 0)
    put(cross(n1, dza).astype(bf16), UNIT, UNIT)
    put(cross(n2, dzf).astype(bf16), UNIT, 2 * UNIT)
    for at in range(4):
        put(cross(n2, du_ref[:, at * 512 : at * 512 + 512]).astype(bf16), UNIT, (3 + at) * UNIT)
    put(cross(h, df).astype(bf16), 4 * UNIT, 7 * UNIT)
    small = jnp.concatenate([sums, jnp.zeros((8, sums.shape[1]), f32)], axis=0).astype(bf16)
    for ref in (keep, send):
        for y in range(2):
            ref[y, REST:, :] = small


def keep_rows(at_rows, refs, values):
    for ref, value in zip(refs, values):
        ref[at_rows, :] = value


def add_sums(sums, dza, dzf):
    rows = [jnp.sum(part.astype(f32), axis=0, keepdims=True) for part in (dza, dzf)]
    new = jnp.concatenate(rows + [jnp.zeros((6, dza.shape[1]), f32)], axis=0)
    sums[...] = jnp.where(pl.program_id(0) == 0, new, sums[...] + new)


def turn_kernel(count, place, x_ref, n1_ref, o_ref, e_ref, vec_ref, o_cols, n1_cols, rest_ref,
                y_ref, dm_ref, dza_ref, do_ref, keep, send, buf, h, du, slope, n2, df, dzf, da, dza, sums, sems):
    step = pl.program_id(0)
    near = rest_copy(rest_ref, buf, sems.at[0], 0, 3 * UNIT, 0)
    far = rest_copy(rest_ref, buf, sems.at[1], 3 * UNIT, REST, 0)

    @pl.when(step == 0)
    def _():
        near.start()
        far.start()
        near.wait()

    @pl.when(step < count)
    def _():
        at_rows = pl.ds(pl.multiple_of(step * ROWS, ROWS), ROWS)
        vec = vec_ref[...]
        middle, low, hat, scale, ga, ta = gated_rows(x_ref[...], n1_ref[...], o_ref[...], vec, buf)

        @pl.when(step == 0)
        def _():
            far.wait()

        y, gf, tf = feed_rows(middle, low, vec, buf, h, slope, at_rows)
        y_ref[...] = y.astype(bf16)
        e = e_ref[...].astype(f32)
        dm, *parts, grad_o = back_rows(e, hat, scale, ga, ta, slope, gf, tf, vec[1:2, :], buf, du, at_rows)
        dm_ref[...] = dm
        do_ref[...] = grad_o
        keep_rows(at_rows, (n2, df, dzf, da, dza), (low, *parts))
        dza_ref[...] = parts[3]
        add_sums(sums, parts[3], parts[1])

    @pl.when(step >= count)
    def _():
        at = step - count
        narrow, wide = pl.ds(pl.multiple_of(at * 128, 128), 128), pl.ds(pl.multiple_of(at * 512, 512), 512)
        lefts = (o_cols[...], n1_cols[...], n2[:, narrow], h[:, wide])
        rest_grads(place, keep, send, *lefts, da[...], dza[...], dzf[...], du, df[...], sums[...])


def late_specs(length, width, count):
    row = pl.BlockSpec((ROWS, width), lambda i, place: (jnp.minimum(i, count - 1), 0))
    cols = pl.BlockSpec((length, width // 4), lambda i, place: (0, jnp.maximum(i - count, 0)))
    grad = pl.BlockSpec((2, REST + 16, width), lambda i, place: (jnp.maximum(i - count, 0), 0, 0))
    return row, cols, grad


def turn(place, x, n1, o, e, vec, rest, waits=()):
    length, width = x.shape
    wide, count = 4 * width, length // ROWS
    row, cols, grad = late_specs(length, width, count)
    half, tall = struct((length, width), bf16), pltpu.VMEM((length, width), bf16)
    return call(
        functools.partial(turn_kernel, count),
        (count + 4,),
        [row] * 4 + [whole(16, width), cols, cols, ANY],
        [row] * 4 + [grad] * 2,
        [half, struct((length, width), f32), half, half] + [struct((PARTS // 2, REST + 16, width), bf16)] * 2,
        [pltpu.VMEM((PARTS, REST, width), bf16)]
        + [pltpu.VMEM((length, wide), bf16)] * 2
        + [pltpu.VMEM((ROWS, wide), bf16)]
        + [tall] * 5
        + [pltpu.VMEM((8, width), f32), pltpu.SemaphoreType.DMA((2,))],
        flops=6 * length * width * (3 * width + 2 * wide),
        moved=24_000_000,
        waits=waits,
    )(place, x, n1, o, e, vec, o, n1, rest)


def dx_rows(x, dm, dqkv, dza, gain, buf, gate):
    width = x.shape[1]
    dn = against(dza, gate[...].reshape(PARTS * UNIT, width))
    for at, part in enumerate(dqkv):
        dn = dn + against(part, unit(buf, at))
    hat, scale = normalise(x.astype(f32))
    return dm + norm_back(dn, hat, scale, gain)


def joint_kernel(count, many, place, x_ref, dm1_ref, dq_ref, dk_ref, dv_ref, dza1_ref, e_ref,
                 n2_ref, scale_ref, ga_ref, ta_ref, slope_ref, gf_ref, tf_ref, vec1_ref, vec_ref,
                 o_cols, n1_cols, n2_cols, h_cols, rest1_ref, rest_ref, *refs):
    dx_ref, low_ref, dm_ref, dza_ref, do_ref, keep, send, head, gate, buf, du, df, dzf, da, dza, sums, sems = refs[many:]
    step = pl.program_id(0)
    copies = fetches(place, refs[:many], head, sems, ((0, 3 * UNIT),))[0]
    copies.append(rest_copy(rest1_ref, gate, sems.at[1], UNIT, 2 * UNIT, UNIT))
    copies.append(rest_copy(rest_ref, buf, sems.at[2], 0, REST, 0))
    at_start(copies)

    @pl.when(step < count)
    def _():
        at_rows = pl.ds(pl.multiple_of(step * ROWS, ROWS), ROWS)
        dqkv = (dq_ref[...], dk_ref[...], dv_ref[...])
        dx = dx_rows(x_ref[...], dm1_ref[...], dqkv, dza1_ref[...], vec1_ref[0:1, :], head, gate)
        dx_ref[...] = dx
        low = dx.astype(bf16)
        low_ref[...] = low
        e = e_ref[...].astype(f32) + low.astype(f32)
        gain = vec_ref[1:2, :]
        hat = n2_ref[...].astype(f32) * (1.0 / gain)
        ga, ta, gf, tf = (ref[...].astype(f32) for ref in (ga_ref, ta_ref, gf_ref, tf_ref))
        dm, *parts, grad_o = back_rows(e, hat, scale_ref[:, 0:1], ga, ta, slope_ref, gf, tf, gain, buf, du, at_rows)
        dm_ref[...] = dm
        do_ref[...] = grad_o
        keep_rows(at_rows, (df, dzf, da, dza), parts)
        dza_ref[...] = parts[3]
        add_sums(sums, parts[3], parts[1])

    @pl.when(step >= count)
    def _():
        lefts = (o_cols[...], n1_cols[...], n2_cols[...], h_cols[...])
        rest_grads(place, keep, send, *lefts, da[...], dza[...], dzf[...], du, df[...], sums[...])


def joint_back(place, x, dm1, dqkv, dza1, vec1, head, rest1, e, kept, rest, waits=()):
    n1, o, vec, n2, scale, ga, ta, h, slope, gf, tf = kept
    length, width = x.shape
    wide, count = 4 * width, length // ROWS
    row, cols, grad = late_specs(length, width, count)
    lanes = pl.BlockSpec((ROWS, 128), lambda i, place: (jnp.minimum(i, count - 1), 0))
    big = pl.BlockSpec((ROWS, wide), lambda i, place: (jnp.minimum(i, count - 1), 0))
    wides = pl.BlockSpec((length, wide // 4), lambda i, place: (0, jnp.maximum(i - count, 0)))
    half, tall = struct((length, width), bf16), pltpu.VMEM((length, width), bf16)
    floats = struct((length, width), f32)
    return call(
        functools.partial(joint_kernel, count, len(head)),
        (count + 4,),
        [row] * 8 + [lanes, row, row, big, row, row, whole(16, width), whole(16, width), cols, cols, cols, wides, ANY, ANY]
        + [ANY] * len(head),
        [row] * 5 + [grad] * 2,
        [floats, half, floats, half, half] + [struct((PARTS // 2, REST + 16, width), bf16)] * 2,
        [pltpu.VMEM((PARTS, 3 * UNIT, width), bf16), pltpu.VMEM((PARTS, UNIT, width), bf16), pltpu.VMEM((PARTS, REST, width), bf16)]
        + [pltpu.VMEM((length, wide), bf16)]
        + [tall] * 4
        + [pltpu.VMEM((8, width), f32), pltpu.SemaphoreType.DMA((3,))],
        flops=4 * length * width * (5 * width + 2 * wide),
        moved=40_000_000,
        waits=waits,
    )(place, x, dm1, *dqkv, dza1, e, n2, scale, ga, ta, slope, gf, tf, vec1, vec, o, n1, n2, h, rest1, rest, *head)


def split3(value):
    first = value.astype(bf16)
    rest = value - first.astype(f32)
    second = rest.astype(bf16)
    third = (rest - second.astype(f32)).astype(bf16)
    return first, second, third


def attend_back_kernel(block, place, q_ref, k_ref, v_ref, o_ref, s_ref, do_ref, dq_ref, dk_ref, dv_ref,
                       q_s, k_s, v_s, do_s, acc):
    length = q_ref.shape[0]
    lane = lax.broadcasted_iota(jnp.int32, (length, 128), 1)
    row = lax.broadcasted_iota(jnp.int32, (block, block), 0)
    col = lax.broadcasted_iota(jnp.int32, (block, block), 1)
    q, k, v, do = q_ref[...], k_ref[...], v_ref[...], do_ref[...]
    zero = jnp.zeros_like(q)
    product = do.astype(f32) * o_ref[...].astype(f32)
    for head in range(2):
        low = head * HD
        other = (1 - head) * HD
        mine = (lane >= low) & (lane < low + HD)
        logs = -s_ref[:, low : low + 1]
        delta = -jnp.sum(jnp.where(mine, product, 0.0), axis=1, keepdims=True)
        one = jnp.where((lane >= other) & (lane < other + 3), jnp.ones_like(q), zero)
        q_aug, do_aug = jnp.where(mine, q, zero), jnp.where(mine, do, zero)
        for at, (part, piece) in enumerate(zip(split3(logs), split3(delta))):
            here = lane == other + at
            q_aug = jnp.where(here, part, q_aug)
            do_aug = jnp.where(here, piece, do_aug)
        q_s[head] = q_aug
        do_s[head] = do_aug
        k_s[head] = jnp.where(mine, k, one)
        v_s[head] = jnp.where(mine, v, one)
    for index in range(length // block):
        start, stop = index * block, (index + 1) * block
        kgrads, vgrads = [], []
        for head in range(2):
            kb, vb = k_s[head, start:stop, :], v_s[head, start:stop, :]
            scores = against(kb, q_s[head, start:, :])
            first = jnp.where(row <= col, scores[:, :block], -1e30)
            scores = jnp.concatenate([first, scores[:, block:]], axis=1) if stop < length else first
            probs = jnp.exp(scores)
            grads = (probs * against(vb, do_s[head, start:, :])).astype(bf16)
            vgrads.append(dense(probs.astype(bf16), do_ref[start:, :]))
            kgrads.append(dense(grads, q_ref[start:, :]))
            part = cross(grads, kb)
            if index == 0:
                acc[head] = part
            else:
                acc[head, start:, :] += part
        half = lane[:block] < HD
        dk_ref[start:stop, :] = jnp.where(half, kgrads[0], kgrads[1]).astype(bf16)
        dv_ref[start:stop, :] = jnp.where(half, vgrads[0], vgrads[1]).astype(bf16)
    dq_ref[...] = (jnp.where(lane < HD, acc[0], acc[1]) * 0.125).astype(bf16)


def attend_back(place, q, k, v, o, s, do, start, count=2, onto=(), waits=(), block=256):
    length, width = q.shape
    pair = pl.BlockSpec((length, 128), lambda i, place: (0, i + start))
    return call(
        functools.partial(attend_back_kernel, block),
        (count,),
        [pair] * 6,
        [pair] * 3,
        [struct((length, width), bf16)] * 3,
        [pltpu.VMEM((2, length, 128), bf16)] * 4 + [pltpu.VMEM((2, length, 128), f32)],
        flops=5_000_000_000 * count,
        moved=5_000_000,
        onto=onto,
        waits=waits,
    )(place, q, k, v, o, s, do)


def qkv_back_kernel(many, place, x_ref, dm_ref, dq_ref, dk_ref, dv_ref, dza_ref, vec_ref, rest_ref, *refs):
    dx_ref, low_ref, buf, gate, sems = refs[many:]
    copies = fetches(place, refs[:many], buf, sems, ((0, 3 * UNIT),))[0]
    at_start(copies + [rest_copy(rest_ref, gate, sems.at[1], UNIT, 2 * UNIT, UNIT)])
    dqkv = (dq_ref[...], dk_ref[...], dv_ref[...])
    dx = dx_rows(x_ref[...], dm_ref[...], dqkv, dza_ref[...], vec_ref[0:1, :], buf, gate)
    dx_ref[...] = dx
    low_ref[...] = dx.astype(bf16)


def qkv_back(place, x, dm, dq, dk, dv, dza, vec, weights, rest, waits=()):
    length, width = x.shape
    row = rows_of(width)
    return call(
        functools.partial(qkv_back_kernel, len(weights)),
        (length // ROWS,),
        [row] * 6 + [whole(16, width), ANY] + [ANY] * len(weights),
        [row, row],
        [struct((length, width), f32), struct((length, width), bf16)],
        [pltpu.VMEM((PARTS, 3 * UNIT, width), bf16), pltpu.VMEM((PARTS, UNIT, width), bf16), pltpu.SemaphoreType.DMA((2,))],
        flops=2 * length * width * 4 * width,
        moved=12_000_000,
        waits=waits,
    )(place, x, dm, dq, dk, dv, dza, vec, rest, *weights)


def put(place, outs, values, rows, first):
    keep, send = outs
    for y in range(2):
        low, high = (values[(y * 2 + c) * rows : (y * 2 + c + 1) * rows] for c in range(2))
        at = place[1] ^ y
        swap = place[2] == 1
        keep[at, 0, first : first + rows, :] = jnp.where(swap, high, low)
        send[at, 0, first : first + rows, :] = jnp.where(swap, low, high)


def grad_outs(rows, width):
    out = pl.BlockSpec((2, 1, rows, width), lambda i, place: (0, (i - place[0]) & 3, 0, 0))
    return [out, out], [struct((2, 4, rows, width), bf16)] * 2


def first_grad_kernel(place, *refs):
    outs = refs[-2:]
    for layer in range(len(refs) // 4):
        n1_ref = refs[4 * layer]
        for at, ref in enumerate(refs[4 * layer + 1 : 4 * layer + 4]):
            put(place, outs, cross(n1_ref[...], ref[...]).astype(bf16), UNIT, (3 * layer + at) * UNIT)


def first_grad(place, *layers, waits=()):
    length, width = layers[0][0].shape
    cols = pl.BlockSpec((length, width // 4), lambda i, place: (0, i))
    specs, shapes = grad_outs(3 * UNIT * len(layers), width)
    return call(
        first_grad_kernel,
        (4,),
        ([cols] + [whole(length, width)] * 3) * len(layers),
        specs,
        shapes,
        flops=2 * length * width * 3 * width * len(layers),
        moved=9_000_000 * len(layers),
        waits=waits,
    )(place, *(value for layer in layers for value in layer))


def moved_z(value, steps):
    count = lax.axis_size("dp")
    return lax.ppermute(value, "dp", [(d, (d + 4 * steps) % count) for d in range(count)])


def swapped(value, bit):
    return lax.ppermute(value, "dp", [(d, d ^ bit) for d in range(lax.axis_size("dp"))])


def crossed(value, sources=(0, 1)):
    return lax.ppermute(value, "section", [(s, 1 - s) for s in sources])


def along_z(block):
    return [block] + [moved_z(block, k) for k in (1, 2, 3)]


def across(own):
    beside = swapped(own, 2)
    return own, beside, swapped(own, 1), swapped(beside, 1)


def spread_whole(blocks):
    blocks = blocks.reshape(4, 2, 2, *blocks.shape[1:])
    blocks = jnp.stack([blocks[0], blocks[3], blocks[2], blocks[1]])
    return tuple(blocks[:, index & 1, index >> 1] for index in range(4))


def gather_whole(values, axis):
    values = lax.all_gather(values.astype(bf16), "dp", axis=axis, tiled=True)
    return lax.all_gather(values, "section", axis=0, tiled=True)


def split_rows(matrix, cols):
    rows, width = matrix.shape[0] // PARTS, matrix.shape[1] // cols
    return matrix.reshape(PARTS, rows, cols, width).transpose(0, 2, 1, 3).reshape(PARTS, cols * rows, width)


def merge_rows(blocks, cols):
    rows, width = blocks.shape[1] // cols, blocks.shape[2]
    return blocks.reshape(PARTS, cols, rows, width).transpose(0, 2, 1, 3).reshape(PARTS * rows, cols * width)


def weights_whole(w_qkv, w_out, w_gates, w_up, w_down, gains, biases):
    w_qkv, w_out, w_up, w_down = (gather_whole(w, 1) for w in (w_qkv, w_out, w_up, w_down))
    w_gates, gains, biases = (gather_whole(w, 2) for w in (w_gates, gains, biases))
    heads, tails = [], []
    for layer in range(2):
        lines = jnp.concatenate([gains[layer], biases[layer], jnp.zeros((12, gains.shape[2]), bf16)], axis=0)
        lines = jnp.concatenate([lines[None], jnp.zeros((PARTS - 1, *lines.shape), bf16)], axis=0)
        heads.append(spread_whole(jnp.concatenate([split_rows(w_qkv[layer], 3), lines], axis=1)))
        parts = [w_out[layer], w_gates[layer, 0], w_gates[layer, 1]]
        parts = [split_rows(part, 1) for part in parts] + [split_rows(w_up[layer], 4), split_rows(w_down[layer], 1)]
        tails.append(jnp.concatenate(parts, axis=1))
    return heads, tails


def joined(pieces):
    return jnp.stack(pieces).transpose(2, 1, 0, 3, 4).reshape(PARTS, *pieces[0].shape[2:])


def collect_whole(early, rest):
    early, rest = joined(early), jnp.stack(rest, axis=1).reshape(PARTS, *rest[0].shape[1:])
    parts = [merge_rows(early, 3), merge_rows(rest[:, :UNIT], 1)]
    parts += [jnp.stack([merge_rows(rest[:, at * UNIT : (at + 1) * UNIT], 1) for at in (1, 2)])]
    parts += [merge_rows(rest[:, 3 * UNIT : 7 * UNIT], 4), merge_rows(rest[:, 7 * UNIT : REST], 1), rest[0, REST : REST + 2]]
    axes = (0, 0, 1, 0, 0, 1)
    parts = [lax.psum_scatter(part.astype(f32), "dp", scatter_dimension=axis, tiled=True) for part, axis in zip(parts, axes)]
    return [lax.psum(part, "section") for part in parts]


def fold_core(keep, got):
    away = (keep[1].astype(f32) + got[1].astype(f32)).astype(bf16)
    return away, keep[0].astype(f32) + got[0].astype(f32)


def scattered(keep, got):
    lanes = [[d for d in range(PARTS) if d % 2 == c] for c in range(2)]
    both = (keep.astype(f32) + got.astype(f32)).astype(bf16)
    return lax.psum_scatter(both, "dp", scatter_dimension=0, axis_index_groups=lanes)


def fold_y(near, got):
    near = near + got.astype(f32)
    return near[0], [near[k].astype(bf16) for k in (1, 2, 3)]


def fold_z(total, gots):
    for got in gots:
        total = total + got.astype(f32)
    return total


def pack_kernel(place, qkv_ref, out_ref, gates_ref, up_ref, down_ref, lines_ref, head_ref, tail_ref):
    width = out_ref.shape[2]
    for at in range(3):
        head_ref[at * UNIT : (at + 1) * UNIT, :] = qkv_ref[0, :, at * width : (at + 1) * width].astype(bf16)
    head_ref[3 * UNIT :, :] = lines_ref[...].astype(bf16)
    tail_ref[:UNIT, :] = out_ref[0].astype(bf16)
    for at in range(2):
        tail_ref[(1 + at) * UNIT : (2 + at) * UNIT, :] = gates_ref[0, at].astype(bf16)
    for at in range(4):
        tail_ref[(3 + at) * UNIT : (4 + at) * UNIT, :] = up_ref[0, :, at * width : (at + 1) * width].astype(bf16)
    tail_ref[7 * UNIT :, :] = down_ref[0].astype(bf16)


def pack(place, index, w_qkv, w_out, w_gates, w_up, w_down, gains, biases):
    width = w_out.shape[2]
    lines = jnp.concatenate([gains[0], biases[0]], axis=0)
    mine = jnp.arange(width)[None, :] // UNIT == index
    lines = jnp.concatenate([jnp.where(mine, jnp.tile(lines, (1, PARTS)), 0.0), jnp.zeros((12, width), f32)], axis=0)
    arrays = (w_qkv, w_out, w_gates, w_up, w_down, lines)
    return call(
        pack_kernel,
        (1,),
        [whole(*array.shape) for array in arrays],
        [whole(FIRST, width), whole(REST, width)],
        [struct((FIRST, width), bf16), struct((REST, width), bf16)],
        moved=3_000_000,
    )(place, *arrays)


def after(value, *others):
    return lax.optimization_barrier((value, *others))[0]


def gain_grads(grads, w_qkv, w_gates, w_up, gains):
    d_qkv, _, d_gates, d_up = grads[:4]
    w_qkv, w_gates, w_up, gains = (w[0].astype(bf16).astype(f32) for w in (w_qkv, w_gates, w_up, gains))
    first = jnp.sum(w_qkv * d_qkv, axis=1) + jnp.sum(w_gates[0] * d_gates[0], axis=1)
    second = jnp.sum(w_up * d_up, axis=1) + jnp.sum(w_gates[1] * d_gates[1], axis=1)
    return jnp.stack([first, second]) / gains


def finish_kernel(place, own0, got0, own1, got1, own2, got2, own3, got3, w_qkv, w_gates, w_up, gains,
                  g_qkv, g_out, g_gates, g_up, g_down, g_gains, g_biases):
    width = own0.shape[1]
    first = place[3] == 0

    def total(start, stop):
        early = own0[start:stop, :] + got0[start:stop, :].astype(f32), own1[start:stop, :] + got1[start:stop, :].astype(f32)
        return jnp.where(first, *early)

    def rest(start, stop):
        return jnp.where(
            first,
            own2[start:stop, :].astype(f32) + got2[start:stop, :].astype(f32),
            own3[start:stop, :].astype(f32) + got3[start:stop, :].astype(f32),
        )

    def against_weight(weight, grad):
        return jnp.sum(weight.astype(bf16).astype(f32) * grad, axis=1, keepdims=True)

    rows = lax.broadcasted_iota(jnp.int32, (UNIT, UNIT), 0)
    diagonal = rows == lax.broadcasted_iota(jnp.int32, (UNIT, UNIT), 1)
    lines = [None, None]
    for at in range(2):
        part = rest((1 + at) * UNIT, (2 + at) * UNIT)
        g_gates[0, at] = part
        lines[at] = against_weight(w_gates[0, at], part)
    for at in range(3):
        cut = slice(at * width, at * width + width)
        part = total(at * UNIT, (at + 1) * UNIT)
        g_qkv[0, :, cut] = part
        lines[0] += against_weight(w_qkv[0, :, cut], part)
    for at in range(4):
        cut = slice(at * width, at * width + width)
        part = rest((3 + at) * UNIT, (4 + at) * UNIT)
        g_up[0, :, cut] = part
        lines[1] += against_weight(w_up[0, :, cut], part)
    g_out[0] = rest(0, UNIT)
    g_down[0] = rest(7 * UNIT, REST)
    sums = rest(REST, REST + 16)
    index = (place[0] * 2 + place[1]) * 2 + place[2]
    for at in range(2):
        line = jnp.sum(jnp.where(diagonal, lines[at], 0.0), axis=0, keepdims=True)
        g_gains[0, at : at + 1, :] = line / gains[0, at : at + 1, :].astype(bf16).astype(f32)
        mine = jnp.zeros((1, UNIT), f32)
        for part in range(PARTS):
            mine = jnp.where(index == part, sums[at : at + 1, part * UNIT : (part + 1) * UNIT], mine)
        g_biases[0, at : at + 1, :] = mine


def finish(place, sums, masters):
    w_qkv, w_out, w_gates, w_up, w_down, gains, biases = masters
    inputs = (*sums, w_qkv, w_gates, w_up, gains)
    shapes = [struct(master.shape, f32) for master in (w_qkv, w_out, w_gates, w_up, w_down, gains, biases)]
    return call(
        finish_kernel,
        (1,),
        [whole(*value.shape) for value in inputs],
        [whole(*shape.shape) for shape in shapes],
        shapes,
        moved=6_000_000,
    )(place, *inputs)


def per_device(tokens, cotangent, w_qkv, w_out, w_gates, w_up, w_down, norm_gains, gate_biases):
    section = lax.axis_index("section")
    index = lax.axis_index("dp")
    fast = lax.axis_size("dp") == PARTS
    first = section == 0
    masters = (w_qkv, w_out, w_gates, w_up, w_down, norm_gains, gate_biases)

    def pick(own, other):
        return jnp.where(first, own, other), jnp.where(first, other, own)

    x = jnp.where(first, tokens[0, 0], tokens[1, 0])
    seeds = [cotangent[0, m, 0] for m in range(2)]
    own_seed, other_seed = jnp.where(first, seeds[0], seeds[1]), jnp.where(first, seeds[1], seeds[0])
    if fast:
        y0, y1, theirs, dxs, lows, grads = run(x, own_seed, other_seed, masters, index, section, pick)
    else:
        place = jnp.zeros((3,), jnp.int32)
        heads, rest = weights_whole(*masters)
        n0, q0, k0, v0, vec0 = qkv_forward(place, x, heads[0])
        o0, s0 = attend_forward(place, q0, k0, v0, 2, onto=attend_forward(place, q0, k0, v0, 0))
        y0, *kept = feed_forward(place, x, n0, o0, vec0, rest[0])
        n1, q1, k1, v1, vec1 = qkv_forward(place, y0, heads[1])
        o1, s1 = attend_forward(place, q1, k1, v1, 2, onto=attend_forward(place, q1, k1, v1, 0))
        seeds = pick(own_seed, crossed(other_seed))
        y1, dm, dza, do, *later1 = turn(place, y0, n1, o1, seeds[1], vec1, rest[1])
        dqkv = attend_back(place, q1, k1, v1, o1, s1, do, 2, onto=attend_back(place, q1, k1, v1, o1, s1, do, 0))
        early1 = first_grad(place, (n1, *dqkv))
        dx1, low1, dm, dza, do, *later0 = joint_back(
            place, y0, dm, dqkv, dza, vec1, heads[1], rest[1], seeds[0], (n0, o0, vec0, *kept), rest[0]
        )
        dqkv = attend_back(place, q0, k0, v0, o0, s0, do, 2, onto=attend_back(place, q0, k0, v0, o0, s0, do, 0))
        early0 = first_grad(place, (n0, *dqkv))
        dx0, low0 = qkv_back(place, x, dm, *dqkv, dza, vec0, heads[0], rest[0])
        grads0, grads1 = collect_whole(early0, later0), collect_whole(early1, later1)
        dxs, lows = (dx0, dx1), (crossed(low0, (1,)), crossed(low1, (0,)))
        theirs = crossed(jnp.where(first, y1, y0))
        grads = [jnp.where(first, *pair) for pair in zip(grads0, grads1)]
        grads.insert(5, gain_grads(grads, w_qkv, w_gates, w_up, norm_gains))
        grads = [grad[None] for grad in grads]

    mine = jnp.where(first, y0, y1)
    block = jnp.stack([jnp.where(first, mine, theirs), jnp.where(first, theirs, mine)])[None, :, None]
    in_grads = jnp.stack([jnp.where(first, dxs[0], lows[1].astype(f32)), dxs[1]])
    last = jnp.where(first, lows[0].astype(f32), dxs[1])
    in_grads = lax.dynamic_update_slice(in_grads, last[None], (1, 0, 0))[None, :, None]
    return (block, in_grads, *grads)


def run(x, own_seed, other_seed, masters, index, section, pick):
    first = section == 0
    width = x.shape[1]
    place = jnp.stack([index // 4, (index // 2) & 1, index & 1, section]).astype(jnp.int32)
    head, tail = pack(place, index, *masters)
    heads = pick(head, crossed(head))
    tails = pick(tail, crossed(tail))
    tail0 = lax.all_gather(tails[0], "dp", axis=0)

    def cores(z, y):
        return z, y, swapped(z, 1), swapped(y, 1)

    zh0 = jnp.stack(along_z(heads[0]))
    yh0 = swapped(zh0, 2)
    zh1 = along_z(after(heads[1], yh0))
    head0 = cores(zh0, yh0)
    n1, q, k, v, vec = qkv_forward(place, x, head0)
    o, s = attend_forward(place, q, k, v, 0)
    zh1 = jnp.stack([after(part, o) for part in zh1])
    yh1 = swapped(zh1, 2)
    o, s = attend_forward(place, q, k, v, 2, onto=(o, s), waits=(zh1,))
    tail0 = after(tail0, o)
    tail1 = lax.all_gather(after(tails[1], tail0), "dp", axis=0)
    other_seed = crossed(after(other_seed, o))
    y0, *held = feed_forward(place, x, n1, o, vec, tail0)
    head1 = cores(after(zh1, y0), after(yh1, y0))
    kept0 = (n1, o, vec, *held)
    layer0 = (q, k, v, o, s)

    n1, q, k, v, vec = qkv_forward(place, y0, head1)
    o, s = attend_forward(place, q, k, v, 0)
    o, s = attend_forward(place, q, k, v, 2, onto=(o, s))
    seeds = pick(own_seed, after(other_seed, o))
    y1, dm, dza, do, keep, send = turn(place, y0, n1, o, seeds[1], vec, tail1)
    got = swapped(send, 1)
    theirs = crossed(jnp.where(first, y1, y0))
    dqkv = attend_back(place, q, k, v, o, s, do, 0, 1)
    rest1 = scattered(keep, after(got, dqkv[0]))
    dqkv = attend_back(place, q, k, v, o, s, do, 1, 3, onto=dqkv)
    keep_b, send_b = first_grad(place, (n1, *dqkv))
    got_b = swapped(send_b, 1)
    dx1, low1, dm, dza, do, keep, send = joint_back(
        place, y0, dm, dqkv, dza, vec, head1, tail1, seeds[0], kept0, tail0, waits=(keep_b, theirs)
    )
    n1, o, vec = kept0[:3]
    q, k, v, o, s = layer0
    got = swapped(send, 1)
    away, near = fold_core(keep_b, after(got_b, low1))
    got_b = swapped(away, 2)
    other1 = crossed(low1, (0,))
    dqkv = attend_back(place, q, k, v, o, s, do, 0, 1, waits=(away,))
    rest0 = scattered(keep, after(got, dqkv[0]))
    dqkv = attend_back(place, q, k, v, o, s, do, 1, 3, onto=dqkv)
    own, sends = fold_y(near, after(got_b, dqkv[0]))
    gots = [moved_z(part, at + 1) for at, part in enumerate(sends)]
    keep, send = first_grad(place, (n1, *dqkv), waits=(other1, *sends))
    got = swapped(send, 1)
    away, near = fold_core(keep, got)
    got = swapped(away, 2)
    dx0, low0 = qkv_back(place, x, dm, *dqkv, dza, vec, head0, tail0, waits=(away,))
    early1 = fold_z(own, [after(part, low0) for part in gots])
    rest1 = after(rest1, low0)
    last1 = crossed(jnp.concatenate([rest1, early1.astype(bf16)]), (0,))
    other0 = crossed(low0, (1,))
    own, sends = fold_y(near, after(got, low0))
    gots = [moved_z(part, at + 1) for at, part in enumerate(sends)]
    early0 = fold_z(own, gots)
    last0 = crossed(early0.astype(bf16), (1,))
    rest0 = after(rest0, last0, last1, other0)
    later0 = crossed(rest0, (1,))
    sums = (early0, last0, early1, last1[REST + 16 :], rest0, later0, rest1, last1[: REST + 16])
    grads = finish(place, sums, masters)
    return y0, y1, theirs, (dx0, dx1), (other0, other1), grads


def solution(mesh):
    placed = (
        P(None, "dp", None, None),
        P("section", None, "dp", None, None),
        P("section", "dp", None),
        P("section", "dp", None),
        P("section", None, "dp", None),
        P("section", "dp", None),
        P("section", "dp", None),
        P("section", None, "dp"),
        P("section", None, "dp"),
    )
    return jax.shard_map(
        per_device,
        mesh=mesh,
        in_specs=placed,
        out_specs=(P("section", None, "dp", None, None), P("section", None, "dp", None, None)) + placed[2:],
        check_vma=False,
    )
```
